512 devices in a mesh: row: 16 (over x_lo, y, core), col: 32 (over x_hi, z).
Axes of the slice: x: 4 (x_hi: 2, x_lo: 2; x = x_hi * 2 + x_lo), y: 4, z: 16, core: 2. Of those that a mesh axis runs over, the one named last changes fastest.
Arguments:
- coarse_blocks: bfloat16 [16, 32, 2, 20, 128], P('row', 'col'), may hold values from -18 to 18
- block_ids: int32 [16, 32, 6], P('row', 'col'), may hold values from 0 to 1023, as said below
- quadrant: int32 [16, 32, 6], P('row', 'col'), may hold values from 0 to 1
- land_mask: int32 [512, 1024], P('row', 'col'), may hold values from 0 to 1
- lift_weight: bfloat16 [20, 128], replicated, may hold values from -1.25 to 1.25
- land_vector: float32 [128], replicated, may hold values from -6 to 6
- norm_gain: float32 [128], replicated, may hold values from 0.5 to 2
- first_weight: bfloat16 [9, 128, 128], replicated, may hold values from -0.1875 to 0.1875
- second_weight: bfloat16 [9, 128, 128], replicated, may hold values from -0.1875 to 0.1875
- cotangent: bfloat16 [512, 1024, 128], P('row', 'col'), may hold values from -6 to 6
Outputs:
- features: bfloat16 [512, 1024, 128], P('row', 'col')
- grad_coarse: float32 [16, 32, 2, 20, 128], P('row', 'col')
- grad_first: float32 [9, 128, 128], replicated
- grad_second: float32 [9, 128, 128], replicated
- grad_lift: float32 [20, 128], replicated
- grad_land: float32 [128], replicated
- grad_gain: float32 [128], replicated
The draws below stay inside these ranges and needn't reach their ends.
Inputs may be any that keep to these rules, and one draw needn't show every extreme that they name: `block_ids`: each entry names a block whose owning tile lies at most one tile away along the rows and along the columns (diagonals included) from the listing tile; the first entry of each list names a block of the listing tile itself.
All inputs are finite; a program needn't handle non-finite values.
Results may differ from the reference program's by a relative error of at most 0.005.
Values may be sent and summed in bfloat16 or wider, within the bound.
A program may use at most 64 MiB of HBM per device.

```python
import math
import jax
import jax.numpy as jnp
from jax import lax

CH = 128
CIN = 20
GROUPS = 32
TILE_R = 32
TILE_C = 32
NBLK = 2
NLIST = 6
GRID_R = 16
GRID_C = 32
NY = 512
NX = 1024
HALF_R = 16
CROW = 8
CCOL = 16
CC = 128


def draw_coarse_blocks(key, part):
    key = jax.random.fold_in(key, 11)
    block_shape = (GRID_R, GRID_C, NBLK, CIN, CC)
    row_rise = 1.0 + 2.0 * jnp.arange(GRID_R, dtype=jnp.float32) / max(GRID_R - 1, 1)
    col_rise = 1.0 + 2.0 * jnp.arange(GRID_C, dtype=jnp.float32) / max(GRID_C - 1, 1)
    spread = (row_rise[:, None] * col_rise[None, :] / 3.0)[:, :, None, None, None]
    values = jnp.clip(jax.random.normal(key, block_shape, jnp.float32), -6.0, 6.0) * spread
    return values.astype(jnp.bfloat16)


def draw_block_ids(key, part):
    key = jax.random.fold_in(key, 21)
    list_shape = (GRID_R, GRID_C, NLIST)
    key_row, key_col, key_member = jax.random.split(key, 3)
    entry = jnp.arange(NLIST, dtype=jnp.int32)[None, None, :]
    row_step = jnp.where(entry == 0, 0, jax.random.randint(key_row, list_shape, -1, 2))
    col_step = jnp.where(entry == 0, 0, jax.random.randint(key_col, list_shape, -1, 2))
    rows_at = jnp.arange(GRID_R, dtype=jnp.int32)[:, None, None]
    cols_at = jnp.arange(GRID_C, dtype=jnp.int32)[None, :, None]
    owner_row = jnp.clip(rows_at + row_step, 0, GRID_R - 1)
    owner_col = jnp.clip(cols_at + col_step, 0, GRID_C - 1)
    member = jax.random.randint(key_member, list_shape, 0, NBLK)
    first_tile = (rows_at == 0) & (cols_at == 0) & (entry == 0)
    last_tile = (rows_at == GRID_R - 1) & (cols_at == GRID_C - 1) & (entry == 0)
    member = jnp.where(first_tile, 0, jnp.where(last_tile, NBLK - 1, member))
    return ((owner_row * GRID_C + owner_col) * NBLK + member).astype(jnp.int32)


def draw_quadrant(key, part):
    key = jax.random.fold_in(key, 31)
    list_shape = (GRID_R, GRID_C, NLIST)
    halves = jax.random.randint(key, list_shape, 0, 2)
    entry = jnp.arange(NLIST, dtype=jnp.int32)[None, None, :]
    corner = (jnp.arange(GRID_R, dtype=jnp.int32)[:, None, None] == 0) & (jnp.arange(GRID_C, dtype=jnp.int32)[None, :, None] == 0)
    halves = jnp.where(corner & (entry == 0), 0, halves)
    halves = jnp.where(corner & (entry == 1), 1, halves)
    return halves.astype(jnp.int32)


def draw_land_mask(key, part):
    key = jax.random.fold_in(key, 41)
    tile_row = jnp.arange(NY, dtype=jnp.int32) // TILE_R
    tile_col = jnp.arange(NX, dtype=jnp.int32) // TILE_C
    threshold = 12 + 50 * (tile_col % 2)[None, :] + 20 * tile_row[:, None] // max(GRID_R - 1, 1)
    rolled = jax.random.randint(key, (NY, NX), 0, 100)
    return (rolled < threshold).astype(jnp.int32)


def draw_cotangent(key, part):
    key = jax.random.fold_in(key, 51)
    key_base, key_offset = jax.random.split(key, 2)
    field_shape = (NY, NX, CH)
    tile_offset = jax.random.normal(key_offset, (GRID_R, GRID_C, CH), jnp.float32)
    offset = jnp.repeat(jnp.repeat(tile_offset, TILE_R, axis=0), TILE_C, axis=1)
    base_draw = jnp.clip(jax.random.normal(key_base, field_shape, jnp.float32), -5.0, 5.0)
    values = 0.7 * base_draw + 1.8 * offset
    return jnp.clip(values, -6.0, 6.0).astype(jnp.bfloat16)


def gaussian(key, shape, deviation, most, held_as=jnp.bfloat16):
    drawn = jax.random.normal(key, shape, jnp.float32) * deviation
    return jnp.minimum(jnp.maximum(drawn, -most), most).astype(held_as)


def setup_inputs(seed: int = 0) -> dict:
    splits = jax.random.split(jax.random.key(seed), 11)
    return {
        "coarse_blocks": draw_coarse_blocks(jax.random.fold_in(splits[10], 71), 0),
        "block_ids": draw_block_ids(jax.random.fold_in(splits[10], 71), 0),
        "quadrant": draw_quadrant(jax.random.fold_in(splits[10], 71), 0),
        "land_mask": draw_land_mask(jax.random.fold_in(splits[10], 71), 0),
        "lift_weight": gaussian(splits[4], (CIN, CH), CIN ** -0.5, 1.25),
        "land_vector": gaussian(splits[5], (CH,), 1.0, 6.0, jnp.float32),
        "norm_gain": jnp.clip(jnp.exp(jax.random.uniform(splits[6], (CH,), jnp.float32, math.log(0.5), math.log(2.0))), 0.5, 2.0),
        "first_weight": gaussian(splits[7], (9, CH, CH), (9 * CH) ** -0.5, 0.1875),
        "second_weight": gaussian(splits[8], (9, CH, CH), (9 * CH) ** -0.5, 0.1875),
        "cotangent": draw_cotangent(jax.random.fold_in(splits[10], 71), 0),
    }


EPSILON = 1e-05
PRECISE = lax.Precision.HIGHEST

def upsample_matrix(fine_len, coarse_len):
    position = jnp.arange(fine_len, dtype=jnp.float32)
    location = jnp.clip((position + 0.5) / 2.0 - 0.5, 0.0, coarse_len - 1.0)
    lower = jnp.floor(location)
    fraction = location - lower
    lower_idx = lower.astype(jnp.int32)
    upper_idx = jnp.minimum(lower_idx + 1, coarse_len - 1).astype(jnp.int32)
    columns = jnp.arange(coarse_len, dtype=jnp.int32)
    low_part = (columns[None, :] == lower_idx[:, None]).astype(jnp.float32)
    high_part = (columns[None, :] == upper_idx[:, None]).astype(jnp.float32)
    return (1.0 - fraction)[:, None] * low_part + fraction[:, None] * high_part

def apply_taps(padded, weight, row_count, col_count, flipped):
    channels = padded.shape[2]
    summed = jnp.zeros((row_count * col_count, weight.shape[2]), jnp.float32)
    for number in range(9):
        row_off, col_off = divmod(number, 3)
        if flipped:
            window = padded[2 - row_off:2 - row_off + row_count, 2 - col_off:2 - col_off + col_count]
            summed = summed + jnp.dot(window.reshape(-1, channels), weight[number].T, preferred_element_type=jnp.float32)
        else:
            window = padded[row_off:row_off + row_count, col_off:col_off + col_count]
            summed = summed + jnp.dot(window.reshape(-1, channels), weight[number], preferred_element_type=jnp.float32)
    return summed

def tap_grads(padded, grads, row_count, col_count):
    channels = padded.shape[2]
    stacked = []
    for number in range(9):
        row_off, col_off = divmod(number, 3)
        window = padded[row_off:row_off + row_count, col_off:col_off + col_count].reshape(-1, channels)
        stacked.append(lax.dot_general(window, grads, (((0,), (0,)), ((), ())), preferred_element_type=jnp.float32))
    return jnp.stack(stacked)

def silu_slope(values):
    gate_part = jax.nn.sigmoid(values)
    return gate_part * (1.0 + values * (1.0 - gate_part))

def pad_image(image):
    return jnp.pad(image, ((1, 1), (1, 1), (0, 0)))

def reference(coarse_blocks, block_ids, quadrant, land_mask, lift_weight, land_vector, norm_gain, first_weight, second_weight, cotangent):
    block_width = CIN * CC
    flat_blocks = coarse_blocks.reshape(GRID_R * GRID_C * NBLK, block_width).astype(jnp.float32)
    picked = flat_blocks[block_ids]
    half_hot = (quadrant[..., None] == jnp.arange(2, dtype=jnp.int32)).astype(jnp.float32)
    block_sums = jnp.einsum('rckq,rckx->rcqx', half_hot, picked, precision=PRECISE)
    coarse_grid = block_sums.reshape(GRID_R, GRID_C, 2, CIN, CROW, CCOL)
    row_up = upsample_matrix(HALF_R, CROW)
    col_up = upsample_matrix(TILE_C, CCOL)
    upsampled = jnp.einsum('ia,rcqhab,jb->rqicjh', row_up, coarse_grid, col_up, precision=PRECISE)
    fine_input = upsampled.reshape(NY * NX, CIN).astype(jnp.bfloat16)
    land_float = land_mask.reshape(-1).astype(jnp.float32)
    lifted = jnp.dot(fine_input, lift_weight, preferred_element_type=jnp.float32) + land_float[:, None] * land_vector[None, :]
    pixels = NY * NX
    members = float(pixels * (CH // GROUPS))
    grouped = lifted.reshape(pixels, GROUPS, CH // GROUPS)
    group_mean = lax.optimization_barrier(jnp.sum(grouped, axis=(0, 2))) / members
    centered = grouped - group_mean[None, :, None]
    variance = lax.optimization_barrier(jnp.sum(centered * centered, axis=(0, 2))) / members
    inv_spread = lax.rsqrt(variance + EPSILON)
    normed = (centered * inv_spread[None, :, None]).reshape(pixels, CH)
    scaled = normed * norm_gain[None, :]
    first_act = jax.nn.silu(scaled).astype(jnp.bfloat16).reshape(NY, NX, CH)
    padded_first = pad_image(first_act)
    hidden_pre = apply_taps(padded_first, first_weight, NY, NX, False)
    second_act = jax.nn.silu(hidden_pre).astype(jnp.bfloat16).reshape(NY, NX, CH)
    padded_second = pad_image(second_act)
    features = (lifted + apply_taps(padded_second, second_weight, NY, NX, False)).astype(jnp.bfloat16).reshape(NY, NX, CH)
    report = 1.0 / math.sqrt(NY * NX)
    flat_cot = cotangent.reshape(-1, CH)
    grad_act_two = apply_taps(pad_image(cotangent), second_weight, NY, NX, True)
    grad_hidden = (grad_act_two * silu_slope(hidden_pre)).astype(jnp.bfloat16)
    grad_second = tap_grads(padded_second, flat_cot, NY, NX) * report
    grad_act_one = apply_taps(pad_image(grad_hidden.reshape(NY, NX, CH)), first_weight, NY, NX, True)
    grad_first = tap_grads(padded_first, grad_hidden, NY, NX) * report
    grad_scaled = grad_act_one * silu_slope(scaled)
    grad_gain = lax.optimization_barrier(jnp.sum(grad_scaled * normed, axis=0)) * report
    grad_normed = (grad_scaled * norm_gain[None, :]).reshape(pixels, GROUPS, -1)
    normed_groups = normed.reshape(pixels, GROUPS, -1)
    plain_sum = lax.optimization_barrier(jnp.sum(grad_normed, axis=(0, 2)))
    cross_sum = lax.optimization_barrier(jnp.sum(grad_normed * normed_groups, axis=(0, 2)))
    grad_lifted = (inv_spread[None, :, None] * (grad_normed - plain_sum[None, :, None] / members - normed_groups * cross_sum[None, :, None] / members)).reshape(pixels, CH) + flat_cot.astype(jnp.float32)
    grad_lifted_low = grad_lifted.astype(jnp.bfloat16)
    grad_land = lax.optimization_barrier(jnp.sum(land_float[:, None] * grad_lifted, axis=0)) * report
    grad_lift = jnp.dot(fine_input.T, grad_lifted_low, preferred_element_type=jnp.float32) * report
    grad_fine = jnp.dot(grad_lifted_low, lift_weight.T, preferred_element_type=jnp.float32).reshape(GRID_R, 2, HALF_R, GRID_C, TILE_C, CIN)
    grad_sums = jnp.einsum('ia,rqicjh,jb->rcqhab', row_up, grad_fine, col_up, precision=PRECISE).reshape(GRID_R, GRID_C, 2, block_width)
    grad_entries = jnp.einsum('rckq,rcqx->rckx', half_hot, grad_sums, precision=PRECISE)
    grad_coarse = jnp.zeros_like(flat_blocks).at[block_ids.reshape(-1)].add(grad_entries.reshape(-1, block_width))
    grad_coarse = grad_coarse.reshape(GRID_R, GRID_C, NBLK, CIN, CC)
    return (features, grad_coarse, grad_first, grad_second, grad_lift, grad_land, grad_gain)
```

```python
import math

import jax
import jax.numpy as jnp
from jax import lax
from jax.experimental import pallas as pl
from jax.experimental.pallas import tpu as pltpu
from jax.sharding import PartitionSpec as P

GROUPS = 32
EPSILON = 1e-05
MESH = pl.DeviceIdType.MESH
F32 = jnp.float32
BF16 = jnp.bfloat16

TILE = 32
ROWS = TILE + 4
WIDE = 48
LEFT = 8
CH = 128
CIN = 20
PIX = TILE * TILE
TAPS = 9
HALF = TAPS * CH


def log2(n):
    return n.bit_length() - 1


def size_of(group):
    n = 1
    for _, _, count in group:
        n *= count
    return n


def place_in(group, at):
    m = 0
    for axis, stride, count in group:
        m = (m << log2(count)) | ((at[axis] >> log2(stride)) & (count - 1))
    return m


def member_of(group, at, m):
    new = dict(at)
    for axis, stride, count in reversed(group):
        digit = m & (count - 1)
        m = m >> log2(count)
        new[axis] = (new[axis] & ~((count - 1) * stride)) | (digit << log2(stride))
    return (new["row"], new["col"])


def each_other(group, at, act):
    n = size_of(group)
    me = place_in(group, at)

    def body(k, carry):
        m = (me + k) & (n - 1)
        act(member_of(group, at, m), m)
        return carry

    lax.fori_loop(1, n, body, 0)


def remote(src, dst, send, recv, device):
    return pltpu.make_async_remote_copy(
        src_ref=src,
        dst_ref=dst,
        send_sem=send,
        recv_sem=recv,
        device_id=device,
        device_id_type=MESH,
    )


def dot(a, b):
    return jnp.dot(a, b, preferred_element_type=F32)


def dot_tn(a, b):
    return lax.dot_general(a, b, (((0,), (0,)), ((), ())), preferred_element_type=F32)


def dot_nt(a, b):
    return lax.dot_general(a, b, (((1,), (1,)), ((), ())), preferred_element_type=F32)


def split_two(x):
    hi = x.astype(BF16)
    return hi, (x - hi.astype(F32)).astype(BF16)


def split_three(x):
    hi = x.astype(BF16)
    rest = x - hi.astype(F32)
    mid = rest.astype(BF16)
    return hi, mid, (rest - mid.astype(F32)).astype(BF16)


def sigmoid(v):
    return 1.0 / (1.0 + jnp.exp(-v))


def group_sums(v):
    lane = lax.broadcasted_iota(jnp.int32, v.shape, 1)
    one = v + jnp.where((lane & 1) == 1, pltpu.roll(v, 1, 1), pltpu.roll(v, CH - 1, 1))
    return one + jnp.where((lane & 2) == 2, pltpu.roll(one, 2, 1), pltpu.roll(one, CH - 2, 1))


def kernel(
    n_row,
    n_col,
    coarse,
    ids,
    quad,
    land,
    lift_w,
    land_v,
    gain_ref,
    w1_hbm,
    w2_hbm,
    cot_hbm,
    feat,
    gcoarse,
    grads,
    glift,
    gland,
    ggain,
    padf,
    cand,
    up,
    ft,
    wext,
    w1,
    w2,
    cotv,
    wt1,
    wt2,
    ext,
    rh_s,
    rh_r,
    ch_s,
    ch_r,
    x3a,
    x3b,
    x3c,
    x3g,
    gic,
    gig,
    t2,
    gsc,
    glb,
    a1c,
    a1x,
    a1z,
    a2c,
    a2x,
    a2z,
    a3c,
    a3x,
    a3z,
    gbuf,
    cbuf,
    acc,
    xyb,
    zsrc,
    zb,
    ret_s,
    ret_r,
    dma,
    snd,
    rcv,
):
    row = lax.axis_index("row")
    col = lax.axis_index("col")
    at = {"row": row, "col": col}
    core_g = (("row", 1, 2),)
    xy_g = (("row", 2, n_row // 2), ("col", n_col // 2, 2))
    z_g = (("col", 1, n_col // 2),)
    n_xy = size_of(xy_g)
    n_z = size_of(z_g)
    members = float(n_row * TILE * n_col * TILE * (CH // GROUPS))
    report = 1.0 / math.sqrt(n_row * TILE * n_col * TILE)
    pixels_all = float(n_row * TILE * n_col * TILE)

    core = place_in(core_g, at)
    xy = place_in(xy_g, at)
    z = place_in(z_g, at)
    core_dev = member_of(core_g, at, 1 - core)

    def near(dr, dc):
        return ((row + dr + n_row) & (n_row - 1), (col + dc + n_col) & (n_col - 1))

    around = [(dr, dc) for dr in (-1, 0, 1) for dc in (-1, 0, 1)]

    def waiter(ref, k):
        return remote(ref, ref, snd.at[k], rcv.at[k], core_dev)

    loads = [
        pltpu.make_async_copy(w1_hbm, w1, dma.at[0]),
        pltpu.make_async_copy(w2_hbm, w2, dma.at[1]),
        pltpu.make_async_copy(cot_hbm, cotv, dma.at[2]),
    ]
    for load in loads:
        load.start()

    barrier = pltpu.get_barrier_semaphore()

    def greet(device, m):
        pl.semaphore_signal(barrier, inc=1, device_id=device, device_id_type=MESH)

    for dr, dc in around:
        if (dr, dc) != (0, 0):
            greet(near(dr, dc), 0)
    for group in (core_g, xy_g, z_g):
        each_other(group, at, greet)

    padf[...] = jnp.zeros_like(padf)
    padf[0:2, 0:CIN, :] = coarse[0, 0].astype(F32)
    padf[2, 0:CIN, :] = lift_w[...].astype(F32)
    cand[4] = padf[0:2].astype(BF16)

    codes = []
    for k in range(ids.shape[2]):
        block = ids[0, 0, k]
        owner = block >> 1
        slot_row = (owner >> log2(n_col)) - row + 1
        slot_col = (owner & (n_col - 1)) - col + 1
        codes.append(((quad[0, 0, k] * 9) + slot_row * 3 + slot_col) * 2 + (block & 1))

    def picks(q, s, m):
        want = (q * 9 + s) * 2 + m
        total = jnp.float32(0.0)
        for code in codes:
            total = total + jnp.where(code == want, jnp.float32(1.0), jnp.float32(0.0))
        return total

    weight = {(q, s, m): picks(q, s, m) for q in range(2) for s in range(9) for m in range(2)}

    pl.semaphore_wait(barrier, 8 + 1 + n_xy - 1 + n_z - 1)

    for s, (dr, dc) in enumerate(around):
        if s != 4:
            remote(cand.at[4], cand.at[8 - s], snd.at[0], rcv.at[0], near(dr, dc)).start()

    fine = lax.broadcasted_iota(jnp.int32, (CH, 512), 1)
    cell = lax.broadcasted_iota(jnp.int32, (CH, 512), 0)

    def hat(fine_at, cell_at, count):
        where = jnp.clip((fine_at.astype(F32) + 0.5) * 0.5 - 0.5, 0.0, count - 1.0)
        return jnp.maximum(1.0 - jnp.abs(where - cell_at.astype(F32)), 0.0)

    up[...] = (hat(fine >> 5, cell >> 4, 8) * hat(fine & 31, cell & 15, 16)).astype(BF16)

    pix = lax.broadcasted_iota(jnp.int32, (TILE, PIX), 1)
    line = lax.broadcasted_iota(jnp.int32, (TILE, PIX), 0)
    spread = jnp.where((pix & 31) == line, 1.0, 0.0).astype(BF16)
    lines = dot(land[...].astype(F32).astype(BF16), spread)
    lines = jnp.where((pix >> 5) == line, lines, 0.0).astype(BF16)
    wext[0:32] = padf[2].astype(BF16)
    for k, part in enumerate(split_three(jnp.broadcast_to(land_v[...], (32, CH)))):
        ft[32 * (k + 1) : 32 * (k + 2), :] = lines
        wext[32 * (k + 1) : 32 * (k + 2), :] = part

    for lo, hi in ((0, LEFT), (LEFT + TILE, WIDE)):
        ext[:, :, lo:hi, :] = jnp.zeros((2, ROWS, 8, CH), F32)
    for edge in (0, ROWS - 1):
        gic[edge] = jnp.zeros((WIDE, CH), BF16)
        gig[edge] = jnp.zeros((WIDE, CH), BF16)

    for load in loads:
        load.wait()
    for k in range(TAPS):
        wt1[:, k * CH : (k + 1) * CH] = w1[8 - k]
        wt2[:, k * CH : (k + 1) * CH] = w2[8 - k]
    ext[1, 2 : 2 + TILE, LEFT : LEFT + TILE, :] = cotv[...].astype(F32)

    waiter(cand.at[pl.ds(0, 8)], 0).wait_recv()
    sums = []
    for q in range(2):
        total = jnp.zeros((32, CH), F32)
        for s in range(9):
            for m in range(2):
                total = total + weight[q, s, m] * cand[s, m].astype(F32)
        sums.append(total)
    parts = split_three(jnp.concatenate(sums, axis=0))
    raised = dot(jnp.concatenate(parts, axis=0), up[...])
    raised = raised[0:64] + raised[64:128] + raised[128:192]
    ft[0:32, 0:512] = raised[0:32].astype(BF16)
    ft[0:32, 512:1024] = raised[32:64].astype(BF16)
    lifted = dot_tn(ft[...], wext[...])
    ext[0, 2 : 2 + TILE, LEFT : LEFT + TILE, :] = lifted.reshape(TILE, TILE, CH)
    mean_here = jnp.sum(lifted, axis=0, keepdims=True) * (1.0 / PIX)
    apart = lifted - mean_here
    square_here = jnp.sum(apart * apart, axis=0, keepdims=True)

    def start_level(group, buf, k, value):
        me = place_in(group, at)
        buf[me] = value

        def send(device, m):
            remote(buf.at[me], buf.at[me], snd.at[k], rcv.at[k], device).start()

        each_other(group, at, send)

    def end_level(buf, k):
        waiter(buf.at[pl.ds(0, buf.shape[0] - 1)], k).wait()
        return [buf[i] for i in range(buf.shape[0])]

    def add_up(values):
        while len(values) > 1:
            values = [a + b for a, b in zip(values[::2], values[1::2])]
        return values[0]

    def merge(values, count):
        mean = add_up([v[0:1] for v in values]) * (1.0 / len(values))
        square = add_up([v[1:2] for v in values])
        off = add_up([(v[0:1] - mean) * (v[0:1] - mean) for v in values])
        return jnp.concatenate([mean, square + count * off], axis=0)

    start_level(core_g, a1c, 1, jnp.concatenate([mean_here, square_here], axis=0))

    rh_s[0] = ext[:, 2:4, LEFT : LEFT + TILE, :]
    rh_s[1] = ext[:, TILE : TILE + 2, LEFT : LEFT + TILE, :]

    moments = merge(end_level(a1c, 1), float(PIX))
    start_level(xy_g, a1x, 2, moments)
    remote(rh_s.at[0], rh_r.at[0], snd.at[4], rcv.at[4], near(-1, 0)).start()
    remote(rh_s.at[1], rh_r.at[1], snd.at[4], rcv.at[4], near(1, 0)).start()

    moments = merge(end_level(a1x, 2), float(2 * PIX))
    start_level(z_g, a1z, 3, moments)

    waiter(rh_r, 4).wait()
    ext[:, 2 + TILE : 4 + TILE, LEFT : LEFT + TILE, :] = rh_r[0]
    ext[:, 0:2, LEFT : LEFT + TILE, :] = rh_r[1]
    for a in range(2):
        for k in range(2):
            ch_s[0, a, k, 0:ROWS, :] = ext[a, :, LEFT + k, :]
            ch_s[1, a, k, 0:ROWS, :] = ext[a, :, LEFT + TILE - 2 + k, :]
    remote(ch_s.at[0], ch_r.at[0], snd.at[5], rcv.at[5], near(0, -1)).start()
    remote(ch_s.at[1], ch_r.at[1], snd.at[5], rcv.at[5], near(0, 1)).start()
    waiter(ch_r, 5).wait()
    for a in range(2):
        for k in range(2):
            ext[a, :, LEFT + TILE + k, :] = ch_r[0, a, k, 0:ROWS, :]
            ext[a, :, LEFT - 2 + k, :] = ch_r[1, a, k, 0:ROWS, :]

    row_lo = jnp.where(row == 0, 2, 0)
    row_hi = jnp.where(row == n_row - 1, 2 + TILE, ROWS)
    col_lo = jnp.where(col == 0, LEFT, 0)
    col_hi = jnp.where(col == n_col - 1, LEFT + TILE, WIDE)

    def masks(first, count):
        r = lax.broadcasted_iota(jnp.int32, (count, WIDE, CH), 0) + first
        c = lax.broadcasted_iota(jnp.int32, (count, WIDE, CH), 1)
        in_grid = (r >= row_lo) & (r < row_hi) & (c >= col_lo) & (c < col_hi)
        in_tile = (r >= 2) & (r < 2 + TILE) & (c >= LEFT) & (c < LEFT + TILE)
        shape = (count * WIDE, CH)
        return in_grid.reshape(shape), in_tile.reshape(shape)

    def put_taps(x3, first, count, flat):
        length = count * WIDE
        x3[pl.ds(first, count), :, 0:CH] = pltpu.roll(flat, 1, 0).astype(BF16).reshape(count, WIDE, CH)
        x3[pl.ds(first, count), :, CH : 2 * CH] = flat.astype(BF16).reshape(count, WIDE, CH)
        x3[pl.ds(first, count), :, 2 * CH :] = (
            pltpu.roll(flat, length - 1, 0).astype(BF16).reshape(count, WIDE, CH)
        )

    def windows(x3, first, count):
        return jnp.concatenate(
            [x3[pl.ds(first - 1 + u, count)].reshape(count * WIDE, 3 * CH) for u in range(3)],
            axis=1,
        )

    def loop(trips, body):
        def step(i, carry):
            body(i)
            return carry

        lax.fori_loop(0, trips, step, 0)

    def cot_rows(i):
        first = i * 4
        in_grid, in_tile = masks(first, 4)
        flat = ext[1, pl.ds(first, 4)].reshape(4 * WIDE, CH)
        put_taps(x3c, first, 4, jnp.where(in_grid, flat, 0.0))
        gic[pl.ds(first, 4)] = jnp.where(in_tile, flat, 0.0).astype(BF16).reshape(4, WIDE, CH)

    loop(9, cot_rows)

    def cot_conv(i):
        first = 1 + i * 17
        t2[pl.ds(first, 17)] = dot_nt(windows(x3c, first, 17), wt2[...]).reshape(17, WIDE, CH)

    loop(2, cot_conv)

    moments = merge(end_level(a1z, 3), float(2 * n_xy * PIX))
    mean_ch = moments[0:1]
    group_mean = group_sums(mean_ch) * (GROUPS / CH)
    off = mean_ch - group_mean
    variance = group_sums(moments[1:2] + pixels_all * off * off) / members
    inv_spread = lax.rsqrt(variance + EPSILON)
    gain = gain_ref[...]

    def act_rows(i):
        first = i * 4
        in_grid, _ = masks(first, 4)
        flat = ext[0, pl.ds(first, 4)].reshape(4 * WIDE, CH)
        scaled = (flat - group_mean) * inv_spread * gain
        act = scaled * sigmoid(scaled)
        put_taps(x3a, first, 4, jnp.where(in_grid, act, 0.0))

    loop(9, act_rows)

    def hidden_rows(i):
        first = 1 + i * 17
        in_grid, in_tile = masks(first, 17)
        hidden = dot(windows(x3a, first, 17), w1[...].reshape(HALF, CH))
        gate = sigmoid(hidden)
        act = jnp.where(in_grid, hidden * gate, 0.0)
        slope = gate * (1.0 + hidden * (1.0 - gate))
        grad = jnp.where(in_grid, t2[pl.ds(first, 17)].reshape(17 * WIDE, CH) * slope, 0.0)
        put_taps(x3b, first, 17, act)
        put_taps(x3g, first, 17, grad)
        gig[pl.ds(first, 17)] = jnp.where(in_tile, grad, 0.0).astype(BF16).reshape(17, WIDE, CH)

    loop(2, hidden_rows)

    def tap_grads(x3, gi, half):
        length = (ROWS - 2) * WIDE
        grad = jnp.concatenate(
            [gi[2 - u : 2 - u + ROWS - 2].reshape(length, CH) for u in range(3)], axis=1
        )
        out = dot_tn(x3[1 : ROWS - 1].reshape(length, 3 * CH), grad)
        for u in range(3):
            for v in range(3):
                gbuf[half, (3 * u + v) * CH : (3 * u + v + 1) * CH, :] = out[
                    v * CH : (v + 1) * CH, u * CH : (u + 1) * CH
                ]

    tap_grads(x3b, gic, 0)
    tap_grads(x3a, gig, 1)

    swap = remote(gbuf.at[1 - core], cbuf, snd.at[6], rcv.at[6], core_dev)
    swap.start()

    def back_rows(i, sums):
        first = 2 + i * 8
        inner = slice(LEFT, LEFT + TILE)
        grad_act = dot_nt(windows(x3g, first, 8), wt1[...]).reshape(8, WIDE, CH)[:, inner, :]
        normed = (ext[0, pl.ds(first, 8), inner, :] - group_mean[None]) * inv_spread[None]
        scaled = normed * gain[None]
        gate = sigmoid(scaled)
        grad = grad_act * (gate * (1.0 + scaled * (1.0 - gate)))
        gsc[pl.ds(i * 8, 8)] = grad
        plain, cross = sums
        return (
            plain + jnp.sum(grad.reshape(32, 8, CH), axis=0),
            cross + jnp.sum((grad * normed).reshape(32, 8, CH), axis=0),
        )

    nothing = jnp.zeros((8, CH), F32)
    plain, cross = lax.fori_loop(0, 4, back_rows, (nothing, nothing))
    both = jnp.concatenate(
        [jnp.sum(plain, axis=0, keepdims=True), jnp.sum(cross, axis=0, keepdims=True)], axis=0
    )
    start_level(core_g, a2c, 7, both)

    swap.wait_recv()
    acc[...] = gbuf[core] + cbuf[...]
    share = HALF // n_xy

    def share_of(ref, m):
        return ref.at[pl.ds(pl.multiple_of(m * share, 8), share)]

    def send_share(device, m):
        remote(share_of(acc, m), xyb.at[xy], snd.at[8], rcv.at[8], device).start()

    start_level(xy_g, a2x, 9, add_up(end_level(a2c, 7)))
    each_other(xy_g, at, send_share)
    xyb[xy] = acc[pl.ds(pl.multiple_of(xy * share, 8), share), :]

    def out_rows(i):
        first = 2 + i * 16
        inner = slice(LEFT, LEFT + TILE)
        out = dot(windows(x3b, first, 16), w2[...].reshape(HALF, CH)).reshape(16, WIDE, CH)
        feat[pl.ds(i * 16, 16)] = (ext[0, pl.ds(first, 16), inner, :] + out[:, inner, :]).astype(BF16)

    loop(2, out_rows)

    start_level(z_g, a2z, 10, add_up(end_level(a2x, 9)))

    waiter(xyb.at[pl.ds(0, n_xy - 1)], 8).wait()
    zsrc[...] = add_up([xyb[i] for i in range(n_xy)])
    tiles = share // 8
    turn = (xy + 8 * core) & (n_z - 1)
    mine = (z - turn) & (n_z - 1)
    owner = mine < tiles
    strip = pl.ds(pl.multiple_of(jnp.minimum(mine, tiles - 1) * 8, 8), 8)

    def send_tile(t, carry):
        goal = (t + turn) & (n_z - 1)

        @pl.when(goal != z)
        def _():
            remote(
                zsrc.at[pl.ds(pl.multiple_of(t * 8, 8), 8)],
                zb.at[z],
                snd.at[11],
                rcv.at[11],
                member_of(z_g, at, goal),
            ).start()

        return carry

    lax.fori_loop(0, tiles, send_tile, 0)

    totals = add_up(end_level(a2z, 10))
    ggain[...] = totals[1:2] * report
    plain_sum = group_sums(totals[0:1] * gain) * (1.0 / members)
    cross_sum = group_sums(totals[1:2] * gain) * (1.0 / members)

    def lifted_rows(i):
        first = 2 + i * 8
        inner = slice(LEFT, LEFT + TILE)
        normed = (ext[0, pl.ds(first, 8), inner, :] - group_mean[None]) * inv_spread[None]
        grad = gsc[pl.ds(i * 8, 8)] * gain[None] - plain_sum[None] - normed * cross_sum[None]
        grad = inv_spread[None] * grad + ext[1, pl.ds(first, 8), inner, :]
        hi, lo = split_two(grad.reshape(256, CH))
        spot = pl.ds(pl.multiple_of(i * 256, 256), 256)
        glb[spot, 0:CH] = hi
        glb[spot, CH:] = lo

    loop(4, lifted_rows)
    both = dot(ft[...], glb[...])
    on_land = jnp.sum(both[32:64, 0:CH] + both[32:64, CH:], axis=0, keepdims=True)
    which = lax.broadcasted_iota(jnp.int32, (24, CH), 0)
    start_level(core_g, a3c, 12, jnp.where(which == CIN, on_land, both[0:24, 0:CH]))

    fine_hi, fine_lo = split_two(dot_nt(wext[0:32], glb[:, 0:CH]))
    stacked = jnp.concatenate(
        [fine_hi[:, 0:512], fine_hi[:, 512:], fine_lo[:, 0:512], fine_lo[:, 512:]], axis=0
    )
    lowered = dot_nt(stacked, up[...])
    lowered = lowered[0:64] + lowered[64:128]
    for s, (dr, dc) in enumerate(around):
        for m in range(2):
            ret_s[s, m] = weight[0, s, m] * lowered[0:24] + weight[1, s, m] * lowered[32:56]

    start_level(xy_g, a3x, 13, add_up(end_level(a3c, 12)))
    for s, (dr, dc) in enumerate(around):
        if s != 4:
            remote(ret_s.at[s], ret_r.at[8 - s], snd.at[14], rcv.at[14], near(dr, dc)).start()

    @pl.when(owner)
    def _():
        zb[z] = zsrc[strip, :]
        waiter(zb.at[pl.ds(0, n_z - 1)], 11).wait_recv()
        waiter(zsrc.at[pl.ds(0, share - 8)], 11).wait_send()
        whole = add_up([zb[i] for i in range(n_z)]) * report
        spot = pl.ds(pl.multiple_of(xy * share + mine * 8, 8), 8)
        grads[core, spot, :] = whole

        def send_whole(device, m):
            piece = grads.at[core, spot]
            remote(piece, piece, snd.at[15], rcv.at[15], device).start()

        each_other(z_g, at, send_whole)

    @pl.when(jnp.logical_not(owner))
    def _():
        waiter(zsrc, 11).wait_send()

    start_level(z_g, a3z, 16, add_up(end_level(a3x, 13)))

    @pl.when(owner)
    def _():
        waiter(zb.at[pl.ds(0, n_z - 1)], 15).wait_send()
        waiter(zsrc.at[pl.ds(0, share - 8)], 15).wait_recv()

    @pl.when(jnp.logical_not(owner))
    def _():
        waiter(zsrc, 15).wait_recv()

    here = grads.at[core, pl.ds(pl.multiple_of(xy * share, 8), share)]

    def send_back(device, m):
        remote(here, here, snd.at[17], rcv.at[17], device).start()

    each_other(xy_g, at, send_back)

    waiter(ret_r.at[pl.ds(0, 8)], 14).wait()
    for m in range(2):
        total = ret_s[4, m]
        for s in range(9):
            if s != 4:
                total = total + ret_r[s, m]
        gcoarse[0, 0, m] = total[0:CIN]

    totals = add_up(end_level(a3z, 16)) * report
    glift[...] = totals[0:CIN]
    gland[...] = totals[CIN : CIN + 1]

    waiter(xyb.at[pl.ds(0, n_xy - 1)], 17).wait()
    half = remote(grads.at[core], grads.at[core], snd.at[18], rcv.at[18], core_dev)
    half.start()
    waiter(cand.at[pl.ds(0, 8)], 0).wait_send()
    swap.wait_send()
    half.wait()


def shards(*args):
    (
        coarse_blocks,
        block_ids,
        quadrant,
        land_mask,
        lift_weight,
        land_vector,
        norm_gain,
        first_weight,
        second_weight,
        cotangent,
    ) = args
    n_row, n_col = lax.axis_size("row"), lax.axis_size("col")
    n_xy, n_z = n_row, n_col // 2

    def body(*refs):
        kernel(n_row, n_col, *refs)

    vmem = pl.BlockSpec(memory_space=pltpu.VMEM)
    smem = pl.BlockSpec(memory_space=pltpu.SMEM)
    anywhere = pl.BlockSpec(memory_space=pl.ANY)
    scratch = [
        pltpu.VMEM((3, 32, CH), F32),
        pltpu.VMEM((9, 2, 32, CH), BF16),
        pltpu.VMEM((CH, 512), BF16),
        pltpu.VMEM((CH, PIX), BF16),
        pltpu.VMEM((CH, CH), BF16),
        pltpu.VMEM((TAPS, CH, CH), BF16),
        pltpu.VMEM((TAPS, CH, CH), BF16),
        pltpu.VMEM((TILE, TILE, CH), BF16),
        pltpu.VMEM((CH, HALF), BF16),
        pltpu.VMEM((CH, HALF), BF16),
        pltpu.VMEM((2, ROWS, WIDE, CH), F32),
        pltpu.VMEM((2, 2, 2, TILE, CH), F32),
        pltpu.VMEM((2, 2, 2, TILE, CH), F32),
        pltpu.VMEM((2, 2, 2, 40, CH), F32),
        pltpu.VMEM((2, 2, 2, 40, CH), F32),
        pltpu.VMEM((ROWS, WIDE, 3 * CH), BF16),
        pltpu.VMEM((ROWS, WIDE, 3 * CH), BF16),
        pltpu.VMEM((ROWS, WIDE, 3 * CH), BF16),
        pltpu.VMEM((ROWS, WIDE, 3 * CH), BF16),
        pltpu.VMEM((ROWS, WIDE, CH), BF16),
        pltpu.VMEM((ROWS, WIDE, CH), BF16),
        pltpu.VMEM((ROWS, WIDE, CH), F32),
        pltpu.VMEM((TILE, TILE, CH), F32),
        pltpu.VMEM((PIX, 2 * CH), BF16),
        pltpu.VMEM((2, 2, CH), F32),
        pltpu.VMEM((n_xy, 2, CH), F32),
        pltpu.VMEM((n_z, 2, CH), F32),
        pltpu.VMEM((2, 2, CH), F32),
        pltpu.VMEM((n_xy, 2, CH), F32),
        pltpu.VMEM((n_z, 2, CH), F32),
        pltpu.VMEM((2, 24, CH), F32),
        pltpu.VMEM((n_xy, 24, CH), F32),
        pltpu.VMEM((n_z, 24, CH), F32),
        pltpu.VMEM((2, HALF, CH), F32),
        pltpu.VMEM((HALF, CH), F32),
        pltpu.VMEM((HALF, CH), F32),
        pltpu.VMEM((n_xy, HALF // n_xy, CH), F32),
        pltpu.VMEM((HALF // n_xy, CH), F32),
        pltpu.VMEM((n_z, 8, CH), F32),
        pltpu.VMEM((9, 2, 24, CH), F32),
        pltpu.VMEM((9, 2, 24, CH), F32),
        pltpu.SemaphoreType.DMA((3,)),
        pltpu.SemaphoreType.DMA((19,)),
        pltpu.SemaphoreType.DMA((19,)),
    ]
    features, grad_coarse, grads, grad_lift, grad_land, grad_gain = pl.pallas_call(
        body,
        out_shape=[
            jax.ShapeDtypeStruct((TILE, TILE, CH), BF16),
            jax.ShapeDtypeStruct((1, 1, 2, CIN, CH), F32),
            jax.ShapeDtypeStruct((2, HALF, CH), F32),
            jax.ShapeDtypeStruct((CIN, CH), F32),
            jax.ShapeDtypeStruct((1, CH), F32),
            jax.ShapeDtypeStruct((1, CH), F32),
        ],
        in_specs=[vmem, smem, smem, vmem, vmem, vmem, vmem, anywhere, anywhere, anywhere],
        out_specs=[vmem] * 6,
        scratch_shapes=scratch,
        compiler_params=pltpu.CompilerParams(
            collective_id=0, has_side_effects=True, vmem_limit_bytes=48 << 20
        ),
        name="block",
    )(
        coarse_blocks,
        block_ids,
        quadrant,
        land_mask,
        lift_weight,
        land_vector.reshape(1, CH),
        norm_gain.reshape(1, CH),
        first_weight,
        second_weight,
        cotangent,
    )
    return (
        features,
        grad_coarse,
        grads[1].reshape(TAPS, CH, CH),
        grads[0].reshape(TAPS, CH, CH),
        grad_lift,
        grad_land.reshape(CH),
        grad_gain.reshape(CH),
    )


def solution(mesh):
    in_specs = (
        P("row", "col", None, None, None),
        P("row", "col", None),
        P("row", "col", None),
        P("row", "col"),
        P(),
        P(),
        P(),
        P(),
        P(),
        P("row", "col", None),
    )
    out_specs = (P("row", "col", None), P("row", "col", None, None, None), P(), P(), P(), P(), P())
    return jax.shard_map(shards, mesh=mesh, in_specs=in_specs, out_specs=out_specs, check_vma=False)
```

```python
import math

import jax
import jax.numpy as jnp
from jax import lax
from jax.experimental import pallas as pl
from jax.experimental.pallas import tpu as pltpu
from jax.sharding import PartitionSpec as P

GROUPS = 32
EPSILON = 1e-05
MESH = pl.DeviceIdType.MESH
F32 = jnp.float32
BF16 = jnp.bfloat16

TILE = 32
ROWS = TILE + 4
WIDE = 48
LEFT = 8
CH = 128
CIN = 20
PIX = TILE * TILE
TAPS = 9
HALF = TAPS * CH


def log2(n):
    return n.bit_length() - 1


def size_of(group):
    n = 1
    for _, _, count in group:
        n *= count
    return n


def place_in(group, at):
    m = 0
    for axis, stride, count in group:
        m = (m << log2(count)) | ((at[axis] >> log2(stride)) & (count - 1))
    return m


def member_of(group, at, m):
    new = dict(at)
    for axis, stride, count in reversed(group):
        digit = m & (count - 1)
        m = m >> log2(count)
        new[axis] = (new[axis] & ~((count - 1) * stride)) | (digit << log2(stride))
    return (new["row"], new["col"])


def each_other(group, at, act):
    n = size_of(group)
    me = place_in(group, at)

    def body(k, carry):
        m = (me + k) & (n - 1)
        act(member_of(group, at, m), m)
        return carry

    lax.fori_loop(1, n, body, 0)


def remote(src, dst, send, recv, device):
    return pltpu.make_async_remote_copy(
        src_ref=src,
        dst_ref=dst,
        send_sem=send,
        recv_sem=recv,
        device_id=device,
        device_id_type=MESH,
    )


def dot(a, b):
    return jnp.dot(a, b, preferred_element_type=F32)


def dot_tn(a, b):
    return lax.dot_general(a, b, (((0,), (0,)), ((), ())), preferred_element_type=F32)


def dot_nt(a, b):
    return lax.dot_general(a, b, (((1,), (1,)), ((), ())), preferred_element_type=F32)


def split_two(x):
    hi = x.astype(BF16)
    return hi, (x - hi.astype(F32)).astype(BF16)


def split_three(x):
    hi = x.astype(BF16)
    rest = x - hi.astype(F32)
    mid = rest.astype(BF16)
    return hi, mid, (rest - mid.astype(F32)).astype(BF16)


def sigmoid(v):
    return 1.0 / (1.0 + jnp.exp(-v))


def group_sums(v):
    lane = lax.broadcasted_iota(jnp.int32, v.shape, 1)
    one = v + jnp.where((lane & 1) == 1, pltpu.roll(v, 1, 1), pltpu.roll(v, CH - 1, 1))
    return one + jnp.where((lane & 2) == 2, pltpu.roll(one, 2, 1), pltpu.roll(one, CH - 2, 1))


def kernel(
    n_row,
    n_col,
    coarse_hbm,
    ids_hbm,
    quad_hbm,
    land_hbm,
    lift_hbm,
    land_v_hbm,
    gain_hbm,
    w1_hbm,
    w2_hbm,
    cot_hbm,
    feat_hbm,
    gcoarse_hbm,
    grads_hbm,
    glift_hbm,
    gland_hbm,
    ggain_hbm,
    coarse,
    ids,
    quad,
    land,
    lift_w,
    land_v,
    gain_ref,
    padf,
    cand,
    up,
    ft,
    wext,
    w1,
    w2,
    cotv,
    wt1,
    wt2,
    ext,
    rh_s,
    rh_r,
    ch_s,
    ch_r,
    x3a,
    x3b,
    x3c,
    x3g,
    gic,
    gig,
    t2,
    gsc,
    glb,
    a1c,
    a1x,
    a1z,
    a2c,
    a2x,
    a2z,
    feat,
    gcoarse,
    grads,
    glift,
    gland,
    ggain,
    long_out,
    short_out,
    msend,
    mrecv,
    mxy,
    mown,
    mz,
    mall,
    glong,
    gshort,
    clong,
    cshort,
    along,
    ashort,
    xylong,
    xyshort,
    zsrc,
    zb,
    zres,
    ret_s,
    ret_r,
    dma,
    snd,
    rcv,
):
    row = lax.axis_index("row")
    col = lax.axis_index("col")
    at = {"row": row, "col": col}
    core_g = (("row", 1, 2),)
    xy_g = (("row", 2, n_row // 2), ("col", n_col // 2, 2))
    z_g = (("col", 1, n_col // 2),)
    n_xy = size_of(xy_g)
    n_z = size_of(z_g)
    members = float(n_row * TILE * n_col * TILE * (CH // GROUPS))
    report = 1.0 / math.sqrt(n_row * TILE * n_col * TILE)
    pixels_all = float(n_row * TILE * n_col * TILE)

    core = place_in(core_g, at)
    xy = place_in(xy_g, at)
    z = place_in(z_g, at)
    core_dev = member_of(core_g, at, 1 - core)

    def near(dr, dc):
        return ((row + dr + n_row) & (n_row - 1), (col + dc + n_col) & (n_col - 1))

    around = [(dr, dc) for dr in (-1, 0, 1) for dc in (-1, 0, 1)]

    def waiter(ref, k):
        return remote(ref, ref, snd.at[k], rcv.at[k], core_dev)

    barrier = pltpu.get_barrier_semaphore()

    def greet(device, m):
        pl.semaphore_signal(barrier, inc=1, device_id=device, device_id_type=MESH)

    for dr, dc in around:
        if (dr, dc) != (0, 0):
            greet(near(dr, dc), 0)
    for group in (core_g, xy_g, z_g):
        each_other(group, at, greet)

    pairs = [
        (coarse_hbm, coarse),
        (lift_hbm, lift_w),
        (ids_hbm, ids),
        (quad_hbm, quad),
        (land_hbm, land),
        (land_v_hbm, land_v),
        (gain_hbm, gain_ref),
        (cot_hbm, cotv),
        (w2_hbm, w2),
        (w1_hbm, w1),
    ]
    loads = [pltpu.make_async_copy(a, b, dma.at[k]) for k, (a, b) in enumerate(pairs)]
    for load in loads:
        load.start()

    padf[...] = jnp.zeros_like(padf)
    for load in loads[:2]:
        load.wait()
    for m in range(2):
        padf[m, 0:CIN, :] = coarse[:, m, :].astype(F32)
    padf[2, 0:CIN, :] = lift_w[...].astype(F32)
    cand[4] = padf[0:2].astype(BF16)

    pl.semaphore_wait(barrier, 8 + 1 + n_xy - 1 + n_z - 1)

    for s, (dr, dc) in enumerate(around):
        if s != 4:
            remote(cand.at[4], cand.at[8 - s], snd.at[0], rcv.at[0], near(dr, dc)).start()

    for load in loads[2:]:
        load.wait()
    codes = []
    for k in range(ids.shape[2]):
        block = ids[0, 0, k]
        owner = block >> 1
        slot_row = (owner >> log2(n_col)) - row + 1
        slot_col = (owner & (n_col - 1)) - col + 1
        codes.append(((quad[0, 0, k] * 9) + slot_row * 3 + slot_col) * 2 + (block & 1))

    def picks(q, s, m):
        want = (q * 9 + s) * 2 + m
        total = jnp.float32(0.0)
        for code in codes:
            total = total + jnp.where(code == want, jnp.float32(1.0), jnp.float32(0.0))
        return total

    weight = {(q, s, m): picks(q, s, m) for q in range(2) for s in range(9) for m in range(2)}

    fine = lax.broadcasted_iota(jnp.int32, (CH, 512), 1)
    cell = lax.broadcasted_iota(jnp.int32, (CH, 512), 0)

    def hat(fine_at, cell_at, count):
        where = jnp.clip((fine_at.astype(F32) + 0.5) * 0.5 - 0.5, 0.0, count - 1.0)
        return jnp.maximum(1.0 - jnp.abs(where - cell_at.astype(F32)), 0.0)

    up[...] = (hat(fine >> 5, cell >> 4, 8) * hat(fine & 31, cell & 15, 16)).astype(BF16)

    pix = lax.broadcasted_iota(jnp.int32, (TILE, PIX), 1)
    line = lax.broadcasted_iota(jnp.int32, (TILE, PIX), 0)
    spread = jnp.where((pix & 31) == line, 1.0, 0.0).astype(BF16)
    lines = dot(land[...].astype(F32).astype(BF16), spread)
    lines = jnp.where((pix >> 5) == line, lines, 0.0).astype(BF16)
    wext[0:32] = padf[2].astype(BF16)
    for k, part in enumerate(split_three(jnp.broadcast_to(land_v[...], (32, CH)))):
        ft[32 * (k + 1) : 32 * (k + 2), :] = lines
        wext[32 * (k + 1) : 32 * (k + 2), :] = part

    for lo, hi in ((0, LEFT), (LEFT + TILE, WIDE)):
        ext[:, :, lo:hi, :] = jnp.zeros((2, ROWS, 8, CH), F32)
    for edge in (0, ROWS - 1):
        gic[edge] = jnp.zeros((WIDE, CH), BF16)
        gig[edge] = jnp.zeros((WIDE, CH), BF16)

    for k in range(TAPS):
        wt1[:, k * CH : (k + 1) * CH] = w1[8 - k]
        wt2[:, k * CH : (k + 1) * CH] = w2[8 - k]
    ext[1, 2 : 2 + TILE, LEFT : LEFT + TILE, :] = cotv[...].astype(F32)

    waiter(cand.at[pl.ds(0, 8)], 0).wait_recv()
    sums = []
    for q in range(2):
        total = jnp.zeros((32, CH), F32)
        for s in range(9):
            for m in range(2):
                total = total + weight[q, s, m] * cand[s, m].astype(F32)
        sums.append(total)
    parts = split_three(jnp.concatenate(sums, axis=0))
    raised = dot(jnp.concatenate(parts, axis=0), up[...])
    raised = raised[0:64] + raised[64:128] + raised[128:192]
    ft[0:32, 0:512] = raised[0:32].astype(BF16)
    ft[0:32, 512:1024] = raised[32:64].astype(BF16)
    lifted = dot_tn(ft[...], wext[...])
    ext[0, 2 : 2 + TILE, LEFT : LEFT + TILE, :] = lifted.reshape(TILE, TILE, CH)
    mean_here = jnp.sum(lifted, axis=0, keepdims=True) * (1.0 / PIX)
    apart = lifted - mean_here
    square_here = jnp.sum(apart * apart, axis=0, keepdims=True)

    def start_level(group, buf, k, value):
        me = place_in(group, at)
        buf[me] = value

        def send(device, m):
            remote(buf.at[me], buf.at[me], snd.at[k], rcv.at[k], device).start()

        each_other(group, at, send)

    def end_level(buf, k):
        waiter(buf.at[pl.ds(0, buf.shape[0] - 1)], k).wait()
        return [buf[i] for i in range(buf.shape[0])]

    def add_up(values):
        while len(values) > 1:
            values = [a + b for a, b in zip(values[::2], values[1::2])]
        return values[0]

    def merge(values, count):
        mean = add_up([v[0:1] for v in values]) * (1.0 / len(values))
        square = add_up([v[1:2] for v in values])
        off = add_up([(v[0:1] - mean) * (v[0:1] - mean) for v in values])
        return jnp.concatenate([mean, square + count * off], axis=0)

    start_level(core_g, a1c, 1, jnp.concatenate([mean_here, square_here], axis=0))

    rh_s[0] = ext[:, 2:4, LEFT : LEFT + TILE, :]
    rh_s[1] = ext[:, TILE : TILE + 2, LEFT : LEFT + TILE, :]

    moments = merge(end_level(a1c, 1), float(PIX))
    start_level(xy_g, a1x, 2, moments)
    remote(rh_s.at[0], rh_r.at[0], snd.at[4], rcv.at[4], near(-1, 0)).start()
    remote(rh_s.at[1], rh_r.at[1], snd.at[4], rcv.at[4], near(1, 0)).start()

    moments = merge(end_level(a1x, 2), float(2 * PIX))
    start_level(z_g, a1z, 3, moments)

    waiter(rh_r, 4).wait()
    ext[:, 2 + TILE : 4 + TILE, LEFT : LEFT + TILE, :] = rh_r[0]
    ext[:, 0:2, LEFT : LEFT + TILE, :] = rh_r[1]
    for a in range(2):
        for k in range(2):
            ch_s[0, a, k, 0:ROWS, :] = ext[a, :, LEFT + k, :]
            ch_s[1, a, k, 0:ROWS, :] = ext[a, :, LEFT + TILE - 2 + k, :]
    remote(ch_s.at[0], ch_r.at[0], snd.at[5], rcv.at[5], near(0, -1)).start()
    remote(ch_s.at[1], ch_r.at[1], snd.at[5], rcv.at[5], near(0, 1)).start()
    waiter(ch_r, 5).wait()
    for a in range(2):
        for k in range(2):
            ext[a, :, LEFT + TILE + k, :] = ch_r[0, a, k, 0:ROWS, :]
            ext[a, :, LEFT - 2 + k, :] = ch_r[1, a, k, 0:ROWS, :]

    row_lo = jnp.where(row == 0, 2, 0)
    row_hi = jnp.where(row == n_row - 1, 2 + TILE, ROWS)
    col_lo = jnp.where(col == 0, LEFT, 0)
    col_hi = jnp.where(col == n_col - 1, LEFT + TILE, WIDE)

    def masks(first, count):
        r = lax.broadcasted_iota(jnp.int32, (count, WIDE, CH), 0) + first
        c = lax.broadcasted_iota(jnp.int32, (count, WIDE, CH), 1)
        in_grid = (r >= row_lo) & (r < row_hi) & (c >= col_lo) & (c < col_hi)
        in_tile = (r >= 2) & (r < 2 + TILE) & (c >= LEFT) & (c < LEFT + TILE)
        shape = (count * WIDE, CH)
        return in_grid.reshape(shape), in_tile.reshape(shape)

    def put_taps(x3, first, count, flat):
        length = count * WIDE
        x3[pl.ds(first, count), :, 0:CH] = pltpu.roll(flat, 1, 0).astype(BF16).reshape(count, WIDE, CH)
        x3[pl.ds(first, count), :, CH : 2 * CH] = flat.astype(BF16).reshape(count, WIDE, CH)
        x3[pl.ds(first, count), :, 2 * CH :] = (
            pltpu.roll(flat, length - 1, 0).astype(BF16).reshape(count, WIDE, CH)
        )

    def windows(x3, first, count):
        return jnp.concatenate(
            [x3[pl.ds(first - 1 + u, count)].reshape(count * WIDE, 3 * CH) for u in range(3)],
            axis=1,
        )

    def loop(trips, body):
        def step(i, carry):
            body(i)
            return carry

        lax.fori_loop(0, trips, step, 0)

    def cot_rows(i):
        first = i * 4
        in_grid, in_tile = masks(first, 4)
        flat = ext[1, pl.ds(first, 4)].reshape(4 * WIDE, CH)
        put_taps(x3c, first, 4, jnp.where(in_grid, flat, 0.0))
        gic[pl.ds(first, 4)] = jnp.where(in_tile, flat, 0.0).astype(BF16).reshape(4, WIDE, CH)

    loop(9, cot_rows)

    def cot_conv(i):
        first = 1 + i * 17
        t2[pl.ds(first, 17)] = dot_nt(windows(x3c, first, 17), wt2[...]).reshape(17, WIDE, CH)

    loop(2, cot_conv)

    moments = merge(end_level(a1z, 3), float(2 * n_xy * PIX))
    mean_ch = moments[0:1]
    group_mean = group_sums(mean_ch) * (GROUPS / CH)
    off = mean_ch - group_mean
    variance = group_sums(moments[1:2] + pixels_all * off * off) / members
    inv_spread = lax.rsqrt(variance + EPSILON)
    gain = gain_ref[...]

    def act_rows(i):
        first = i * 4
        in_grid, _ = masks(first, 4)
        flat = ext[0, pl.ds(first, 4)].reshape(4 * WIDE, CH)
        scaled = (flat - group_mean) * inv_spread * gain
        act = scaled * sigmoid(scaled)
        put_taps(x3a, first, 4, jnp.where(in_grid, act, 0.0))

    loop(9, act_rows)

    def hidden_rows(i):
        first = 1 + i * 17
        in_grid, in_tile = masks(first, 17)
        hidden = dot(windows(x3a, first, 17), w1[...].reshape(HALF, CH))
        gate = sigmoid(hidden)
        act = jnp.where(in_grid, hidden * gate, 0.0)
        slope = gate * (1.0 + hidden * (1.0 - gate))
        grad = jnp.where(in_grid, t2[pl.ds(first, 17)].reshape(17 * WIDE, CH) * slope, 0.0)
        put_taps(x3b, first, 17, act)
        put_taps(x3g, first, 17, grad)
        gig[pl.ds(first, 17)] = jnp.where(in_tile, grad, 0.0).astype(BF16).reshape(17, WIDE, CH)

    loop(2, hidden_rows)

    def tap_grads(x3, gi, half, us):
        length = (ROWS - 2) * WIDE
        grad = jnp.concatenate(
            [gi[2 - u : 2 - u + ROWS - 2].reshape(length, CH) for u in us], axis=1
        )
        out = dot_tn(x3[1 : ROWS - 1].reshape(length, 3 * CH), grad)
        for n, u in enumerate(us):
            for v in range(3):
                to, first = (glong, 3 * u + v) if u < 2 else (gshort, v)
                to[half, first * CH : (first + 1) * CH, :] = out[
                    v * CH : (v + 1) * CH, n * CH : (n + 1) * CH
                ]

    tap_grads(x3b, gic, 0, (0, 1))
    tap_grads(x3a, gig, 1, (0, 1))
    swap_long = remote(glong.at[1 - core], clong, snd.at[6], rcv.at[6], core_dev)
    swap_long.start()
    tap_grads(x3b, gic, 0, (2,))
    tap_grads(x3a, gig, 1, (2,))
    swap_short = remote(gshort.at[1 - core], cshort, snd.at[7], rcv.at[7], core_dev)
    swap_short.start()

    inner = slice(LEFT, LEFT + TILE)
    written = []

    def write_out(src, dst):
        written.append(pltpu.make_async_copy(src, dst, dma.at[10 + len(written)]))
        written[-1].start()

    def out_rows(i):
        first = 2 + i * 16
        out = dot(windows(x3b, first, 16), w2[...].reshape(HALF, CH)).reshape(16, WIDE, CH)
        feat[pl.ds(i * 16, 16)] = (ext[0, pl.ds(first, 16), inner, :] + out[:, inner, :]).astype(BF16)

    out_rows(0)

    def share_out(mine, theirs, to, landing, k):
        def add(m, carry):
            rows = pl.ds(pl.multiple_of(m * mine.shape[1] // n_xy, 8), mine.shape[1] // n_xy)
            total = mine[core, rows, :] + theirs[rows, :]
            to[m] = total
            return carry

        lax.fori_loop(0, n_xy, add, 0)

        def send(device, m):
            remote(to.at[m], landing.at[xy], snd.at[k], rcv.at[k], device).start()

        each_other(xy_g, at, send)
        landing[xy] = to[xy]

    swap_long.wait_recv()
    share_out(glong, clong, along, xylong, 8)
    swap_short.wait_recv()
    share_out(gshort, cshort, ashort, xyshort, 9)

    def back_rows(i, sums):
        first = 2 + i * 8
        grad_act = dot_nt(windows(x3g, first, 8), wt1[...]).reshape(8, WIDE, CH)[:, inner, :]
        normed = (ext[0, pl.ds(first, 8), inner, :] - group_mean[None]) * inv_spread[None]
        scaled = normed * gain[None]
        gate = sigmoid(scaled)
        grad = grad_act * (gate * (1.0 + scaled * (1.0 - gate)))
        gsc[pl.ds(i * 8, 8)] = grad
        straight = inv_spread[None] * (grad * gain[None]) + ext[1, pl.ds(first, 8), inner, :]
        spot = pl.ds(pl.multiple_of(i * 256, 256), 256)
        for k, part in enumerate(split_two(straight.reshape(256, CH)) + split_two(normed.reshape(256, CH))):
            glb[spot, k * CH : (k + 1) * CH] = part
        plain, cross = sums
        return (
            plain + jnp.sum(grad.reshape(32, 8, CH), axis=0),
            cross + jnp.sum((grad * normed).reshape(32, 8, CH), axis=0),
        )

    nothing = jnp.zeros((8, CH), F32)
    plain, cross = lax.fori_loop(0, 4, back_rows, (nothing, nothing))
    both = jnp.concatenate(
        [jnp.sum(plain, axis=0, keepdims=True), jnp.sum(cross, axis=0, keepdims=True)], axis=0
    )
    start_level(core_g, a2c, 10, both)

    which = lax.broadcasted_iota(jnp.int32, (24, CH), 0)
    lane = lax.broadcasted_iota(jnp.int32, (24, CH), 1)
    field_rows = dot(ft[...], glb[...])

    def by_field(k):
        part = field_rows[:, k * CH : (k + 1) * CH] + field_rows[:, (k + 1) * CH : (k + 2) * CH]
        on_land = jnp.sum(part[32:64], axis=0, keepdims=True)
        return jnp.where(which == CIN, on_land, part[0:24])

    alone = dot_nt(jnp.full((8, PIX), 1.0, BF16), ft[...])[0:1]
    msend[0] = by_field(0)
    msend[1] = jnp.where(which == CIN + 1, alone, by_field(2))
    m_swap = remote(msend.at[1 - core], mrecv, snd.at[13], rcv.at[13], core_dev)
    m_swap.start()

    out_rows(1)
    write_out(feat, feat_hbm)

    start_level(xy_g, a2x, 11, add_up(end_level(a2c, 10)))

    goals = [(5 * t + 8 * core + 1) & (n_xy - 1) for t in range(3)]
    held = [goal == xy for goal in goals]
    holder = held[0] | held[1] | held[2]

    m_swap.wait_recv()
    mown[...] = msend[core] + mrecv[...]
    for t in range(3):
        strip = mown.at[8 * t : 8 * t + 8]

        @pl.when(jnp.logical_not(held[t]))
        def _():
            remote(strip, mxy.at[xy], snd.at[14], rcv.at[14], member_of(xy_g, at, goals[t])).start()

        @pl.when(held[t])
        def _():
            mxy[xy] = mown[8 * t : 8 * t + 8]

    long_rows = glong.shape[1] // n_xy
    long_tiles = long_rows // 8
    tiles = zsrc.shape[0] // 8
    turn = (xy + 8 * core) & (n_z - 1)
    mine = (z - turn) & (n_z - 1)

    def send_tile(t, carry):
        goal = (t + turn) & (n_z - 1)

        @pl.when(goal != z)
        def _():
            remote(
                zsrc.at[pl.ds(pl.multiple_of(t * 8, 8), 8)],
                zb.at[z],
                snd.at[16],
                rcv.at[16],
                member_of(z_g, at, goal),
            ).start()

        return carry

    waiter(xylong.at[pl.ds(0, n_xy - 1)], 8).wait_recv()
    zsrc[0:long_rows] = add_up([xylong[i] for i in range(n_xy)])
    lax.fori_loop(0, long_tiles, send_tile, 0)
    waiter(xyshort.at[pl.ds(0, n_xy - 1)], 9).wait_recv()
    zsrc[long_rows:] = add_up([xyshort[i] for i in range(n_xy)])
    lax.fori_loop(long_tiles, tiles, send_tile, 0)

    start_level(z_g, a2z, 12, add_up(end_level(a2x, 11)))

    @pl.when(holder)
    def _():
        waiter(mxy.at[pl.ds(0, n_xy - 1)], 14).wait_recv()
        start_level(z_g, mz, 15, add_up([mxy[i] for i in range(n_xy)]))

    spot = pl.ds(pl.multiple_of(jnp.minimum(mine, tiles - 1) * 8, 8), 8)

    def whole_tile(k):
        zb[z] = zsrc[spot, :]
        waiter(zb.at[pl.ds(0, n_z - 1)], 16).wait_recv()
        zres[spot, :] = add_up([zb[i] for i in range(n_z)]) * report

        def send(device, m):
            remote(zres.at[spot], zres.at[spot], snd.at[17], rcv.at[k], device).start()

        each_other(z_g, at, send)

    in_long = mine < long_tiles
    in_short = (mine >= long_tiles) & (mine < tiles)
    owner = mine < tiles

    @pl.when(in_long)
    def _():
        whole_tile(17)

    @pl.when(in_short)
    def _():
        whole_tile(18)

    totals = add_up(end_level(a2z, 12))
    ggain[...] = totals[1:2] * report
    write_out(ggain, ggain_hbm)
    plain_sum = group_sums(totals[0:1] * gain) * (1.0 / members)
    cross_sum = group_sums(totals[1:2] * gain) * (1.0 / members)

    def lifted_rows(i):
        first = 2 + i * 8
        normed = (ext[0, pl.ds(first, 8), inner, :] - group_mean[None]) * inv_spread[None]
        grad = gsc[pl.ds(i * 8, 8)] * gain[None] - plain_sum[None] - normed * cross_sum[None]
        grad = inv_spread[None] * grad + ext[1, pl.ds(first, 8), inner, :]
        glb[pl.ds(pl.multiple_of(i * 256, 256), 256), 0:CH] = grad.reshape(256, CH).astype(BF16)

    loop(4, lifted_rows)

    fine_hi, fine_lo = split_two(dot_nt(wext[0:32], glb[:, 0:CH]))
    stacked = jnp.concatenate(
        [fine_hi[:, 0:512], fine_hi[:, 512:], fine_lo[:, 0:512], fine_lo[:, 512:]], axis=0
    )
    lowered = dot_nt(stacked, up[...])
    lowered = lowered[0:64] + lowered[64:128]
    for s, (dr, dc) in enumerate(around):
        for m in range(2):
            ret_s[s, m] = weight[0, s, m] * lowered[0:24] + weight[1, s, m] * lowered[32:56]
        if s != 4:
            remote(ret_s.at[s], ret_r.at[8 - s], snd.at[19], rcv.at[19], near(dr, dc)).start()

    @pl.when(holder)
    def _():
        waiter(mz.at[pl.ds(0, n_z - 1)], 15).wait()

    for t in range(3):
        place = mall.at[core, 8 * t : 8 * t + 8]

        @pl.when(held[t])
        def _():
            mall[core, 8 * t : 8 * t + 8, :] = add_up([mz[i] for i in range(n_z)])

            def send(device, m):
                remote(place, place, snd.at[20], rcv.at[20], device).start()

            each_other(xy_g, at, send)

    def wait_tiles(count, mine_too, k):
        @pl.when(mine_too)
        def _():
            waiter(zres.at[pl.ds(0, (count - 1) * 8)], k).wait_recv()

        @pl.when(jnp.logical_not(mine_too))
        def _():
            waiter(zres.at[pl.ds(0, count * 8)], k).wait_recv()

    def send_shares(out, k):
        piece = out.at[core, xy]

        def send(device, m):
            remote(piece, piece, snd.at[k], rcv.at[k], device).start()

        each_other(xy_g, at, send)

    wait_tiles(long_tiles, in_long, 17)
    long_out[core, xy] = zres[0:long_rows].astype(BF16)
    send_shares(long_out, 21)
    wait_tiles(tiles - long_tiles, in_short, 18)
    rest = zres[long_rows:]
    short_out[core, xy] = jnp.concatenate([rest, jnp.zeros((short_out.shape[2] - rest.shape[0], CH), F32)], axis=0).astype(BF16)
    send_shares(short_out, 22)

    waiter(ret_r.at[pl.ds(0, 8)], 19).wait()
    for m in range(2):
        total = ret_s[4, m]
        for s in range(9):
            if s != 4:
                total = total + ret_r[s, m]
        gcoarse[:, m, :] = total[0:CIN]
    write_out(gcoarse, gcoarse_hbm)

    @pl.when(holder)
    def _():
        waiter(mall.at[core, 0:16], 20).wait_recv()

    @pl.when(jnp.logical_not(holder))
    def _():
        waiter(mall.at[core], 20).wait_recv()

    m_back = remote(mall.at[core], mall.at[core], snd.at[23], rcv.at[23], core_dev)
    m_back.start()

    long_all = n_xy * long_rows
    short_rows = zsrc.shape[0] - long_rows

    def widen_long(half):
        grads[half, 0:long_all, :] = long_out[half].astype(F32).reshape(long_all, CH)
        piece = (half, pl.ds(0, long_all))
        write_out(grads.at[piece], grads_hbm.at[piece])

    def widen_short(half):
        part = short_out[half][:, 0:short_rows, :].astype(F32)
        grads[half, long_all:, :] = part.reshape(n_xy * short_rows, CH)
        piece = (half, pl.ds(long_all, n_xy * short_rows))
        write_out(grads.at[piece], grads_hbm.at[piece])

    waiter(long_out.at[core, pl.ds(0, n_xy - 1)], 21).wait_recv()
    back_long = remote(long_out.at[core], long_out.at[core], snd.at[24], rcv.at[24], core_dev)
    back_long.start()
    widen_long(core)

    m_back.wait()
    straight, crossed = mall[0], mall[1]
    fields = ((lane == which) & (which < CIN)) | ((which == CIN) & (lane >= 32) & (lane < 64))
    alone = jnp.sum(jnp.where(fields, crossed[CIN + 1 : CIN + 2], 0.0), axis=1, keepdims=True)
    lift_all = straight - (inv_spread * plain_sum) * alone - (inv_spread * cross_sum) * crossed
    lift_all = lift_all * report
    glift[...] = lift_all[0:CIN]
    gland[...] = lift_all[CIN : CIN + 1]
    write_out(glift, glift_hbm)
    write_out(gland, gland_hbm)

    waiter(short_out.at[core, pl.ds(0, n_xy - 1)], 22).wait_recv()
    back_short = remote(short_out.at[core], short_out.at[core], snd.at[25], rcv.at[25], core_dev)
    back_short.start()
    widen_short(core)

    waiter(cand.at[pl.ds(0, 8)], 0).wait_send()
    swap_long.wait_send()
    swap_short.wait_send()
    m_swap.wait_send()
    waiter(xylong.at[pl.ds(0, n_xy - 1)], 8).wait_send()
    waiter(xyshort.at[pl.ds(0, n_xy - 1)], 9).wait_send()
    waiter(long_out.at[core, pl.ds(0, n_xy - 1)], 21).wait_send()
    waiter(short_out.at[core, pl.ds(0, n_xy - 1)], 22).wait_send()

    @pl.when(holder)
    def _():
        waiter(mown.at[0:16], 14).wait_send()
        waiter(mxy.at[pl.ds(0, n_xy - 1)], 20).wait_send()

    @pl.when(jnp.logical_not(holder))
    def _():
        waiter(mown, 14).wait_send()

    @pl.when(owner)
    def _():
        waiter(zsrc.at[pl.ds(0, (tiles - 1) * 8)], 16).wait_send()
        waiter(zb.at[pl.ds(0, n_z - 1)], 17).wait_send()

    @pl.when(jnp.logical_not(owner))
    def _():
        waiter(zsrc, 16).wait_send()

    back_long.wait()
    widen_long(1 - core)
    back_short.wait()
    widen_short(1 - core)
    for copy in written:
        copy.wait()


def finish(feat, gcoarse, grads, glift, gland, ggain, *rest):
    outs, held, dma = rest[:7], rest[7:14], rest[14]
    sources = (grads.at[1], grads.at[0], feat, gcoarse, glift, gland, ggain)
    ins = [pltpu.make_async_copy(a, b, dma.at[0, k]) for k, (a, b) in enumerate(zip(sources, held))]
    for copy in ins:
        copy.start()
    copies = [pltpu.make_async_copy(a, b, dma.at[1, k]) for k, (a, b) in enumerate(zip(held, outs))]
    for arrived, copy in zip(ins, copies):
        arrived.wait()
        copy.start()
    for copy in copies:
        copy.wait()


def shards(*args):
    (
        coarse_blocks,
        block_ids,
        quadrant,
        land_mask,
        lift_weight,
        land_vector,
        norm_gain,
        first_weight,
        second_weight,
        cotangent,
    ) = args
    n_row, n_col = lax.axis_size("row"), lax.axis_size("col")
    n_xy, n_z = n_row, n_col // 2

    def body(*refs):
        kernel(n_row, n_col, *refs)

    hbm = pl.BlockSpec(memory_space=pltpu.HBM)
    rows_long = 6 * CH // n_xy
    rows_short = 3 * CH // n_xy
    pad_short = -(-rows_short // 16) * 16
    results = [
        jax.ShapeDtypeStruct((TILE, TILE, CH), BF16),
        jax.ShapeDtypeStruct((CIN, 2, CH), F32),
        jax.ShapeDtypeStruct((2, HALF, CH), F32),
        jax.ShapeDtypeStruct((CIN, CH), F32),
        jax.ShapeDtypeStruct((1, CH), F32),
        jax.ShapeDtypeStruct((1, CH), F32),
    ]
    scratch = [
        pltpu.VMEM((CIN, 2, CH), BF16),
        pltpu.SMEM(block_ids.shape, jnp.int32),
        pltpu.SMEM(quadrant.shape, jnp.int32),
        pltpu.VMEM((TILE, TILE), jnp.int32),
        pltpu.VMEM((CIN, CH), BF16),
        pltpu.VMEM((1, CH), F32),
        pltpu.VMEM((1, CH), F32),
        pltpu.VMEM((3, 32, CH), F32),
        pltpu.VMEM((9, 2, 32, CH), BF16),
        pltpu.VMEM((CH, 512), BF16),
        pltpu.VMEM((CH, PIX), BF16),
        pltpu.VMEM((CH, CH), BF16),
        pltpu.VMEM((TAPS, CH, CH), BF16),
        pltpu.VMEM((TAPS, CH, CH), BF16),
        pltpu.VMEM((TILE, TILE, CH), BF16),
        pltpu.VMEM((CH, HALF), BF16),
        pltpu.VMEM((CH, HALF), BF16),
        pltpu.VMEM((2, ROWS, WIDE, CH), F32),
        pltpu.VMEM((2, 2, 2, TILE, CH), F32),
        pltpu.VMEM((2, 2, 2, TILE, CH), F32),
        pltpu.VMEM((2, 2, 2, 40, CH), F32),
        pltpu.VMEM((2, 2, 2, 40, CH), F32),
        pltpu.VMEM((ROWS, WIDE, 3 * CH), BF16),
        pltpu.VMEM((ROWS, WIDE, 3 * CH), BF16),
        pltpu.VMEM((ROWS, WIDE, 3 * CH), BF16),
        pltpu.VMEM((ROWS, WIDE, 3 * CH), BF16),
        pltpu.VMEM((ROWS, WIDE, CH), BF16),
        pltpu.VMEM((ROWS, WIDE, CH), BF16),
        pltpu.VMEM((ROWS, WIDE, CH), F32),
        pltpu.VMEM((TILE, TILE, CH), F32),
        pltpu.VMEM((PIX, 4 * CH), BF16),
        pltpu.VMEM((2, 2, CH), F32),
        pltpu.VMEM((n_xy, 2, CH), F32),
        pltpu.VMEM((n_z, 2, CH), F32),
        pltpu.VMEM((2, 2, CH), F32),
        pltpu.VMEM((n_xy, 2, CH), F32),
        pltpu.VMEM((n_z, 2, CH), F32),
        pltpu.VMEM((TILE, TILE, CH), BF16),
        pltpu.VMEM((CIN, 2, CH), F32),
        pltpu.VMEM((2, HALF, CH), F32),
        pltpu.VMEM((CIN, CH), F32),
        pltpu.VMEM((1, CH), F32),
        pltpu.VMEM((1, CH), F32),
        pltpu.VMEM((2, n_xy, rows_long, CH), BF16),
        pltpu.VMEM((2, n_xy, pad_short, CH), BF16),
        pltpu.VMEM((2, 24, CH), F32),
        pltpu.VMEM((24, CH), F32),
        pltpu.VMEM((n_xy, 8, CH), F32),
        pltpu.VMEM((24, CH), F32),
        pltpu.VMEM((n_z, 8, CH), F32),
        pltpu.VMEM((2, 24, CH), F32),
        pltpu.VMEM((2, 6 * CH, CH), F32),
        pltpu.VMEM((2, 3 * CH, CH), F32),
        pltpu.VMEM((6 * CH, CH), F32),
        pltpu.VMEM((3 * CH, CH), F32),
        pltpu.VMEM((n_xy, rows_long, CH), F32),
        pltpu.VMEM((n_xy, rows_short, CH), F32),
        pltpu.VMEM((n_xy, rows_long, CH), F32),
        pltpu.VMEM((n_xy, rows_short, CH), F32),
        pltpu.VMEM((rows_long + rows_short, CH), F32),
        pltpu.VMEM((n_z, 8, CH), F32),
        pltpu.VMEM((rows_long + rows_short, CH), F32),
        pltpu.VMEM((9, 2, 24, CH), F32),
        pltpu.VMEM((9, 2, 24, CH), F32),
        pltpu.SemaphoreType.DMA((19,)),
        pltpu.SemaphoreType.DMA((26,)),
        pltpu.SemaphoreType.DMA((26,)),
    ]
    parts = pl.pallas_call(
        body,
        out_shape=results,
        in_specs=[hbm] * 10,
        out_specs=[hbm] * 6,
        scratch_shapes=scratch,
        compiler_params=pltpu.CompilerParams(
            collective_id=0, has_side_effects=True, vmem_limit_bytes=60 << 20
        ),
        name="block",
    )(
        jnp.transpose(coarse_blocks[0, 0], (1, 0, 2)),
        block_ids,
        quadrant,
        land_mask,
        lift_weight,
        land_vector.reshape(1, CH),
        norm_gain.reshape(1, CH),
        first_weight,
        second_weight,
        cotangent,
    )
    wide = jax.ShapeDtypeStruct((HALF, CH), F32)
    outputs = [wide, wide, results[0], results[1]] + results[3:]
    grad_first, grad_second, features, grad_coarse, grad_lift, grad_land, grad_gain = pl.pallas_call(
        finish,
        out_shape=outputs,
        in_specs=[hbm] * 6,
        out_specs=[hbm] * 7,
        scratch_shapes=[pltpu.VMEM(out.shape, out.dtype) for out in outputs]
        + [pltpu.SemaphoreType.DMA((2, 7))],
        compiler_params=pltpu.CompilerParams(vmem_limit_bytes=60 << 20),
        name="finish",
    )(*parts)
    return (
        features,
        jnp.transpose(grad_coarse, (1, 0, 2))[None, None],
        grad_first.reshape(TAPS, CH, CH),
        grad_second.reshape(TAPS, CH, CH),
        grad_lift,
        grad_land.reshape(CH),
        grad_gain.reshape(CH),
    )


def solution(mesh):
    in_specs = (
        P("row", "col", None, None, None),
        P("row", "col", None),
        P("row", "col", None),
        P("row", "col"),
        P(),
        P(),
        P(),
        P(),
        P(),
        P("row", "col", None),
    )
    out_specs = (P("row", "col", None), P("row", "col", None, None, None), P(), P(), P(), P(), P())
    return jax.shard_map(shards, mesh=mesh, in_specs=in_specs, out_specs=out_specs, check_vma=False)
```

```python
import math

import jax
import jax.numpy as jnp
from jax import lax
from jax.experimental import pallas as pl
from jax.experimental.pallas import tpu as pltpu
from jax.sharding import PartitionSpec as P

GROUPS = 32
EPSILON = 1e-05
MESH = pl.DeviceIdType.MESH
F32 = jnp.float32
BF16 = jnp.bfloat16

TILE = 32
ROWS = TILE + 4
WIDE = 48
LEFT = 8
CH = 128
CIN = 20
PIX = TILE * TILE
TAPS = 9
FAR_FIRST = tuple(
    sum(step << (4 * k) for k, step in enumerate(half))
    for half in ((5, 3, 7, 12, 13, 1, 4, 2), (10, 11, 14, 15, 6, 8, 9))
)
HALF = TAPS * CH


def log2(n):
    return n.bit_length() - 1


def size_of(group):
    n = 1
    for _, _, count in group:
        n *= count
    return n


def place_in(group, at):
    m = 0
    for axis, stride, count in group:
        m = (m << log2(count)) | ((at[axis] >> log2(stride)) & (count - 1))
    return m


def member_of(group, at, m):
    new = dict(at)
    for axis, stride, count in reversed(group):
        digit = m & (count - 1)
        m = m >> log2(count)
        new[axis] = (new[axis] & ~((count - 1) * stride)) | (digit << log2(stride))
    return (new["row"], new["col"])


def each_other(group, at, act):
    n = size_of(group)
    me = place_in(group, at)
    flat = len(group) == 2 and n == 16

    def body(k, carry):
        if flat:
            step = jnp.where(k < 8, FAR_FIRST[0], FAR_FIRST[1])
            m = me ^ ((step >> ((k & 7) * 4)) & 15)
        else:
            away = (k + 1) >> 1
            m = (me + n // 2 + jnp.where((k & 1) == 1, away, -away) + n) & (n - 1)
        act(member_of(group, at, m), m)
        return carry

    lax.fori_loop(0, n - 1, body, 0)


def remote(src, dst, send, recv, device):
    return pltpu.make_async_remote_copy(
        src_ref=src,
        dst_ref=dst,
        send_sem=send,
        recv_sem=recv,
        device_id=device,
        device_id_type=MESH,
    )


def dot(a, b):
    return jnp.dot(a, b, preferred_element_type=F32)


def dot_tn(a, b):
    return lax.dot_general(a, b, (((0,), (0,)), ((), ())), preferred_element_type=F32)


def dot_nt(a, b):
    return lax.dot_general(a, b, (((1,), (1,)), ((), ())), preferred_element_type=F32)


def split_two(x):
    hi = x.astype(BF16)
    return hi, (x - hi.astype(F32)).astype(BF16)


def split_three(x):
    hi = x.astype(BF16)
    rest = x - hi.astype(F32)
    mid = rest.astype(BF16)
    return hi, mid, (rest - mid.astype(F32)).astype(BF16)


def sigmoid(v):
    return 1.0 / (1.0 + jnp.exp(-v))


def group_sums(v):
    lane = lax.broadcasted_iota(jnp.int32, v.shape, 1)
    one = v + jnp.where((lane & 1) == 1, pltpu.roll(v, 1, 1), pltpu.roll(v, CH - 1, 1))
    return one + jnp.where((lane & 2) == 2, pltpu.roll(one, 2, 1), pltpu.roll(one, CH - 2, 1))


def kernel(
    n_row,
    n_col,
    coarse_hbm,
    ids_hbm,
    quad_hbm,
    land_hbm,
    lift_hbm,
    land_v_hbm,
    gain_hbm,
    w1_hbm,
    w2_hbm,
    cot_hbm,
    feat_hbm,
    gcoarse_hbm,
    grads_hbm,
    glift_hbm,
    gland_hbm,
    ggain_hbm,
    coarse,
    ids,
    quad,
    land,
    lift_w,
    land_v,
    gain_ref,
    padf,
    cand,
    up,
    ft,
    wext,
    w1,
    w2,
    cotv,
    wt1,
    wt2,
    ext,
    rh_s,
    rh_r,
    ch_s,
    ch_r,
    x3ab,
    x3c,
    x3g,
    gi,
    t2,
    gsc,
    glb,
    a1c,
    a1x,
    a1z,
    a2c,
    a2x,
    a2z,
    feat,
    gcoarse,
    grads,
    glift,
    gland,
    ggain,
    long_out,
    short_out,
    msend,
    mrecv,
    mxy,
    mown,
    mz,
    mall,
    glong,
    gshort,
    clong,
    cshort,
    along,
    ashort,
    xylong,
    xyshort,
    zsrc,
    zb,
    zres,
    ret_s,
    ret_r,
    dma,
    snd,
    rcv,
):
    row = lax.axis_index("row")
    col = lax.axis_index("col")
    at = {"row": row, "col": col}
    core_g = (("row", 1, 2),)
    xy_g = (("row", 2, n_row // 2), ("col", n_col // 2, 2))
    z_g = (("col", 1, n_col // 2),)
    n_xy = size_of(xy_g)
    n_z = size_of(z_g)
    members = float(n_row * TILE * n_col * TILE * (CH // GROUPS))
    report = 1.0 / math.sqrt(n_row * TILE * n_col * TILE)
    pixels_all = float(n_row * TILE * n_col * TILE)

    core = place_in(core_g, at)
    xy = place_in(xy_g, at)
    z = place_in(z_g, at)
    core_dev = member_of(core_g, at, 1 - core)
    x3b, x3a = x3ab.at[0], x3ab.at[1]
    gic, gig = gi.at[0], gi.at[1]

    def near(dr, dc):
        return ((row + dr + n_row) & (n_row - 1), (col + dc + n_col) & (n_col - 1))

    around = [(dr, dc) for dr in (-1, 0, 1) for dc in (-1, 0, 1)]

    def waiter(ref, k):
        return remote(ref, ref, snd.at[k], rcv.at[k], core_dev)

    barrier = pltpu.get_barrier_semaphore()

    def greet(device, m):
        pl.semaphore_signal(barrier, inc=1, device_id=device, device_id_type=MESH)

    for dr, dc in around:
        if (dr, dc) != (0, 0):
            greet(near(dr, dc), 0)
    for group in (core_g, xy_g, z_g):
        each_other(group, at, greet)

    pairs = [
        (coarse_hbm, coarse),
        (lift_hbm, lift_w),
        (ids_hbm, ids),
        (quad_hbm, quad),
        (land_hbm, land),
        (land_v_hbm, land_v),
        (gain_hbm, gain_ref),
        (cot_hbm, cotv),
        (w2_hbm, w2),
        (w1_hbm, w1),
    ]
    loads = [pltpu.make_async_copy(a, b, dma.at[k]) for k, (a, b) in enumerate(pairs)]
    for load in loads:
        load.start()

    padf[...] = jnp.zeros_like(padf)
    for load in loads[:2]:
        load.wait()
    for m in range(2):
        padf[m, 0:CIN, :] = coarse[:, m, :].astype(F32)
    padf[2, 0:CIN, :] = lift_w[...].astype(F32)
    cand[4] = padf[0:2].astype(BF16)

    pl.semaphore_wait(barrier, 8 + 1 + n_xy - 1 + n_z - 1)

    for s, (dr, dc) in enumerate(around):
        if s != 4:
            remote(cand.at[4], cand.at[8 - s], snd.at[0], rcv.at[0], near(dr, dc)).start()

    for load in loads[2:]:
        load.wait()
    codes = []
    for k in range(ids.shape[2]):
        block = ids[0, 0, k]
        owner = block >> 1
        slot_row = (owner >> log2(n_col)) - row + 1
        slot_col = (owner & (n_col - 1)) - col + 1
        codes.append(((quad[0, 0, k] * 9) + slot_row * 3 + slot_col) * 2 + (block & 1))

    def picks(q, s, m):
        want = (q * 9 + s) * 2 + m
        total = jnp.float32(0.0)
        for code in codes:
            total = total + jnp.where(code == want, jnp.float32(1.0), jnp.float32(0.0))
        return total

    weight = {(q, s, m): picks(q, s, m) for q in range(2) for s in range(9) for m in range(2)}

    fine = lax.broadcasted_iota(jnp.int32, (CH, 512), 1)
    cell = lax.broadcasted_iota(jnp.int32, (CH, 512), 0)

    def hat(fine_at, cell_at, count):
        where = jnp.clip((fine_at.astype(F32) + 0.5) * 0.5 - 0.5, 0.0, count - 1.0)
        return jnp.maximum(1.0 - jnp.abs(where - cell_at.astype(F32)), 0.0)

    up[...] = (hat(fine >> 5, cell >> 4, 8) * hat(fine & 31, cell & 15, 16)).astype(BF16)

    pix = lax.broadcasted_iota(jnp.int32, (TILE, PIX), 1)
    line = lax.broadcasted_iota(jnp.int32, (TILE, PIX), 0)
    spread = jnp.where((pix & 31) == line, 1.0, 0.0).astype(BF16)
    lines = dot(land[...].astype(F32).astype(BF16), spread)
    lines = jnp.where((pix >> 5) == line, lines, 0.0).astype(BF16)
    wext[0:32] = padf[2].astype(BF16)
    for k, part in enumerate(split_three(jnp.broadcast_to(land_v[...], (32, CH)))):
        ft[32 * (k + 1) : 32 * (k + 2), :] = lines
        wext[32 * (k + 1) : 32 * (k + 2), :] = part

    for lo, hi in ((0, LEFT), (LEFT + TILE, WIDE)):
        ext[:, :, lo:hi, :] = jnp.zeros((2, ROWS, 8, CH), F32)
    for edge in (0, ROWS - 1):
        gi[:, edge] = jnp.zeros((2, WIDE, CH), BF16)

    for k in range(TAPS):
        wt1[:, k * CH : (k + 1) * CH] = w1[8 - k]
        wt2[:, k * CH : (k + 1) * CH] = w2[8 - k]
    ext[1, 2 : 2 + TILE, LEFT : LEFT + TILE, :] = cotv[...].astype(F32)

    def pack_rows(a):
        rh_s[a, 0] = ext[a, 2:4, LEFT : LEFT + TILE, :]
        rh_s[a, 1] = ext[a, TILE : TILE + 2, LEFT : LEFT + TILE, :]

    def send_rows(a, k):
        for side, step in ((0, -1), (1, 1)):
            remote(rh_s.at[a, side], rh_r.at[a, side], snd.at[k], rcv.at[k], near(step, 0)).start()

    def rows_to_columns(a, k_rows, k_cols):
        waiter(rh_r.at[a], k_rows).wait()
        ext[a, 2 + TILE : 4 + TILE, LEFT : LEFT + TILE, :] = rh_r[a, 0]
        ext[a, 0:2, LEFT : LEFT + TILE, :] = rh_r[a, 1]
        for k in range(2):
            ch_s[a, 0, k, 0:ROWS, :] = ext[a, :, LEFT + k, :]
            ch_s[a, 1, k, 0:ROWS, :] = ext[a, :, LEFT + TILE - 2 + k, :]
        for side, step in ((0, -1), (1, 1)):
            remote(ch_s.at[a, side], ch_r.at[a, side], snd.at[k_cols], rcv.at[k_cols], near(0, step)).start()

    def put_columns(a, k_cols):
        waiter(ch_r.at[a], k_cols).wait()
        for k in range(2):
            ext[a, :, LEFT + TILE + k, :] = ch_r[a, 0, k, 0:ROWS, :]
            ext[a, :, LEFT - 2 + k, :] = ch_r[a, 1, k, 0:ROWS, :]

    pack_rows(1)
    send_rows(1, 27)

    waiter(cand.at[pl.ds(0, 8)], 0).wait_recv()
    sums = []
    for q in range(2):
        total = jnp.zeros((32, CH), F32)
        for s in range(9):
            for m in range(2):
                total = total + weight[q, s, m] * cand[s, m].astype(F32)
        sums.append(total)
    parts = split_three(jnp.concatenate(sums, axis=0))
    raised = dot(jnp.concatenate(parts, axis=0), up[...])
    raised = raised[0:64] + raised[64:128] + raised[128:192]
    ft[0:32, 0:512] = raised[0:32].astype(BF16)
    ft[0:32, 512:1024] = raised[32:64].astype(BF16)
    lifted = dot_tn(ft[...], wext[...])
    ext[0, 2 : 2 + TILE, LEFT : LEFT + TILE, :] = lifted.reshape(TILE, TILE, CH)
    mean_here = jnp.sum(lifted, axis=0, keepdims=True) * (1.0 / PIX)
    apart = lifted - mean_here
    square_here = jnp.sum(apart * apart, axis=0, keepdims=True)

    def start_level(group, buf, k, value):
        me = place_in(group, at)
        buf[me] = value

        def send(device, m):
            remote(buf.at[me], buf.at[me], snd.at[k], rcv.at[k], device).start()

        each_other(group, at, send)

    def end_level(buf, k):
        waiter(buf.at[pl.ds(0, buf.shape[0] - 1)], k).wait()
        return [buf[i] for i in range(buf.shape[0])]

    def add_up(values):
        while len(values) > 1:
            values = [a + b for a, b in zip(values[::2], values[1::2])]
        return values[0]

    def merge(values, count):
        mean = add_up([v[0:1] for v in values]) * (1.0 / len(values))
        square = add_up([v[1:2] for v in values])
        off = add_up([(v[0:1] - mean) * (v[0:1] - mean) for v in values])
        return jnp.concatenate([mean, square + count * off], axis=0)

    start_level(core_g, a1c, 1, jnp.concatenate([mean_here, square_here], axis=0))

    pack_rows(0)
    rows_to_columns(1, 27, 28)

    moments = merge(end_level(a1c, 1), float(PIX))
    start_level(xy_g, a1x, 2, moments)
    send_rows(0, 4)
    rows_to_columns(0, 4, 5)

    moments = merge(end_level(a1x, 2), float(2 * PIX))
    start_level(z_g, a1z, 3, moments)
    put_columns(1, 28)

    row_lo = jnp.where(row == 0, 2, 0)
    row_hi = jnp.where(row == n_row - 1, 2 + TILE, ROWS)
    col_lo = jnp.where(col == 0, LEFT, 0)
    col_hi = jnp.where(col == n_col - 1, LEFT + TILE, WIDE)

    def masks(first, count):
        r = lax.broadcasted_iota(jnp.int32, (count, WIDE, CH), 0) + first
        c = lax.broadcasted_iota(jnp.int32, (count, WIDE, CH), 1)
        in_grid = (r >= row_lo) & (r < row_hi) & (c >= col_lo) & (c < col_hi)
        in_tile = (r >= 2) & (r < 2 + TILE) & (c >= LEFT) & (c < LEFT + TILE)
        shape = (count * WIDE, CH)
        return in_grid.reshape(shape), in_tile.reshape(shape)

    def put_taps(x3, first, count, flat):
        length = count * WIDE
        x3[pl.ds(first, count), :, 0:CH] = pltpu.roll(flat, 1, 0).astype(BF16).reshape(count, WIDE, CH)
        x3[pl.ds(first, count), :, CH : 2 * CH] = flat.astype(BF16).reshape(count, WIDE, CH)
        x3[pl.ds(first, count), :, 2 * CH :] = (
            pltpu.roll(flat, length - 1, 0).astype(BF16).reshape(count, WIDE, CH)
        )

    def windows(x3, first, count):
        return jnp.concatenate(
            [x3[pl.ds(first - 1 + u, count)].reshape(count * WIDE, 3 * CH) for u in range(3)],
            axis=1,
        )

    def loop(trips, body):
        def step(i, carry):
            body(i)
            return carry

        lax.fori_loop(0, trips, step, 0)

    def cot_rows(i):
        first = i * 4
        in_grid, in_tile = masks(first, 4)
        flat = ext[1, pl.ds(first, 4)].reshape(4 * WIDE, CH)
        put_taps(x3c, first, 4, jnp.where(in_grid, flat, 0.0))
        gic[pl.ds(first, 4)] = jnp.where(in_tile, flat, 0.0).astype(BF16).reshape(4, WIDE, CH)

    loop(9, cot_rows)

    def cot_conv(i):
        first = 1 + i * 17
        t2[pl.ds(first, 17)] = dot_nt(windows(x3c, first, 17), wt2[...]).reshape(17, WIDE, CH)

    loop(2, cot_conv)
    put_columns(0, 5)

    moments = merge(end_level(a1z, 3), float(2 * n_xy * PIX))
    mean_ch = moments[0:1]
    group_mean = group_sums(mean_ch) * (GROUPS / CH)
    off = mean_ch - group_mean
    variance = group_sums(moments[1:2] + pixels_all * off * off) / members
    inv_spread = lax.rsqrt(variance + EPSILON)
    gain = gain_ref[...]

    def act_rows(i):
        first = i * 4
        in_grid, _ = masks(first, 4)
        flat = ext[0, pl.ds(first, 4)].reshape(4 * WIDE, CH)
        scaled = (flat - group_mean) * inv_spread * gain
        act = scaled * sigmoid(scaled)
        put_taps(x3a, first, 4, jnp.where(in_grid, act, 0.0))

    loop(9, act_rows)

    def hidden_rows(i):
        first = 1 + i * 17
        in_grid, in_tile = masks(first, 17)
        hidden = dot(windows(x3a, first, 17), w1[...].reshape(HALF, CH))
        gate = sigmoid(hidden)
        act = jnp.where(in_grid, hidden * gate, 0.0)
        slope = gate * (1.0 + hidden * (1.0 - gate))
        grad = jnp.where(in_grid, t2[pl.ds(first, 17)].reshape(17 * WIDE, CH) * slope, 0.0)
        put_taps(x3b, first, 17, act)
        put_taps(x3g, first, 17, grad)
        gig[pl.ds(first, 17)] = jnp.where(in_tile, grad, 0.0).astype(BF16).reshape(17, WIDE, CH)

    loop(2, hidden_rows)

    def tap_grads(half):
        length = (ROWS - 2) * WIDE
        grad = jnp.concatenate(
            [gi[half, 2 - u : 2 - u + ROWS - 2].reshape(length, CH) for u in range(3)], axis=1
        )
        out = dot_tn(x3ab[half, 1 : ROWS - 1].reshape(length, 3 * CH), grad)
        for u in range(3):
            for v in range(3):
                to, first = (glong, 3 * u + v) if u < 2 else (gshort, v)
                to[half, first * CH : (first + 1) * CH, :] = out[
                    v * CH : (v + 1) * CH, u * CH : (u + 1) * CH
                ]

    tap_grads(1 - core)
    swap_long = remote(glong.at[1 - core], clong, snd.at[6], rcv.at[6], core_dev)
    swap_long.start()
    swap_short = remote(gshort.at[1 - core], cshort, snd.at[7], rcv.at[7], core_dev)
    swap_short.start()
    tap_grads(core)

    inner = slice(LEFT, LEFT + TILE)
    written = []

    def write_out(src, dst):
        written.append(pltpu.make_async_copy(src, dst, dma.at[10 + len(written)]))
        written[-1].start()

    def out_rows(i):
        first = 2 + i * 16
        out = dot(windows(x3b, first, 16), w2[...].reshape(HALF, CH)).reshape(16, WIDE, CH)
        feat[pl.ds(i * 16, 16)] = (ext[0, pl.ds(first, 16), inner, :] + out[:, inner, :]).astype(BF16)

    def share_out(mine, theirs, to, landing, k):
        def add(m, carry):
            rows = pl.ds(pl.multiple_of(m * mine.shape[1] // n_xy, 8), mine.shape[1] // n_xy)
            total = mine[core, rows, :] + theirs[rows, :]
            to[m] = total
            return carry

        lax.fori_loop(0, n_xy, add, 0)

        def send(device, m):
            remote(to.at[m], landing.at[xy], snd.at[k], rcv.at[k], device).start()

        each_other(xy_g, at, send)
        landing[xy] = to[xy]

    swap_long.wait_recv()
    share_out(glong, clong, along, xylong, 8)
    swap_short.wait_recv()
    share_out(gshort, cshort, ashort, xyshort, 9)

    def back_rows(i, sums):
        first = 2 + i * 8
        grad_act = dot_nt(windows(x3g, first, 8), wt1[...]).reshape(8, WIDE, CH)[:, inner, :]
        normed = (ext[0, pl.ds(first, 8), inner, :] - group_mean[None]) * inv_spread[None]
        scaled = normed * gain[None]
        gate = sigmoid(scaled)
        grad = grad_act * (gate * (1.0 + scaled * (1.0 - gate)))
        gsc[pl.ds(i * 8, 8)] = grad
        straight = inv_spread[None] * (grad * gain[None]) + ext[1, pl.ds(first, 8), inner, :]
        spot = pl.ds(pl.multiple_of(i * 256, 256), 256)
        for k, part in enumerate(split_two(straight.reshape(256, CH)) + split_two(normed.reshape(256, CH))):
            glb[spot, k * CH : (k + 1) * CH] = part
        plain, cross = sums
        return (
            plain + jnp.sum(grad.reshape(32, 8, CH), axis=0),
            cross + jnp.sum((grad * normed).reshape(32, 8, CH), axis=0),
        )

    nothing = jnp.zeros((8, CH), F32)
    plain, cross = lax.fori_loop(0, 4, back_rows, (nothing, nothing))
    both = jnp.concatenate(
        [jnp.sum(plain, axis=0, keepdims=True), jnp.sum(cross, axis=0, keepdims=True)], axis=0
    )
    start_level(core_g, a2c, 10, both)

    which = lax.broadcasted_iota(jnp.int32, (24, CH), 0)
    lane = lax.broadcasted_iota(jnp.int32, (24, CH), 1)
    field_rows = dot(ft[...], glb[...])

    def by_field(k):
        part = field_rows[:, k * CH : (k + 1) * CH] + field_rows[:, (k + 1) * CH : (k + 2) * CH]
        on_land = jnp.sum(part[32:64], axis=0, keepdims=True)
        return jnp.where(which == CIN, on_land, part[0:24])

    alone = dot_nt(jnp.full((8, PIX), 1.0, BF16), ft[...])[0:1]
    msend[0] = by_field(0)
    msend[1] = jnp.where(which == CIN + 1, alone, by_field(2))
    m_swap = remote(msend.at[1 - core], mrecv, snd.at[13], rcv.at[13], core_dev)
    m_swap.start()

    out_rows(0)
    out_rows(1)
    write_out(feat, feat_hbm)

    start_level(xy_g, a2x, 11, add_up(end_level(a2c, 10)))

    goals = [(5 * t + 8 * core + 1) & (n_xy - 1) for t in range(3)]
    held = [goal == xy for goal in goals]
    holder = held[0] | held[1] | held[2]

    m_swap.wait_recv()
    mown[...] = msend[core] + mrecv[...]
    for t in range(3):
        strip = mown.at[8 * t : 8 * t + 8]

        @pl.when(jnp.logical_not(held[t]))
        def _():
            remote(strip, mxy.at[xy], snd.at[14], rcv.at[14], member_of(xy_g, at, goals[t])).start()

        @pl.when(held[t])
        def _():
            mxy[xy] = mown[8 * t : 8 * t + 8]

    long_rows = glong.shape[1] // n_xy
    long_tiles = long_rows // 8
    tiles = zsrc.shape[0] // 8
    spare = tiles - 1
    turn = (xy + 8 * core) & (n_z - 1)
    own = (z - turn) & (n_z // 2 - 1)
    twice = own == 0

    def send_tile(t, carry):
        for half in range(2):
            goal = (t + turn + half * n_z // 2) & (n_z - 1)
            slot = jnp.where(t == spare, 1, 0)

            @pl.when(goal != z)
            def _():
                remote(
                    zsrc.at[pl.ds(pl.multiple_of(t * 8, 8), 8)],
                    zb.at[slot, z],
                    snd.at[16],
                    rcv.at[jnp.where(t == spare, 26, 16)],
                    member_of(z_g, at, goal),
                ).start()

        return carry

    waiter(xylong.at[pl.ds(0, n_xy - 1)], 8).wait_recv()
    zsrc[0:long_rows] = add_up([xylong[i] for i in range(n_xy)])
    lax.fori_loop(0, long_tiles, send_tile, 0)
    waiter(xyshort.at[pl.ds(0, n_xy - 1)], 9).wait_recv()
    zsrc[long_rows:] = add_up([xyshort[i] for i in range(n_xy)])
    lax.fori_loop(long_tiles, tiles, send_tile, 0)

    start_level(z_g, a2z, 12, add_up(end_level(a2x, 11)))

    @pl.when(holder)
    def _():
        waiter(mxy.at[pl.ds(0, n_xy - 1)], 14).wait_recv()
        start_level(z_g, mz, 15, add_up([mxy[i] for i in range(n_xy)]))

    def whole_tile(slot, tile, k_in, k_out):
        spot = pl.ds(pl.multiple_of(tile * 8, 8), 8)
        zb[slot, z] = zsrc[spot, :]
        waiter(zb.at[slot, pl.ds(0, n_z - 1)], k_in).wait_recv()
        zres[spot, :] = add_up([zb[slot, i] for i in range(n_z)]) * report

        def send(k, carry):
            away = (k + 1) >> 1
            goal = z + jnp.where((k & 1) == 1, n_z // 4 - away, away - n_z // 4)
            device = member_of(z_g, at, (goal + n_z) & (n_z - 1))
            remote(zres.at[spot], zres.at[spot], snd.at[17], rcv.at[k_out], device).start()
            return carry

        lax.fori_loop(0, n_z // 2 - 1, send, 0)

    in_long = own < long_tiles

    @pl.when(in_long)
    def _():
        whole_tile(0, own, 16, 17)

    @pl.when(jnp.logical_not(in_long))
    def _():
        whole_tile(0, own, 16, 18)

    @pl.when(twice)
    def _():
        whole_tile(1, spare, 26, 18)

    totals = add_up(end_level(a2z, 12))
    ggain[...] = totals[1:2] * report
    write_out(ggain, ggain_hbm)
    plain_sum = group_sums(totals[0:1] * gain) * (1.0 / members)
    cross_sum = group_sums(totals[1:2] * gain) * (1.0 / members)

    def lifted_rows(i):
        first = 2 + i * 8
        normed = (ext[0, pl.ds(first, 8), inner, :] - group_mean[None]) * inv_spread[None]
        grad = gsc[pl.ds(i * 8, 8)] * gain[None] - plain_sum[None] - normed * cross_sum[None]
        grad = inv_spread[None] * grad + ext[1, pl.ds(first, 8), inner, :]
        glb[pl.ds(pl.multiple_of(i * 256, 256), 256), 0:CH] = grad.reshape(256, CH).astype(BF16)

    loop(4, lifted_rows)

    fine_hi, fine_lo = split_two(dot_nt(wext[0:32], glb[:, 0:CH]))
    stacked = jnp.concatenate(
        [fine_hi[:, 0:512], fine_hi[:, 512:], fine_lo[:, 0:512], fine_lo[:, 512:]], axis=0
    )
    lowered = dot_nt(stacked, up[...])
    lowered = lowered[0:64] + lowered[64:128]
    for s, (dr, dc) in enumerate(around):
        for m in range(2):
            ret_s[s, m] = weight[0, s, m] * lowered[0:24] + weight[1, s, m] * lowered[32:56]
        if s != 4:
            remote(ret_s.at[s], ret_r.at[8 - s], snd.at[19], rcv.at[19], near(dr, dc)).start()

    @pl.when(holder)
    def _():
        waiter(mz.at[pl.ds(0, n_z - 1)], 15).wait()

    for t in range(3):
        place = mall.at[core, 8 * t : 8 * t + 8]

        @pl.when(held[t])
        def _():
            mall[core, 8 * t : 8 * t + 8, :] = add_up([mz[i] for i in range(n_z)])

            def send(device, m):
                remote(place, place, snd.at[20], rcv.at[20], device).start()

            each_other(xy_g, at, send)

    def wait_tiles(count, some_mine, k):
        @pl.when(some_mine)
        def _():
            waiter(zres.at[pl.ds(0, (count - 1) * 8)], k).wait_recv()

        @pl.when(jnp.logical_not(some_mine))
        def _():
            waiter(zres.at[pl.ds(0, count * 8)], k).wait_recv()

    def send_shares(out, k):
        piece = out.at[core, xy]

        def send(device, m):
            remote(piece, piece, snd.at[k], rcv.at[k], device).start()

        each_other(xy_g, at, send)

    wait_tiles(long_tiles, in_long, 17)
    long_out[core, xy] = zres[0:long_rows].astype(BF16)
    send_shares(long_out, 21)
    wait_tiles(tiles - long_tiles, jnp.logical_not(in_long) | twice, 18)
    rest = zres[long_rows:]
    short_out[core, xy] = jnp.concatenate([rest, jnp.zeros((short_out.shape[2] - rest.shape[0], CH), F32)], axis=0).astype(BF16)
    send_shares(short_out, 22)

    waiter(ret_r.at[pl.ds(0, 8)], 19).wait()
    for m in range(2):
        total = ret_s[4, m]
        for s in range(9):
            if s != 4:
                total = total + ret_r[s, m]
        gcoarse[:, m, :] = total[0:CIN]
    write_out(gcoarse, gcoarse_hbm)

    @pl.when(holder)
    def _():
        waiter(mall.at[core, 0:16], 20).wait_recv()

    @pl.when(jnp.logical_not(holder))
    def _():
        waiter(mall.at[core], 20).wait_recv()

    m_back = remote(mall.at[core], mall.at[core], snd.at[23], rcv.at[23], core_dev)
    m_back.start()

    long_all = n_xy * long_rows
    short_rows = zsrc.shape[0] - long_rows

    def widen_long(half):
        grads[half, 0:long_all, :] = long_out[half].astype(F32).reshape(long_all, CH)
        piece = (half, pl.ds(0, long_all))
        write_out(grads.at[piece], grads_hbm.at[piece])

    def widen_short(half):
        part = short_out[half][:, 0:short_rows, :].astype(F32)
        grads[half, long_all:, :] = part.reshape(n_xy * short_rows, CH)
        piece = (half, pl.ds(long_all, n_xy * short_rows))
        write_out(grads.at[piece], grads_hbm.at[piece])

    waiter(long_out.at[core, pl.ds(0, n_xy - 1)], 21).wait_recv()
    back_long = remote(long_out.at[core], long_out.at[core], snd.at[24], rcv.at[24], core_dev)
    back_long.start()
    widen_long(core)

    m_back.wait()
    straight, crossed = mall[0], mall[1]
    fields = ((lane == which) & (which < CIN)) | ((which == CIN) & (lane >= 32) & (lane < 64))
    alone = jnp.sum(jnp.where(fields, crossed[CIN + 1 : CIN + 2], 0.0), axis=1, keepdims=True)
    lift_all = straight - (inv_spread * plain_sum) * alone - (inv_spread * cross_sum) * crossed
    lift_all = lift_all * report
    glift[...] = lift_all[0:CIN]
    gland[...] = lift_all[CIN : CIN + 1]
    write_out(glift, glift_hbm)
    write_out(gland, gland_hbm)

    waiter(short_out.at[core, pl.ds(0, n_xy - 1)], 22).wait_recv()
    back_short = remote(short_out.at[core], short_out.at[core], snd.at[25], rcv.at[25], core_dev)
    back_short.start()
    widen_short(core)

    waiter(cand.at[pl.ds(0, 8)], 0).wait_send()
    swap_long.wait_send()
    swap_short.wait_send()
    m_swap.wait_send()
    waiter(xylong.at[pl.ds(0, n_xy - 1)], 8).wait_send()
    waiter(xyshort.at[pl.ds(0, n_xy - 1)], 9).wait_send()
    waiter(long_out.at[core, pl.ds(0, n_xy - 1)], 21).wait_send()
    waiter(short_out.at[core, pl.ds(0, n_xy - 1)], 22).wait_send()

    @pl.when(holder)
    def _():
        waiter(mown.at[0:16], 14).wait_send()
        waiter(mxy.at[pl.ds(0, n_xy - 1)], 20).wait_send()

    @pl.when(jnp.logical_not(holder))
    def _():
        waiter(mown, 14).wait_send()

    once = n_z // 2 - 1
    waiter(zsrc, 16).wait_send()
    waiter(zb.at[0, pl.ds(0, once)], 17).wait_send()

    @pl.when(twice)
    def _():
        waiter(zsrc.at[pl.ds(0, (tiles - 2) * 8)], 16).wait_send()
        waiter(zb.at[0, pl.ds(0, once)], 17).wait_send()

    @pl.when(jnp.logical_not(twice))
    def _():
        waiter(zsrc.at[pl.ds(0, (tiles - 1) * 8)], 16).wait_send()

    back_long.wait()
    widen_long(1 - core)
    back_short.wait()
    widen_short(1 - core)
    for copy in written:
        copy.wait()


def finish(feat, gcoarse, grads, glift, gland, ggain, *rest):
    outs, held, dma = rest[:7], rest[7:14], rest[14]
    sources = (grads.at[1], grads.at[0], feat, gcoarse, glift, gland, ggain)
    ins = [pltpu.make_async_copy(a, b, dma.at[0, k]) for k, (a, b) in enumerate(zip(sources, held))]
    for copy in ins:
        copy.start()
    copies = [pltpu.make_async_copy(a, b, dma.at[1, k]) for k, (a, b) in enumerate(zip(held, outs))]
    for arrived, copy in zip(ins, copies):
        arrived.wait()
        copy.start()
    for copy in copies:
        copy.wait()


def shards(*args):
    (
        coarse_blocks,
        block_ids,
        quadrant,
        land_mask,
        lift_weight,
        land_vector,
        norm_gain,
        first_weight,
        second_weight,
        cotangent,
    ) = args
    n_row, n_col = lax.axis_size("row"), lax.axis_size("col")
    n_xy, n_z = n_row, n_col // 2

    def body(*refs):
        kernel(n_row, n_col, *refs)

    hbm = pl.BlockSpec(memory_space=pltpu.HBM)
    rows_long = 6 * CH // n_xy
    rows_short = 3 * CH // n_xy
    pad_short = -(-rows_short // 16) * 16
    results = [
        jax.ShapeDtypeStruct((TILE, TILE, CH), BF16),
        jax.ShapeDtypeStruct((CIN, 2, CH), F32),
        jax.ShapeDtypeStruct((2, HALF, CH), F32),
        jax.ShapeDtypeStruct((CIN, CH), F32),
        jax.ShapeDtypeStruct((1, CH), F32),
        jax.ShapeDtypeStruct((1, CH), F32),
    ]
    scratch = [
        pltpu.VMEM((CIN, 2, CH), BF16),
        pltpu.SMEM(block_ids.shape, jnp.int32),
        pltpu.SMEM(quadrant.shape, jnp.int32),
        pltpu.VMEM((TILE, TILE), jnp.int32),
        pltpu.VMEM((CIN, CH), BF16),
        pltpu.VMEM((1, CH), F32),
        pltpu.VMEM((1, CH), F32),
        pltpu.VMEM((3, 32, CH), F32),
        pltpu.VMEM((9, 2, 32, CH), BF16),
        pltpu.VMEM((CH, 512), BF16),
        pltpu.VMEM((CH, PIX), BF16),
        pltpu.VMEM((CH, CH), BF16),
        pltpu.VMEM((TAPS, CH, CH), BF16),
        pltpu.VMEM((TAPS, CH, CH), BF16),
        pltpu.VMEM((TILE, TILE, CH), BF16),
        pltpu.VMEM((CH, HALF), BF16),
        pltpu.VMEM((CH, HALF), BF16),
        pltpu.VMEM((2, ROWS, WIDE, CH), F32),
        pltpu.VMEM((2, 2, 2, TILE, CH), F32),
        pltpu.VMEM((2, 2, 2, TILE, CH), F32),
        pltpu.VMEM((2, 2, 2, 40, CH), F32),
        pltpu.VMEM((2, 2, 2, 40, CH), F32),
        pltpu.VMEM((2, ROWS, WIDE, 3 * CH), BF16),
        pltpu.VMEM((ROWS, WIDE, 3 * CH), BF16),
        pltpu.VMEM((ROWS, WIDE, 3 * CH), BF16),
        pltpu.VMEM((2, ROWS, WIDE, CH), BF16),
        pltpu.VMEM((ROWS, WIDE, CH), F32),
        pltpu.VMEM((TILE, TILE, CH), F32),
        pltpu.VMEM((PIX, 4 * CH), BF16),
        pltpu.VMEM((2, 2, CH), F32),
        pltpu.VMEM((n_xy, 2, CH), F32),
        pltpu.VMEM((n_z, 2, CH), F32),
        pltpu.VMEM((2, 2, CH), F32),
        pltpu.VMEM((n_xy, 2, CH), F32),
        pltpu.VMEM((n_z, 2, CH), F32),
        pltpu.VMEM((TILE, TILE, CH), BF16),
        pltpu.VMEM((CIN, 2, CH), F32),
        pltpu.VMEM((2, HALF, CH), F32),
        pltpu.VMEM((CIN, CH), F32),
        pltpu.VMEM((1, CH), F32),
        pltpu.VMEM((1, CH), F32),
        pltpu.VMEM((2, n_xy, rows_long, CH), BF16),
        pltpu.VMEM((2, n_xy, pad_short, CH), BF16),
        pltpu.VMEM((2, 24, CH), F32),
        pltpu.VMEM((24, CH), F32),
        pltpu.VMEM((n_xy, 8, CH), F32),
        pltpu.VMEM((24, CH), F32),
        pltpu.VMEM((n_z, 8, CH), F32),
        pltpu.VMEM((2, 24, CH), F32),
        pltpu.VMEM((2, 6 * CH, CH), F32),
        pltpu.VMEM((2, 3 * CH, CH), F32),
        pltpu.VMEM((6 * CH, CH), F32),
        pltpu.VMEM((3 * CH, CH), F32),
        pltpu.VMEM((n_xy, rows_long, CH), F32),
        pltpu.VMEM((n_xy, rows_short, CH), F32),
        pltpu.VMEM((n_xy, rows_long, CH), F32),
        pltpu.VMEM((n_xy, rows_short, CH), F32),
        pltpu.VMEM((rows_long + rows_short, CH), F32),
        pltpu.VMEM((2, n_z, 8, CH), F32),
        pltpu.VMEM((rows_long + rows_short, CH), F32),
        pltpu.VMEM((9, 2, 24, CH), F32),
        pltpu.VMEM((9, 2, 24, CH), F32),
        pltpu.SemaphoreType.DMA((19,)),
        pltpu.SemaphoreType.DMA((29,)),
        pltpu.SemaphoreType.DMA((29,)),
    ]
    parts = pl.pallas_call(
        body,
        out_shape=results,
        in_specs=[hbm] * 10,
        out_specs=[hbm] * 6,
        scratch_shapes=scratch,
        compiler_params=pltpu.CompilerParams(
            collective_id=0, has_side_effects=True, vmem_limit_bytes=60 << 20
        ),
        name="block",
    )(
        jnp.transpose(coarse_blocks[0, 0], (1, 0, 2)),
        block_ids,
        quadrant,
        land_mask,
        lift_weight,
        land_vector.reshape(1, CH),
        norm_gain.reshape(1, CH),
        first_weight,
        second_weight,
        cotangent,
    )
    wide = jax.ShapeDtypeStruct((HALF, CH), F32)
    outputs = [wide, wide, results[0], results[1]] + results[3:]
    grad_first, grad_second, features, grad_coarse, grad_lift, grad_land, grad_gain = pl.pallas_call(
        finish,
        out_shape=outputs,
        in_specs=[hbm] * 6,
        out_specs=[hbm] * 7,
        scratch_shapes=[pltpu.VMEM(out.shape, out.dtype) for out in outputs]
        + [pltpu.SemaphoreType.DMA((2, 7))],
        compiler_params=pltpu.CompilerParams(vmem_limit_bytes=60 << 20),
        name="finish",
    )(*parts)
    return (
        features,
        jnp.transpose(grad_coarse, (1, 0, 2))[None, None],
        grad_first.reshape(TAPS, CH, CH),
        grad_second.reshape(TAPS, CH, CH),
        grad_lift,
        grad_land.reshape(CH),
        grad_gain.reshape(CH),
    )


def solution(mesh):
    in_specs = (
        P("row", "col", None, None, None),
        P("row", "col", None),
        P("row", "col", None),
        P("row", "col"),
        P(),
        P(),
        P(),
        P(),
        P(),
        P("row", "col", None),
    )
    out_specs = (P("row", "col", None), P("row", "col", None, None, None), P(), P(), P(), P(), P())
    return jax.shard_map(shards, mesh=mesh, in_specs=in_specs, out_specs=out_specs, check_vma=False)
```

```python
import math

import jax
import jax.numpy as jnp
from jax import lax
from jax.experimental import pallas as pl
from jax.experimental.pallas import tpu as pltpu
from jax.sharding import PartitionSpec as P

GROUPS = 32
EPSILON = 1e-05
MESH = pl.DeviceIdType.MESH
F32 = jnp.float32
BF16 = jnp.bfloat16

TILE = 32
ROWS = TILE + 4
WIDE = 48
LEFT = 8
CH = 128
CIN = 20
PIX = TILE * TILE
TAPS = 9
FAR_FIRST = tuple(
    sum(step << (4 * k) for k, step in enumerate(half))
    for half in ((5, 3, 7, 12, 13, 1, 4, 2), (10, 11, 14, 15, 6, 8, 9))
)
HALF = TAPS * CH


def log2(n):
    return n.bit_length() - 1


def size_of(group):
    n = 1
    for _, _, count in group:
        n *= count
    return n


def place_in(group, at):
    m = 0
    for axis, stride, count in group:
        m = (m << log2(count)) | ((at[axis] >> log2(stride)) & (count - 1))
    return m


def member_of(group, at, m):
    new = dict(at)
    for axis, stride, count in reversed(group):
        digit = m & (count - 1)
        m = m >> log2(count)
        new[axis] = (new[axis] & ~((count - 1) * stride)) | (digit << log2(stride))
    return (new["row"], new["col"])


def each_other(group, at, act):
    n = size_of(group)
    me = place_in(group, at)
    flat = len(group) == 2 and n == 16

    def body(k, carry):
        if flat:
            step = jnp.where(k < 8, FAR_FIRST[0], FAR_FIRST[1])
            m = me ^ ((step >> ((k & 7) * 4)) & 15)
        else:
            away = (k + 1) >> 1
            m = (me + n // 2 + jnp.where((k & 1) == 1, away, -away) + n) & (n - 1)
        act(member_of(group, at, m), m)
        return carry

    lax.fori_loop(0, n - 1, body, 0)


def remote(src, dst, send, recv, device):
    return pltpu.make_async_remote_copy(
        src_ref=src,
        dst_ref=dst,
        send_sem=send,
        recv_sem=recv,
        device_id=device,
        device_id_type=MESH,
    )


def dot(a, b):
    return jnp.dot(a, b, preferred_element_type=F32)


def dot_tn(a, b):
    return lax.dot_general(a, b, (((0,), (0,)), ((), ())), preferred_element_type=F32)


def dot_nt(a, b):
    return lax.dot_general(a, b, (((1,), (1,)), ((), ())), preferred_element_type=F32)


def split_two(x):
    hi = x.astype(BF16)
    return hi, (x - hi.astype(F32)).astype(BF16)


def split_three(x):
    hi = x.astype(BF16)
    rest = x - hi.astype(F32)
    mid = rest.astype(BF16)
    return hi, mid, (rest - mid.astype(F32)).astype(BF16)


def sigmoid(v):
    return 1.0 / (1.0 + jnp.exp(-v))


def group_sums(v):
    lane = lax.broadcasted_iota(jnp.int32, v.shape, 1)
    one = v + jnp.where((lane & 1) == 1, pltpu.roll(v, 1, 1), pltpu.roll(v, CH - 1, 1))
    return one + jnp.where((lane & 2) == 2, pltpu.roll(one, 2, 1), pltpu.roll(one, CH - 2, 1))


def kernel(
    n_row,
    n_col,
    coarse_hbm,
    ids_hbm,
    quad_hbm,
    land_hbm,
    lift_hbm,
    land_v_hbm,
    gain_hbm,
    w1_hbm,
    w2_hbm,
    cot_hbm,
    feat,
    gcoarse,
    grads,
    glift,
    gland,
    ggain,
    coarse,
    ids,
    quad,
    land,
    lift_w,
    land_v,
    gain_ref,
    padf,
    cand,
    up,
    ft,
    wext,
    wpair,
    upt,
    w1,
    w2,
    cotv,
    wt1,
    wt2,
    ext,
    rh_s,
    rh_r,
    ch_s,
    ch_r,
    x3ab,
    x3c,
    x3g,
    gi,
    t2,
    gsc,
    glb,
    a1c,
    a1x,
    a1z,
    a2c,
    a2x,
    a2z,
    long_out,
    short_out,
    msend,
    mrecv,
    mxy,
    mown,
    mz,
    mall,
    glong,
    gshort,
    clong,
    cshort,
    along,
    ashort,
    xylong,
    xyshort,
    zsrc,
    zb,
    zres,
    ret_s,
    ret_r,
    dma,
    snd,
    rcv,
    answers,
):
    row = lax.axis_index("row")
    col = lax.axis_index("col")
    at = {"row": row, "col": col}
    core_g = (("row", 1, 2),)
    xy_g = (("row", 2, n_row // 2), ("col", n_col // 2, 2))
    z_g = (("col", 1, n_col // 2),)
    n_xy = size_of(xy_g)
    n_z = size_of(z_g)
    members = float(n_row * TILE * n_col * TILE * (CH // GROUPS))
    report = 1.0 / math.sqrt(n_row * TILE * n_col * TILE)
    pixels_all = float(n_row * TILE * n_col * TILE)

    core = place_in(core_g, at)
    xy = place_in(xy_g, at)
    z = place_in(z_g, at)
    core_dev = member_of(core_g, at, 1 - core)
    x3b, x3a = x3ab.at[0], x3ab.at[1]
    gic, gig = gi.at[0], gi.at[1]

    def near(dr, dc):
        return ((row + dr + n_row) & (n_row - 1), (col + dc + n_col) & (n_col - 1))

    around = [(dr, dc) for dr in (-1, 0, 1) for dc in (-1, 0, 1)]

    def waiter(ref, k):
        return remote(ref, ref, snd.at[k], rcv.at[k], core_dev)

    barrier = pltpu.get_barrier_semaphore()

    def greet(device, m):
        pl.semaphore_signal(barrier, inc=1, device_id=device, device_id_type=MESH)

    for dr, dc in around:
        if (dr, dc) != (0, 0):
            greet(near(dr, dc), 0)
    for group in (core_g, xy_g):
        each_other(group, at, greet)

    def along_z(away):
        return member_of(z_g, at, (z + away + n_z) & (n_z - 1))

    quarter = n_z // 4
    for away in range(quarter, 0, -1):
        greet(along_z(away), 0)
        greet(along_z(-away), 0)

    pairs = [
        (coarse_hbm, coarse),
        (lift_hbm, lift_w),
        (ids_hbm, ids),
        (quad_hbm, quad),
        (land_hbm, land),
        (land_v_hbm, land_v),
        (gain_hbm, gain_ref),
        (cot_hbm, cotv),
        (w2_hbm, w2),
        (w1_hbm, w1),
    ]
    loads = [pltpu.make_async_copy(a, b, dma.at[k]) for k, (a, b) in enumerate(pairs)]
    for load in loads:
        load.start()

    padf[...] = jnp.zeros_like(padf)
    for load in loads[:2]:
        load.wait()
    for m in range(2):
        padf[m, 0:CIN, :] = coarse[:, m, :].astype(F32)
    padf[2, 0:CIN, :] = lift_w[...].astype(F32)
    cand[4] = padf[0:2].astype(BF16)

    pl.semaphore_wait(barrier, 8 + 1 + n_xy - 1 + 2 * quarter)

    for s, (dr, dc) in enumerate(around):
        if s != 4:
            remote(cand.at[4], cand.at[8 - s], snd.at[0], rcv.at[0], near(dr, dc)).start()

    for away in (quarter, -quarter):
        pl.semaphore_signal(answers, inc=1, device_id=along_z(away), device_id_type=MESH)

    for load in loads[2:]:
        load.wait()
    codes = []
    for k in range(ids.shape[2]):
        block = ids[0, 0, k]
        owner = block >> 1
        slot_row = (owner >> log2(n_col)) - row + 1
        slot_col = (owner & (n_col - 1)) - col + 1
        codes.append(((quad[0, 0, k] * 9) + slot_row * 3 + slot_col) * 2 + (block & 1))

    def picks(q, s, m):
        want = (q * 9 + s) * 2 + m
        total = jnp.float32(0.0)
        for code in codes:
            total = total + jnp.where(code == want, jnp.float32(1.0), jnp.float32(0.0))
        return total

    weight = {(q, s, m): picks(q, s, m) for q in range(2) for s in range(9) for m in range(2)}

    fine = lax.broadcasted_iota(jnp.int32, (CH, 512), 1)
    cell = lax.broadcasted_iota(jnp.int32, (CH, 512), 0)

    def hat(fine_at, cell_at, count):
        where = jnp.clip((fine_at.astype(F32) + 0.5) * 0.5 - 0.5, 0.0, count - 1.0)
        return jnp.maximum(1.0 - jnp.abs(where - cell_at.astype(F32)), 0.0)

    up[...] = (hat(fine >> 5, cell >> 4, 8) * hat(fine & 31, cell & 15, 16)).astype(BF16)
    fine = lax.broadcasted_iota(jnp.int32, (512, CH), 0)
    cell = lax.broadcasted_iota(jnp.int32, (512, CH), 1)
    turned = (hat(fine >> 5, cell >> 4, 8) * hat(fine & 31, cell & 15, 16)).astype(BF16)
    for k in range(3):
        upt[:, k * CH : (k + 1) * CH] = turned

    pix = lax.broadcasted_iota(jnp.int32, (TILE, PIX), 1)
    line = lax.broadcasted_iota(jnp.int32, (TILE, PIX), 0)
    spread = jnp.where((pix & 31) == line, 1.0, 0.0).astype(BF16)
    lines = dot(land[...].astype(F32).astype(BF16), spread)
    lines = jnp.where((pix >> 5) == line, lines, 0.0).astype(BF16)
    wext[0:32] = padf[2].astype(BF16)
    wpair[...] = jnp.zeros_like(wpair)
    wpair[0, 0:32] = wext[0:32]
    wpair[1, 32:64] = wext[0:32]
    for k, part in enumerate(split_three(jnp.broadcast_to(land_v[...], (32, CH)))):
        ft[32 * (k + 1) : 32 * (k + 2), :] = lines
        wext[32 * (k + 1) : 32 * (k + 2), :] = part
    on_land = dot_tn(ft[32:], wext[32:])
    ext[0, 2 : 2 + TILE, LEFT : LEFT + TILE, :] = on_land.reshape(TILE, TILE, CH)

    for lo, hi in ((0, LEFT), (LEFT + TILE, WIDE)):
        ext[:, :, lo:hi, :] = jnp.zeros((2, ROWS, 8, CH), F32)
    for edge in (0, ROWS - 1):
        gi[:, edge] = jnp.zeros((2, WIDE, CH), BF16)

    for k in range(TAPS):
        wt1[:, k * CH : (k + 1) * CH] = w1[8 - k]
        wt2[:, k * CH : (k + 1) * CH] = w2[8 - k]
    ext[1, 2 : 2 + TILE, LEFT : LEFT + TILE, :] = cotv[...].astype(F32)

    def pack_rows(a):
        rh_s[a, 0] = ext[a, 2:4, LEFT : LEFT + TILE, :]
        rh_s[a, 1] = ext[a, TILE : TILE + 2, LEFT : LEFT + TILE, :]

    def send_rows(a, k):
        for side, step in ((0, -1), (1, 1)):
            remote(rh_s.at[a, side], rh_r.at[a, side], snd.at[k], rcv.at[k], near(step, 0)).start()

    def rows_to_columns(a, k_rows, k_cols):
        waiter(rh_r.at[a], k_rows).wait()
        ext[a, 2 + TILE : 4 + TILE, LEFT : LEFT + TILE, :] = rh_r[a, 0]
        ext[a, 0:2, LEFT : LEFT + TILE, :] = rh_r[a, 1]
        for k in range(2):
            ch_s[a, 0, k, 0:ROWS, :] = ext[a, :, LEFT + k, :]
            ch_s[a, 1, k, 0:ROWS, :] = ext[a, :, LEFT + TILE - 2 + k, :]
        for side, step in ((0, -1), (1, 1)):
            remote(ch_s.at[a, side], ch_r.at[a, side], snd.at[k_cols], rcv.at[k_cols], near(0, step)).start()

    def put_columns(a, k_cols):
        waiter(ch_r.at[a], k_cols).wait()
        for k in range(2):
            ext[a, :, LEFT + TILE + k, :] = ch_r[a, 0, k, 0:ROWS, :]
            ext[a, :, LEFT - 2 + k, :] = ch_r[a, 1, k, 0:ROWS, :]

    pack_rows(1)
    send_rows(1, 27)

    waiter(cand.at[pl.ds(0, 8)], 0).wait_recv()
    sums = []
    for q in range(2):
        total = jnp.zeros((32, CH), F32)
        for s in range(9):
            for m in range(2):
                total = total + weight[q, s, m] * cand[s, m].astype(F32)
        sums.append(total)
    parts = split_three(jnp.concatenate(sums, axis=0))
    raised = dot_nt(upt[...], jnp.concatenate(parts, axis=1)).astype(BF16)
    lifted = jnp.concatenate(
        [
            dot(raised, wpair[q]) + ext[0, 2 + 16 * q : 18 + 16 * q, LEFT : LEFT + TILE, :].reshape(512, CH)
            for q in range(2)
        ],
        axis=0,
    )
    ext[0, 2 : 2 + TILE, LEFT : LEFT + TILE, :] = lifted.reshape(TILE, TILE, CH)
    mean_here = jnp.sum(lifted, axis=0, keepdims=True) * (1.0 / PIX)
    apart = lifted - mean_here
    square_here = jnp.sum(apart * apart, axis=0, keepdims=True)

    def start_level(group, buf, k, value):
        me = place_in(group, at)
        buf[me] = value

        def send(device, m):
            remote(buf.at[me], buf.at[me], snd.at[k], rcv.at[k], device).start()

        each_other(group, at, send)

    def end_level(buf, k):
        waiter(buf.at[pl.ds(0, buf.shape[0] - 1)], k).wait()
        return [buf[i] for i in range(buf.shape[0])]

    def add_up(values):
        while len(values) > 1:
            values = [a + b for a, b in zip(values[::2], values[1::2])]
        return values[0]

    def merge(values, count):
        mean = add_up([v[0:1] for v in values]) * (1.0 / len(values))
        square = add_up([v[1:2] for v in values])
        off = add_up([(v[0:1] - mean) * (v[0:1] - mean) for v in values])
        return jnp.concatenate([mean, square + count * off], axis=0)

    start_level(core_g, a1c, 1, jnp.concatenate([mean_here, square_here], axis=0))

    pack_rows(0)
    rows_to_columns(1, 27, 28)
    by_field = dot(jnp.concatenate(parts, axis=0), up[...])
    by_field = by_field[0:64] + by_field[64:128] + by_field[128:192]
    ft[0:32, 0:512] = by_field[0:32].astype(BF16)
    ft[0:32, 512:1024] = by_field[32:64].astype(BF16)

    moments = merge(end_level(a1c, 1), float(PIX))
    start_level(xy_g, a1x, 2, moments)
    send_rows(0, 4)
    rows_to_columns(0, 4, 5)

    moments = merge(end_level(a1x, 2), float(2 * PIX))
    pl.semaphore_wait(answers, 2)
    start_level(z_g, a1z, 3, moments)
    put_columns(1, 28)

    row_lo = jnp.where(row == 0, 2, 0)
    row_hi = jnp.where(row == n_row - 1, 2 + TILE, ROWS)
    col_lo = jnp.where(col == 0, LEFT, 0)
    col_hi = jnp.where(col == n_col - 1, LEFT + TILE, WIDE)

    def masks(first, count):
        r = lax.broadcasted_iota(jnp.int32, (count, WIDE, CH), 0) + first
        c = lax.broadcasted_iota(jnp.int32, (count, WIDE, CH), 1)
        in_grid = (r >= row_lo) & (r < row_hi) & (c >= col_lo) & (c < col_hi)
        in_tile = (r >= 2) & (r < 2 + TILE) & (c >= LEFT) & (c < LEFT + TILE)
        shape = (count * WIDE, CH)
        return in_grid.reshape(shape), in_tile.reshape(shape)

    def put_taps(x3, first, count, flat):
        length = count * WIDE
        x3[pl.ds(first, count), :, 0:CH] = pltpu.roll(flat, 1, 0).astype(BF16).reshape(count, WIDE, CH)
        x3[pl.ds(first, count), :, CH : 2 * CH] = flat.astype(BF16).reshape(count, WIDE, CH)
        x3[pl.ds(first, count), :, 2 * CH :] = (
            pltpu.roll(flat, length - 1, 0).astype(BF16).reshape(count, WIDE, CH)
        )

    def windows(x3, first, count):
        return jnp.concatenate(
            [x3[pl.ds(first - 1 + u, count)].reshape(count * WIDE, 3 * CH) for u in range(3)],
            axis=1,
        )

    def loop(trips, body):
        def step(i, carry):
            body(i)
            return carry

        lax.fori_loop(0, trips, step, 0)

    def cot_rows(i):
        first = i * 4
        in_grid, in_tile = masks(first, 4)
        flat = ext[1, pl.ds(first, 4)].reshape(4 * WIDE, CH)
        put_taps(x3c, first, 4, jnp.where(in_grid, flat, 0.0))
        gic[pl.ds(first, 4)] = jnp.where(in_tile, flat, 0.0).astype(BF16).reshape(4, WIDE, CH)

    loop(9, cot_rows)

    def cot_conv(i):
        first = 1 + i * 17
        t2[pl.ds(first, 17)] = dot_nt(windows(x3c, first, 17), wt2[...]).reshape(17, WIDE, CH)

    loop(2, cot_conv)
    put_columns(0, 5)

    moments = merge(end_level(a1z, 3), float(2 * n_xy * PIX))
    mean_ch = moments[0:1]
    group_mean = group_sums(mean_ch) * (GROUPS / CH)
    off = mean_ch - group_mean
    variance = group_sums(moments[1:2] + pixels_all * off * off) / members
    inv_spread = lax.rsqrt(variance + EPSILON)
    gain = gain_ref[...]

    def act_rows(i):
        first = i * 4
        in_grid, _ = masks(first, 4)
        flat = ext[0, pl.ds(first, 4)].reshape(4 * WIDE, CH)
        scaled = (flat - group_mean) * inv_spread * gain
        act = scaled * sigmoid(scaled)
        put_taps(x3a, first, 4, jnp.where(in_grid, act, 0.0))

    loop(9, act_rows)

    def hidden_rows(i):
        first = 1 + i * 17
        in_grid, in_tile = masks(first, 17)
        hidden = dot(windows(x3a, first, 17), w1[...].reshape(HALF, CH))
        gate = sigmoid(hidden)
        act = jnp.where(in_grid, hidden * gate, 0.0)
        slope = gate * (1.0 + hidden * (1.0 - gate))
        grad = jnp.where(in_grid, t2[pl.ds(first, 17)].reshape(17 * WIDE, CH) * slope, 0.0)
        put_taps(x3b, first, 17, act)
        put_taps(x3g, first, 17, grad)
        gig[pl.ds(first, 17)] = jnp.where(in_tile, grad, 0.0).astype(BF16).reshape(17, WIDE, CH)

    loop(2, hidden_rows)

    def tap_grads(half):
        length = (ROWS - 2) * WIDE
        grad = jnp.concatenate(
            [gi[half, 2 - u : 2 - u + ROWS - 2].reshape(length, CH) for u in range(3)], axis=1
        )
        out = dot_tn(x3ab[half, 1 : ROWS - 1].reshape(length, 3 * CH), grad)
        for u in range(3):
            for v in range(3):
                to, first = (glong, 3 * u + v) if u < 2 else (gshort, v)
                to[half, first * CH : (first + 1) * CH, :] = out[
                    v * CH : (v + 1) * CH, u * CH : (u + 1) * CH
                ]

    tap_grads(1 - core)
    swap_long = remote(glong.at[1 - core], clong, snd.at[6], rcv.at[6], core_dev)
    swap_long.start()
    swap_short = remote(gshort.at[1 - core], cshort, snd.at[7], rcv.at[7], core_dev)
    swap_short.start()
    tap_grads(core)

    inner = slice(LEFT, LEFT + TILE)

    def out_rows(i):
        first = 2 + i * 16
        out = dot(windows(x3b, first, 16), w2[...].reshape(HALF, CH)).reshape(16, WIDE, CH)
        feat[pl.ds(i * 16, 16)] = (ext[0, pl.ds(first, 16), inner, :] + out[:, inner, :]).astype(BF16)

    def share_out(mine, theirs, to, landing, k):
        def add(m, carry):
            rows = pl.ds(pl.multiple_of(m * mine.shape[1] // n_xy, 8), mine.shape[1] // n_xy)
            total = mine[core, rows, :] + theirs[rows, :]
            to[m] = total
            return carry

        lax.fori_loop(0, n_xy, add, 0)

        def send(device, m):
            remote(to.at[m], landing.at[xy], snd.at[k], rcv.at[k], device).start()

        each_other(xy_g, at, send)
        landing[xy] = to[xy]

    swap_long.wait_recv()
    share_out(glong, clong, along, xylong, 8)
    swap_short.wait_recv()
    share_out(gshort, cshort, ashort, xyshort, 9)

    def back_rows(i, sums):
        first = 2 + i * 8
        grad_act = dot_nt(windows(x3g, first, 8), wt1[...]).reshape(8, WIDE, CH)[:, inner, :]
        normed = (ext[0, pl.ds(first, 8), inner, :] - group_mean[None]) * inv_spread[None]
        scaled = normed * gain[None]
        gate = sigmoid(scaled)
        grad = grad_act * (gate * (1.0 + scaled * (1.0 - gate)))
        gsc[pl.ds(i * 8, 8)] = grad
        straight = inv_spread[None] * (grad * gain[None]) + ext[1, pl.ds(first, 8), inner, :]
        spot = pl.ds(pl.multiple_of(i * 256, 256), 256)
        for k, part in enumerate(split_two(straight.reshape(256, CH)) + split_two(normed.reshape(256, CH))):
            glb[spot, k * CH : (k + 1) * CH] = part
        plain, cross = sums
        return (
            plain + jnp.sum(grad.reshape(32, 8, CH), axis=0),
            cross + jnp.sum((grad * normed).reshape(32, 8, CH), axis=0),
        )

    nothing = jnp.zeros((8, CH), F32)
    plain, cross = lax.fori_loop(0, 4, back_rows, (nothing, nothing))
    both = jnp.concatenate(
        [jnp.sum(plain, axis=0, keepdims=True), jnp.sum(cross, axis=0, keepdims=True)], axis=0
    )
    start_level(core_g, a2c, 10, both)

    which = lax.broadcasted_iota(jnp.int32, (24, CH), 0)
    lane = lax.broadcasted_iota(jnp.int32, (24, CH), 1)
    field_rows = dot(ft[...], glb[...])

    def field_sums(k):
        part = field_rows[:, k * CH : (k + 1) * CH] + field_rows[:, (k + 1) * CH : (k + 2) * CH]
        on_land = jnp.sum(part[32:64], axis=0, keepdims=True)
        return jnp.where(which == CIN, on_land, part[0:24])

    alone = dot_nt(jnp.full((8, PIX), 1.0, BF16), ft[...])[0:1]
    msend[0] = field_sums(0)
    msend[1] = jnp.where(which == CIN + 1, alone, field_sums(2))
    m_swap = remote(msend.at[1 - core], mrecv, snd.at[13], rcv.at[13], core_dev)
    m_swap.start()

    out_rows(0)
    out_rows(1)

    start_level(xy_g, a2x, 11, add_up(end_level(a2c, 10)))

    goals = [(5 * t + 8 * core + 1) & (n_xy - 1) for t in range(3)]
    held = [goal == xy for goal in goals]
    holder = held[0] | held[1] | held[2]

    m_swap.wait_recv()
    mown[...] = msend[core] + mrecv[...]
    for t in range(3):
        strip = mown.at[8 * t : 8 * t + 8]

        @pl.when(jnp.logical_not(held[t]))
        def _():
            remote(strip, mxy.at[xy], snd.at[14], rcv.at[14], member_of(xy_g, at, goals[t])).start()

        @pl.when(held[t])
        def _():
            mxy[xy] = mown[8 * t : 8 * t + 8]

    long_rows = glong.shape[1] // n_xy
    long_tiles = long_rows // 8
    tiles = zsrc.shape[0] // 8
    spare = tiles - 1
    turn = (xy + 8 * core) & (n_z - 1)
    own = (z - turn) & (n_z // 2 - 1)
    twice = own == 0

    def send_tile(t, carry):
        for half in range(2):
            goal = (t + turn + half * n_z // 2) & (n_z - 1)
            slot = jnp.where(t == spare, 1, 0)

            @pl.when(goal != z)
            def _():
                remote(
                    zsrc.at[pl.ds(pl.multiple_of(t * 8, 8), 8)],
                    zb.at[slot, z],
                    snd.at[16],
                    rcv.at[jnp.where(t == spare, 26, 16)],
                    member_of(z_g, at, goal),
                ).start()

        return carry

    waiter(xylong.at[pl.ds(0, n_xy - 1)], 8).wait_recv()
    zsrc[0:long_rows] = add_up([xylong[i] for i in range(n_xy)])
    lax.fori_loop(0, long_tiles, send_tile, 0)
    waiter(xyshort.at[pl.ds(0, n_xy - 1)], 9).wait_recv()
    zsrc[long_rows:] = add_up([xyshort[i] for i in range(n_xy)])
    lax.fori_loop(long_tiles, tiles, send_tile, 0)

    start_level(z_g, a2z, 12, add_up(end_level(a2x, 11)))

    @pl.when(holder)
    def _():
        waiter(mxy.at[pl.ds(0, n_xy - 1)], 14).wait_recv()
        start_level(z_g, mz, 15, add_up([mxy[i] for i in range(n_xy)]))

    def whole_tile(slot, tile, k_in, k_out):
        spot = pl.ds(pl.multiple_of(tile * 8, 8), 8)
        zb[slot, z] = zsrc[spot, :]
        waiter(zb.at[slot, pl.ds(0, n_z - 1)], k_in).wait_recv()
        zres[spot, :] = add_up([zb[slot, i] for i in range(n_z)]) * report

        def send(k, carry):
            away = (k + 1) >> 1
            goal = z + jnp.where((k & 1) == 1, n_z // 4 - away, away - n_z // 4)
            device = member_of(z_g, at, (goal + n_z) & (n_z - 1))
            remote(zres.at[spot], zres.at[spot], snd.at[17], rcv.at[k_out], device).start()
            return carry

        lax.fori_loop(0, n_z // 2 - 1, send, 0)

    in_long = own < long_tiles

    @pl.when(in_long)
    def _():
        whole_tile(0, own, 16, 17)

    @pl.when(jnp.logical_not(in_long))
    def _():
        whole_tile(0, own, 16, 18)

    @pl.when(twice)
    def _():
        whole_tile(1, spare, 26, 18)

    totals = add_up(end_level(a2z, 12))
    ggain[...] = totals[1:2] * report
    plain_sum = group_sums(totals[0:1] * gain) * (1.0 / members)
    cross_sum = group_sums(totals[1:2] * gain) * (1.0 / members)

    def lifted_rows(i):
        first = 2 + i * 8
        normed = (ext[0, pl.ds(first, 8), inner, :] - group_mean[None]) * inv_spread[None]
        grad = gsc[pl.ds(i * 8, 8)] * gain[None] - plain_sum[None] - normed * cross_sum[None]
        grad = inv_spread[None] * grad + ext[1, pl.ds(first, 8), inner, :]
        glb[pl.ds(pl.multiple_of(i * 256, 256), 256), 0:CH] = grad.reshape(256, CH).astype(BF16)

    loop(4, lifted_rows)

    fine_hi, fine_lo = split_two(dot_nt(wext[0:32], glb[:, 0:CH]))
    stacked = jnp.concatenate(
        [fine_hi[:, 0:512], fine_hi[:, 512:], fine_lo[:, 0:512], fine_lo[:, 512:]], axis=0
    )
    lowered = dot_nt(stacked, up[...])
    lowered = lowered[0:64] + lowered[64:128]
    for s, (dr, dc) in enumerate(around):
        for m in range(2):
            ret_s[s, m] = weight[0, s, m] * lowered[0:24] + weight[1, s, m] * lowered[32:56]
        if s != 4:
            remote(ret_s.at[s], ret_r.at[8 - s], snd.at[19], rcv.at[19], near(dr, dc)).start()

    @pl.when(holder)
    def _():
        waiter(mz.at[pl.ds(0, n_z - 1)], 15).wait()

    for t in range(3):
        place = mall.at[core, 8 * t : 8 * t + 8]

        @pl.when(held[t])
        def _():
            mall[core, 8 * t : 8 * t + 8, :] = add_up([mz[i] for i in range(n_z)])

            def send(device, m):
                remote(place, place, snd.at[20], rcv.at[20], device).start()

            each_other(xy_g, at, send)

    def wait_tiles(count, some_mine, k):
        @pl.when(some_mine)
        def _():
            waiter(zres.at[pl.ds(0, (count - 1) * 8)], k).wait_recv()

        @pl.when(jnp.logical_not(some_mine))
        def _():
            waiter(zres.at[pl.ds(0, count * 8)], k).wait_recv()

    def send_shares(out, k):
        piece = out.at[core, xy]

        def send(device, m):
            remote(piece, piece, snd.at[k], rcv.at[k], device).start()

        each_other(xy_g, at, send)

    wait_tiles(long_tiles, in_long, 17)
    long_out[core, xy] = zres[0:long_rows].astype(BF16)
    send_shares(long_out, 21)
    wait_tiles(tiles - long_tiles, jnp.logical_not(in_long) | twice, 18)
    rest = zres[long_rows:]
    short_out[core, xy] = jnp.concatenate([rest, jnp.zeros((short_out.shape[2] - rest.shape[0], CH), F32)], axis=0).astype(BF16)
    send_shares(short_out, 22)

    waiter(ret_r.at[pl.ds(0, 8)], 19).wait()
    for m in range(2):
        total = ret_s[4, m]
        for s in range(9):
            if s != 4:
                total = total + ret_r[s, m]
        gcoarse[:, m, :] = total[0:CIN]

    @pl.when(holder)
    def _():
        waiter(mall.at[core, 0:16], 20).wait_recv()

    @pl.when(jnp.logical_not(holder))
    def _():
        waiter(mall.at[core], 20).wait_recv()

    m_back = remote(mall.at[core], mall.at[core], snd.at[23], rcv.at[23], core_dev)
    m_back.start()

    long_all = n_xy * long_rows
    short_rows = zsrc.shape[0] - long_rows

    def widen_long(half):
        grads[half, 0:long_all, :] = long_out[half].astype(F32).reshape(long_all, CH)

    def widen_short(half):
        part = short_out[half][:, 0:short_rows, :].astype(F32)
        grads[half, long_all:, :] = part.reshape(n_xy * short_rows, CH)

    waiter(long_out.at[core, pl.ds(0, n_xy - 1)], 21).wait_recv()
    back_long = remote(long_out.at[core], long_out.at[core], snd.at[24], rcv.at[24], core_dev)
    back_long.start()
    widen_long(core)

    m_back.wait()
    straight, crossed = mall[0], mall[1]
    fields = ((lane == which) & (which < CIN)) | ((which == CIN) & (lane >= 32) & (lane < 64))
    alone = jnp.sum(jnp.where(fields, crossed[CIN + 1 : CIN + 2], 0.0), axis=1, keepdims=True)
    lift_all = straight - (inv_spread * plain_sum) * alone - (inv_spread * cross_sum) * crossed
    lift_all = lift_all * report
    glift[...] = lift_all[0:CIN]
    gland[...] = lift_all[CIN : CIN + 1]

    waiter(short_out.at[core, pl.ds(0, n_xy - 1)], 22).wait_recv()
    back_short = remote(short_out.at[core], short_out.at[core], snd.at[25], rcv.at[25], core_dev)
    back_short.start()
    widen_short(core)

    waiter(cand.at[pl.ds(0, 8)], 0).wait_send()
    swap_long.wait_send()
    swap_short.wait_send()
    m_swap.wait_send()
    waiter(xylong.at[pl.ds(0, n_xy - 1)], 8).wait_send()
    waiter(xyshort.at[pl.ds(0, n_xy - 1)], 9).wait_send()
    waiter(long_out.at[core, pl.ds(0, n_xy - 1)], 21).wait_send()
    waiter(short_out.at[core, pl.ds(0, n_xy - 1)], 22).wait_send()

    @pl.when(holder)
    def _():
        waiter(mown.at[0:16], 14).wait_send()
        waiter(mxy.at[pl.ds(0, n_xy - 1)], 20).wait_send()

    @pl.when(jnp.logical_not(holder))
    def _():
        waiter(mown, 14).wait_send()

    once = n_z // 2 - 1
    waiter(zsrc, 16).wait_send()
    waiter(zb.at[0, pl.ds(0, once)], 17).wait_send()

    @pl.when(twice)
    def _():
        waiter(zsrc.at[pl.ds(0, (tiles - 2) * 8)], 16).wait_send()
        waiter(zb.at[0, pl.ds(0, once)], 17).wait_send()

    @pl.when(jnp.logical_not(twice))
    def _():
        waiter(zsrc.at[pl.ds(0, (tiles - 1) * 8)], 16).wait_send()

    back_long.wait()
    widen_long(1 - core)
    back_short.wait()
    widen_short(1 - core)


def finish(feat, gcoarse, grads, glift, gland, ggain, *rest):
    outs, dma = rest[:7], rest[7]
    sources = (grads.at[1], grads.at[0], feat, gcoarse, glift, gland, ggain)
    copies = [pltpu.make_async_copy(a, b, dma.at[k]) for k, (a, b) in enumerate(zip(sources, outs))]
    for copy in copies:
        copy.start()
    for copy in copies:
        copy.wait()


def shards(*args):
    (
        coarse_blocks,
        block_ids,
        quadrant,
        land_mask,
        lift_weight,
        land_vector,
        norm_gain,
        first_weight,
        second_weight,
        cotangent,
    ) = args
    n_row, n_col = lax.axis_size("row"), lax.axis_size("col")
    n_xy, n_z = n_row, n_col // 2

    def body(*refs):
        kernel(n_row, n_col, *refs)

    hbm = pl.BlockSpec(memory_space=pltpu.HBM)
    vmem = pl.BlockSpec(memory_space=pltpu.VMEM)
    rows_long = 6 * CH // n_xy
    rows_short = 3 * CH // n_xy
    pad_short = -(-rows_short // 16) * 16
    results = [
        jax.ShapeDtypeStruct((TILE, TILE, CH), BF16),
        jax.ShapeDtypeStruct((CIN, 2, CH), F32),
        jax.ShapeDtypeStruct((2, HALF, CH), F32),
        jax.ShapeDtypeStruct((CIN, CH), F32),
        jax.ShapeDtypeStruct((1, CH), F32),
        jax.ShapeDtypeStruct((1, CH), F32),
    ]
    scratch = [
        pltpu.VMEM((CIN, 2, CH), BF16),
        pltpu.SMEM(block_ids.shape, jnp.int32),
        pltpu.SMEM(quadrant.shape, jnp.int32),
        pltpu.VMEM((TILE, TILE), jnp.int32),
        pltpu.VMEM((CIN, CH), BF16),
        pltpu.VMEM((1, CH), F32),
        pltpu.VMEM((1, CH), F32),
        pltpu.VMEM((3, 32, CH), F32),
        pltpu.VMEM((9, 2, 32, CH), BF16),
        pltpu.VMEM((CH, 512), BF16),
        pltpu.VMEM((CH, PIX), BF16),
        pltpu.VMEM((CH, CH), BF16),
        pltpu.VMEM((2, 64, CH), BF16),
        pltpu.VMEM((512, 3 * CH), BF16),
        pltpu.VMEM((TAPS, CH, CH), BF16),
        pltpu.VMEM((TAPS, CH, CH), BF16),
        pltpu.VMEM((TILE, TILE, CH), BF16),
        pltpu.VMEM((CH, HALF), BF16),
        pltpu.VMEM((CH, HALF), BF16),
        pltpu.VMEM((2, ROWS, WIDE, CH), F32),
        pltpu.VMEM((2, 2, 2, TILE, CH), F32),
        pltpu.VMEM((2, 2, 2, TILE, CH), F32),
        pltpu.VMEM((2, 2, 2, 40, CH), F32),
        pltpu.VMEM((2, 2, 2, 40, CH), F32),
        pltpu.VMEM((2, ROWS, WIDE, 3 * CH), BF16),
        pltpu.VMEM((ROWS, WIDE, 3 * CH), BF16),
        pltpu.VMEM((ROWS, WIDE, 3 * CH), BF16),
        pltpu.VMEM((2, ROWS, WIDE, CH), BF16),
        pltpu.VMEM((ROWS, WIDE, CH), F32),
        pltpu.VMEM((TILE, TILE, CH), F32),
        pltpu.VMEM((PIX, 4 * CH), BF16),
        pltpu.VMEM((2, 2, CH), F32),
        pltpu.VMEM((n_xy, 2, CH), F32),
        pltpu.VMEM((n_z, 2, CH), F32),
        pltpu.VMEM((2, 2, CH), F32),
        pltpu.VMEM((n_xy, 2, CH), F32),
        pltpu.VMEM((n_z, 2, CH), F32),
        pltpu.VMEM((2, n_xy, rows_long, CH), BF16),
        pltpu.VMEM((2, n_xy, pad_short, CH), BF16),
        pltpu.VMEM((2, 24, CH), F32),
        pltpu.VMEM((24, CH), F32),
        pltpu.VMEM((n_xy, 8, CH), F32),
        pltpu.VMEM((24, CH), F32),
        pltpu.VMEM((n_z, 8, CH), F32),
        pltpu.VMEM((2, 24, CH), F32),
        pltpu.VMEM((2, 6 * CH, CH), F32),
        pltpu.VMEM((2, 3 * CH, CH), F32),
        pltpu.VMEM((6 * CH, CH), F32),
        pltpu.VMEM((3 * CH, CH), F32),
        pltpu.VMEM((n_xy, rows_long, CH), F32),
        pltpu.VMEM((n_xy, rows_short, CH), F32),
        pltpu.VMEM((n_xy, rows_long, CH), F32),
        pltpu.VMEM((n_xy, rows_short, CH), F32),
        pltpu.VMEM((rows_long + rows_short, CH), F32),
        pltpu.VMEM((2, n_z, 8, CH), F32),
        pltpu.VMEM((rows_long + rows_short, CH), F32),
        pltpu.VMEM((9, 2, 24, CH), F32),
        pltpu.VMEM((9, 2, 24, CH), F32),
        pltpu.SemaphoreType.DMA((10,)),
        pltpu.SemaphoreType.DMA((29,)),
        pltpu.SemaphoreType.DMA((29,)),
        pltpu.SemaphoreType.REGULAR,
    ]
    parts = pl.pallas_call(
        body,
        out_shape=results,
        in_specs=[hbm] * 10,
        out_specs=[vmem] * 6,
        scratch_shapes=scratch,
        compiler_params=pltpu.CompilerParams(
            collective_id=0, has_side_effects=True, vmem_limit_bytes=44 << 20
        ),
        name="block",
    )(
        *(
            pltpu.with_memory_space_constraint(operand, pltpu.HBM)
            for operand in (
                jnp.transpose(coarse_blocks[0, 0], (1, 0, 2)),
                block_ids,
                quadrant,
                land_mask,
                lift_weight,
                land_vector.reshape(1, CH),
                norm_gain.reshape(1, CH),
                first_weight,
                second_weight,
                cotangent,
            )
        )
    )
    wide = jax.ShapeDtypeStruct((HALF, CH), F32)
    outputs = [wide, wide, results[0], results[1]] + results[3:]
    grad_first, grad_second, features, grad_coarse, grad_lift, grad_land, grad_gain = pl.pallas_call(
        finish,
        out_shape=outputs,
        in_specs=[vmem] * 6,
        out_specs=[hbm] * 7,
        scratch_shapes=[pltpu.SemaphoreType.DMA((7,))],
        compiler_params=pltpu.CompilerParams(vmem_limit_bytes=16 << 20),
        name="finish",
    )(*parts)
    return (
        features,
        jnp.transpose(grad_coarse, (1, 0, 2))[None, None],
        grad_first.reshape(TAPS, CH, CH),
        grad_second.reshape(TAPS, CH, CH),
        grad_lift,
        grad_land.reshape(CH),
        grad_gain.reshape(CH),
    )


def solution(mesh):
    in_specs = (
        P("row", "col", None, None, None),
        P("row", "col", None),
        P("row", "col", None),
        P("row", "col"),
        P(),
        P(),
        P(),
        P(),
        P(),
        P("row", "col", None),
    )
    out_specs = (P("row", "col", None), P("row", "col", None, None, None), P(), P(), P(), P(), P())
    return jax.shard_map(shards, mesh=mesh, in_specs=in_specs, out_specs=out_specs, check_vma=False)
```

```python
import math

import jax
import jax.numpy as jnp
from jax import lax
from jax.experimental import pallas as pl
from jax.experimental.pallas import tpu as pltpu
from jax.sharding import PartitionSpec as P

GROUPS = 32
EPSILON = 1e-05
MESH = pl.DeviceIdType.MESH
F32 = jnp.float32
BF16 = jnp.bfloat16

TILE = 32
ROWS = TILE + 4
WIDE = 48
LEFT = 8
CH = 128
CIN = 20
PIX = TILE * TILE
TAPS = 9
FAR_FIRST = tuple(
    sum(step << (4 * k) for k, step in enumerate(half))
    for half in ((5, 3, 7, 12, 13, 1, 4, 2), (10, 11, 14, 15, 6, 8, 9))
)
HALF = TAPS * CH


def log2(n):
    return n.bit_length() - 1


def size_of(group):
    n = 1
    for _, _, count in group:
        n *= count
    return n


def place_in(group, at):
    m = 0
    for axis, stride, count in group:
        m = (m << log2(count)) | ((at[axis] >> log2(stride)) & (count - 1))
    return m


def member_of(group, at, m):
    new = dict(at)
    for axis, stride, count in reversed(group):
        digit = m & (count - 1)
        m = m >> log2(count)
        new[axis] = (new[axis] & ~((count - 1) * stride)) | (digit << log2(stride))
    return (new["row"], new["col"])


def each_other(group, at, act):
    n = size_of(group)
    me = place_in(group, at)
    flat = len(group) == 2 and n == 16

    def body(k, carry):
        if flat:
            step = jnp.where(k < 8, FAR_FIRST[0], FAR_FIRST[1])
            m = me ^ ((step >> ((k & 7) * 4)) & 15)
        else:
            away = (k + 1) >> 1
            m = (me + n // 2 + jnp.where((k & 1) == 1, away, -away) + n) & (n - 1)
        act(member_of(group, at, m), m)
        return carry

    lax.fori_loop(0, n - 1, body, 0)


def remote(src, dst, send, recv, device):
    return pltpu.make_async_remote_copy(
        src_ref=src,
        dst_ref=dst,
        send_sem=send,
        recv_sem=recv,
        device_id=device,
        device_id_type=MESH,
    )


def dot(a, b):
    return jnp.dot(a, b, preferred_element_type=F32)


def dot_tn(a, b):
    return lax.dot_general(a, b, (((0,), (0,)), ((), ())), preferred_element_type=F32)


def dot_nt(a, b):
    return lax.dot_general(a, b, (((1,), (1,)), ((), ())), preferred_element_type=F32)


def split_two(x):
    hi = x.astype(BF16)
    return hi, (x - hi.astype(F32)).astype(BF16)


def split_three(x):
    hi = x.astype(BF16)
    rest = x - hi.astype(F32)
    mid = rest.astype(BF16)
    return hi, mid, (rest - mid.astype(F32)).astype(BF16)


def sigmoid(v):
    return 1.0 / (1.0 + jnp.exp(-v))


def group_sums(v):
    lane = lax.broadcasted_iota(jnp.int32, v.shape, 1)
    one = v + jnp.where((lane & 1) == 1, pltpu.roll(v, 1, 1), pltpu.roll(v, CH - 1, 1))
    return one + jnp.where((lane & 2) == 2, pltpu.roll(one, 2, 1), pltpu.roll(one, CH - 2, 1))


def kernel(
    n_row,
    n_col,
    coarse_hbm,
    ids_hbm,
    quad_hbm,
    land_hbm,
    lift_hbm,
    land_v_hbm,
    gain_hbm,
    w1_hbm,
    w2_hbm,
    cot_hbm,
    feat,
    gcoarse,
    grads,
    glift,
    gland,
    ggain,
    coarse,
    ids,
    quad,
    land,
    lift_w,
    land_v,
    gain_ref,
    padf,
    cand,
    up,
    ft,
    wext,
    wpair,
    upt,
    w1,
    w2,
    cotv,
    wt1,
    wt2,
    ext,
    rh_s,
    rh_r,
    ch_s,
    ch_r,
    x3ab,
    x3c,
    x3g,
    gi,
    t2,
    gsc,
    glb,
    a1c,
    a1x,
    a1z,
    a2c,
    a2x,
    a2z,
    long_out,
    short_out,
    msend,
    mrecv,
    mxy,
    mown,
    mz,
    mall,
    glong,
    gshort,
    clong,
    cshort,
    along,
    ashort,
    xylong,
    xyshort,
    zsrc,
    zb,
    zres,
    ret_s,
    ret_r,
    dma,
    snd,
    rcv,
    answers,
):
    row = lax.axis_index("row")
    col = lax.axis_index("col")
    at = {"row": row, "col": col}
    core_g = (("row", 1, 2),)
    xy_g = (("row", 2, n_row // 2), ("col", n_col // 2, 2))
    z_g = (("col", 1, n_col // 2),)
    n_xy = size_of(xy_g)
    n_z = size_of(z_g)
    members = float(n_row * TILE * n_col * TILE * (CH // GROUPS))
    report = 1.0 / math.sqrt(n_row * TILE * n_col * TILE)
    pixels_all = float(n_row * TILE * n_col * TILE)

    core = place_in(core_g, at)
    xy = place_in(xy_g, at)
    z = place_in(z_g, at)
    core_dev = member_of(core_g, at, 1 - core)
    x3b, x3a = x3ab.at[0], x3ab.at[1]
    gic, gig = gi.at[0], gi.at[1]

    def near(dr, dc):
        return ((row + dr + n_row) & (n_row - 1), (col + dc + n_col) & (n_col - 1))

    around = [(dr, dc) for dr in (-1, 0, 1) for dc in (-1, 0, 1)]

    def waiter(ref, k):
        return remote(ref, ref, snd.at[k], rcv.at[k], core_dev)

    barrier = pltpu.get_barrier_semaphore()

    def greet(device, m):
        pl.semaphore_signal(barrier, inc=1, device_id=device, device_id_type=MESH)

    for dr, dc in around:
        if (dr, dc) != (0, 0):
            greet(near(dr, dc), 0)
    for group in (core_g, xy_g):
        each_other(group, at, greet)

    def along_z(away):
        return member_of(z_g, at, (z + away + n_z) & (n_z - 1))

    quarter = n_z // 4
    for away in range(quarter, 0, -1):
        greet(along_z(away), 0)
        greet(along_z(-away), 0)

    pairs = [
        (coarse_hbm, coarse),
        (lift_hbm, lift_w),
        (ids_hbm, ids),
        (quad_hbm, quad),
        (land_hbm, land),
        (land_v_hbm, land_v),
        (gain_hbm, gain_ref),
        (cot_hbm, cotv),
        (w2_hbm, w2),
        (w1_hbm, w1),
    ]
    loads = [pltpu.make_async_copy(a, b, dma.at[k]) for k, (a, b) in enumerate(pairs)]
    for load in loads:
        load.start()

    padf[...] = jnp.zeros_like(padf)
    for load in loads[:2]:
        load.wait()
    for m in range(2):
        padf[m, 0:CIN, :] = coarse[:, m, :].astype(F32)
    padf[2, 0:CIN, :] = lift_w[...].astype(F32)
    cand[4] = padf[0:2].astype(BF16)

    pl.semaphore_wait(barrier, 8 + 1 + n_xy - 1 + 2 * quarter)

    for s, (dr, dc) in enumerate(around):
        if s != 4:
            remote(cand.at[4], cand.at[8 - s], snd.at[0], rcv.at[0], near(dr, dc)).start()

    for away in (quarter, -quarter):
        pl.semaphore_signal(answers, inc=1, device_id=along_z(away), device_id_type=MESH)

    for load in loads[2:]:
        load.wait()
    codes = []
    for k in range(ids.shape[2]):
        block = ids[0, 0, k]
        owner = block >> 1
        slot_row = (owner >> log2(n_col)) - row + 1
        slot_col = (owner & (n_col - 1)) - col + 1
        codes.append(((quad[0, 0, k] * 9) + slot_row * 3 + slot_col) * 2 + (block & 1))

    def picks(q, s, m):
        want = (q * 9 + s) * 2 + m
        total = jnp.float32(0.0)
        for code in codes:
            total = total + jnp.where(code == want, jnp.float32(1.0), jnp.float32(0.0))
        return total

    weight = {(q, s, m): picks(q, s, m) for q in range(2) for s in range(9) for m in range(2)}

    fine = lax.broadcasted_iota(jnp.int32, (CH, 512), 1)
    cell = lax.broadcasted_iota(jnp.int32, (CH, 512), 0)

    def hat(fine_at, cell_at, count):
        where = jnp.clip((fine_at.astype(F32) + 0.5) * 0.5 - 0.5, 0.0, count - 1.0)
        return jnp.maximum(1.0 - jnp.abs(where - cell_at.astype(F32)), 0.0)

    up[...] = (hat(fine >> 5, cell >> 4, 8) * hat(fine & 31, cell & 15, 16)).astype(BF16)
    fine = lax.broadcasted_iota(jnp.int32, (512, CH), 0)
    cell = lax.broadcasted_iota(jnp.int32, (512, CH), 1)
    turned = (hat(fine >> 5, cell >> 4, 8) * hat(fine & 31, cell & 15, 16)).astype(BF16)
    for k in range(3):
        upt[:, k * CH : (k + 1) * CH] = turned

    pix = lax.broadcasted_iota(jnp.int32, (TILE, PIX), 1)
    line = lax.broadcasted_iota(jnp.int32, (TILE, PIX), 0)
    spread = jnp.where((pix & 31) == line, 1.0, 0.0).astype(BF16)
    lines = dot(land[...].astype(F32).astype(BF16), spread)
    lines = jnp.where((pix >> 5) == line, lines, 0.0).astype(BF16)
    wext[0:32] = padf[2].astype(BF16)
    wpair[...] = jnp.zeros_like(wpair)
    wpair[0, 0:32] = wext[0:32]
    wpair[1, 32:64] = wext[0:32]
    for k, part in enumerate(split_three(jnp.broadcast_to(land_v[...], (32, CH)))):
        ft[32 * (k + 1) : 32 * (k + 2), :] = lines
        wext[32 * (k + 1) : 32 * (k + 2), :] = part
    on_land = dot_tn(ft[32:], wext[32:])
    ext[0, 2 : 2 + TILE, LEFT : LEFT + TILE, :] = on_land.reshape(TILE, TILE, CH)

    for lo, hi in ((0, LEFT), (LEFT + TILE, WIDE)):
        ext[:, :, lo:hi, :] = jnp.zeros((2, ROWS, 8, CH), F32)
    for edge in (0, ROWS - 1):
        gi[:, edge] = jnp.zeros((2, WIDE, CH), BF16)

    for k in range(TAPS):
        wt1[:, k * CH : (k + 1) * CH] = w1[8 - k]
        wt2[:, k * CH : (k + 1) * CH] = w2[8 - k]
    ext[1, 2 : 2 + TILE, LEFT : LEFT + TILE, :] = cotv[...].astype(F32)

    def pack_rows(a):
        rh_s[a, 0] = ext[a, 2:4, LEFT : LEFT + TILE, :]
        rh_s[a, 1] = ext[a, TILE : TILE + 2, LEFT : LEFT + TILE, :]

    def send_rows(a, k):
        for side, step in ((0, -1), (1, 1)):
            remote(rh_s.at[a, side], rh_r.at[a, side], snd.at[k], rcv.at[k], near(step, 0)).start()

    def rows_to_columns(a, k_rows, k_cols):
        waiter(rh_r.at[a], k_rows).wait()
        ext[a, 2 + TILE : 4 + TILE, LEFT : LEFT + TILE, :] = rh_r[a, 0]
        ext[a, 0:2, LEFT : LEFT + TILE, :] = rh_r[a, 1]
        for k in range(2):
            ch_s[a, 0, k, 0:ROWS, :] = ext[a, :, LEFT + k, :]
            ch_s[a, 1, k, 0:ROWS, :] = ext[a, :, LEFT + TILE - 2 + k, :]
        for side, step in ((0, -1), (1, 1)):
            remote(ch_s.at[a, side], ch_r.at[a, side], snd.at[k_cols], rcv.at[k_cols], near(0, step)).start()

    def put_columns(a, k_cols):
        waiter(ch_r.at[a], k_cols).wait()
        for k in range(2):
            ext[a, :, LEFT + TILE + k, :] = ch_r[a, 0, k, 0:ROWS, :]
            ext[a, :, LEFT - 2 + k, :] = ch_r[a, 1, k, 0:ROWS, :]

    pack_rows(1)
    send_rows(1, 27)

    waiter(cand.at[pl.ds(0, 8)], 0).wait_recv()
    sums = []
    for q in range(2):
        total = jnp.zeros((32, CH), F32)
        for s in range(9):
            for m in range(2):
                total = total + weight[q, s, m] * cand[s, m].astype(F32)
        sums.append(total)
    parts = split_three(jnp.concatenate(sums, axis=0))
    raised = dot_nt(upt[...], jnp.concatenate(parts, axis=1)).astype(BF16)
    lifted = jnp.concatenate(
        [
            dot(raised, wpair[q]) + ext[0, 2 + 16 * q : 18 + 16 * q, LEFT : LEFT + TILE, :].reshape(512, CH)
            for q in range(2)
        ],
        axis=0,
    )
    ext[0, 2 : 2 + TILE, LEFT : LEFT + TILE, :] = lifted.reshape(TILE, TILE, CH)
    mean_here = jnp.sum(lifted, axis=0, keepdims=True) * (1.0 / PIX)
    apart = lifted - mean_here
    square_here = jnp.sum(apart * apart, axis=0, keepdims=True)

    def start_level(group, buf, k, value):
        me = place_in(group, at)
        buf[me] = value

        def send(device, m):
            remote(buf.at[me], buf.at[me], snd.at[k], rcv.at[k], device).start()

        each_other(group, at, send)

    def end_level(buf, k):
        waiter(buf.at[pl.ds(0, buf.shape[0] - 1)], k).wait()
        return [buf[i] for i in range(buf.shape[0])]

    def add_up(values):
        while len(values) > 1:
            values = [a + b for a, b in zip(values[::2], values[1::2])]
        return values[0]

    def merge(values, count):
        mean = add_up([v[0:1] for v in values]) * (1.0 / len(values))
        square = add_up([v[1:2] for v in values])
        off = add_up([(v[0:1] - mean) * (v[0:1] - mean) for v in values])
        return jnp.concatenate([mean, square + count * off], axis=0)

    start_level(core_g, a1c, 1, jnp.concatenate([mean_here, square_here], axis=0))

    pack_rows(0)
    rows_to_columns(1, 27, 28)
    by_field = dot(jnp.concatenate(parts, axis=0), up[...])
    by_field = by_field[0:64] + by_field[64:128] + by_field[128:192]
    ft[0:32, 0:512] = by_field[0:32].astype(BF16)
    ft[0:32, 512:1024] = by_field[32:64].astype(BF16)

    moments = merge(end_level(a1c, 1), float(PIX))
    start_level(xy_g, a1x, 2, moments)
    send_rows(0, 4)
    rows_to_columns(0, 4, 5)

    moments = merge(end_level(a1x, 2), float(2 * PIX))
    pl.semaphore_wait(answers, 2)
    start_level(z_g, a1z, 3, moments)
    put_columns(1, 28)

    row_lo = jnp.where(row == 0, 2, 0)
    row_hi = jnp.where(row == n_row - 1, 2 + TILE, ROWS)
    col_lo = jnp.where(col == 0, LEFT, 0)
    col_hi = jnp.where(col == n_col - 1, LEFT + TILE, WIDE)

    def masks(first, count):
        r = lax.broadcasted_iota(jnp.int32, (count, WIDE, CH), 0) + first
        c = lax.broadcasted_iota(jnp.int32, (count, WIDE, CH), 1)
        in_grid = (r >= row_lo) & (r < row_hi) & (c >= col_lo) & (c < col_hi)
        in_tile = (r >= 2) & (r < 2 + TILE) & (c >= LEFT) & (c < LEFT + TILE)
        shape = (count * WIDE, CH)
        return in_grid.reshape(shape), in_tile.reshape(shape)

    def put_taps(x3, first, count, flat):
        length = count * WIDE
        x3[pl.ds(first, count), :, 0:CH] = pltpu.roll(flat, 1, 0).astype(BF16).reshape(count, WIDE, CH)
        x3[pl.ds(first, count), :, CH : 2 * CH] = flat.astype(BF16).reshape(count, WIDE, CH)
        x3[pl.ds(first, count), :, 2 * CH :] = (
            pltpu.roll(flat, length - 1, 0).astype(BF16).reshape(count, WIDE, CH)
        )

    def windows(x3, first, count):
        return jnp.concatenate(
            [x3[pl.ds(first - 1 + u, count)].reshape(count * WIDE, 3 * CH) for u in range(3)],
            axis=1,
        )

    def loop(trips, body):
        def step(i, carry):
            body(i)
            return carry

        lax.fori_loop(0, trips, step, 0)

    def cot_rows(i):
        first = i * 4
        in_grid, in_tile = masks(first, 4)
        flat = ext[1, pl.ds(first, 4)].reshape(4 * WIDE, CH)
        put_taps(x3c, first, 4, jnp.where(in_grid, flat, 0.0))
        gic[pl.ds(first, 4)] = jnp.where(in_tile, flat, 0.0).astype(BF16).reshape(4, WIDE, CH)

    loop(9, cot_rows)

    def cot_conv(i):
        first = 1 + i * 17
        t2[pl.ds(first, 17)] = dot_nt(windows(x3c, first, 17), wt2[...]).reshape(17, WIDE, CH)

    loop(2, cot_conv)
    put_columns(0, 5)

    moments = merge(end_level(a1z, 3), float(2 * n_xy * PIX))
    mean_ch = moments[0:1]
    group_mean = group_sums(mean_ch) * (GROUPS / CH)
    off = mean_ch - group_mean
    variance = group_sums(moments[1:2] + pixels_all * off * off) / members
    inv_spread = lax.rsqrt(variance + EPSILON)
    gain = gain_ref[...]

    def act_rows(i):
        first = i * 4
        in_grid, _ = masks(first, 4)
        flat = ext[0, pl.ds(first, 4)].reshape(4 * WIDE, CH)
        scaled = (flat - group_mean) * inv_spread * gain
        act = scaled * sigmoid(scaled)
        put_taps(x3a, first, 4, jnp.where(in_grid, act, 0.0))

    loop(9, act_rows)

    def hidden_rows(i):
        first = 1 + i * 17
        in_grid, in_tile = masks(first, 17)
        hidden = dot(windows(x3a, first, 17), w1[...].reshape(HALF, CH))
        gate = sigmoid(hidden)
        act = jnp.where(in_grid, hidden * gate, 0.0)
        slope = gate * (1.0 + hidden * (1.0 - gate))
        grad = jnp.where(in_grid, t2[pl.ds(first, 17)].reshape(17 * WIDE, CH) * slope, 0.0)
        put_taps(x3b, first, 17, act)
        put_taps(x3g, first, 17, grad)
        gig[pl.ds(first, 17)] = jnp.where(in_tile, grad, 0.0).astype(BF16).reshape(17, WIDE, CH)

    loop(2, hidden_rows)

    def tap_grads(half):
        length = (ROWS - 2) * WIDE
        grad = jnp.concatenate(
            [gi[half, 2 - u : 2 - u + ROWS - 2].reshape(length, CH) for u in range(3)], axis=1
        )
        out = dot_tn(x3ab[half, 1 : ROWS - 1].reshape(length, 3 * CH), grad)
        for u in range(3):
            for v in range(3):
                to, first = (glong, 3 * u + v) if u < 2 else (gshort, v)
                to[half, first * CH : (first + 1) * CH, :] = out[
                    v * CH : (v + 1) * CH, u * CH : (u + 1) * CH
                ]

    tap_grads(1 - core)
    swap_long = remote(glong.at[1 - core], clong, snd.at[6], rcv.at[6], core_dev)
    swap_long.start()
    swap_short = remote(gshort.at[1 - core], cshort, snd.at[7], rcv.at[7], core_dev)
    swap_short.start()
    tap_grads(core)

    inner = slice(LEFT, LEFT + TILE)

    def out_rows(i):
        first = 2 + i * 16
        out = dot(windows(x3b, first, 16), w2[...].reshape(HALF, CH)).reshape(16, WIDE, CH)
        feat[pl.ds(i * 16, 16)] = (ext[0, pl.ds(first, 16), inner, :] + out[:, inner, :]).astype(BF16)

    def share_out(mine, theirs, to, landing, k):
        def add(m, carry):
            rows = pl.ds(pl.multiple_of(m * mine.shape[1] // n_xy, 8), mine.shape[1] // n_xy)
            total = mine[core, rows, :] + theirs[rows, :]
            to[m] = total
            return carry

        lax.fori_loop(0, n_xy, add, 0)

        def send(device, m):
            remote(to.at[m], landing.at[xy], snd.at[k], rcv.at[k], device).start()

        each_other(xy_g, at, send)
        landing[xy] = to[xy]

    swap_long.wait_recv()
    share_out(glong, clong, along, xylong, 8)
    swap_short.wait_recv()
    share_out(gshort, cshort, ashort, xyshort, 9)

    def back_rows(i, sums):
        first = 2 + i * 8
        grad_act = dot_nt(windows(x3g, first, 8), wt1[...]).reshape(8, WIDE, CH)[:, inner, :]
        normed = (ext[0, pl.ds(first, 8), inner, :] - group_mean[None]) * inv_spread[None]
        scaled = normed * gain[None]
        gate = sigmoid(scaled)
        grad = grad_act * (gate * (1.0 + scaled * (1.0 - gate)))
        gsc[pl.ds(i * 8, 8)] = grad
        straight = inv_spread[None] * (grad * gain[None]) + ext[1, pl.ds(first, 8), inner, :]
        spot = pl.ds(pl.multiple_of(i * 256, 256), 256)
        for k, part in enumerate(split_two(straight.reshape(256, CH)) + split_two(normed.reshape(256, CH))):
            glb[spot, k * CH : (k + 1) * CH] = part
        plain, cross = sums
        return (
            plain + jnp.sum(grad.reshape(32, 8, CH), axis=0),
            cross + jnp.sum((grad * normed).reshape(32, 8, CH), axis=0),
        )

    nothing = jnp.zeros((8, CH), F32)
    plain, cross = lax.fori_loop(0, 4, back_rows, (nothing, nothing))
    both = jnp.concatenate(
        [jnp.sum(plain, axis=0, keepdims=True), jnp.sum(cross, axis=0, keepdims=True)], axis=0
    )
    start_level(core_g, a2c, 10, both)

    which = lax.broadcasted_iota(jnp.int32, (24, CH), 0)
    lane = lax.broadcasted_iota(jnp.int32, (24, CH), 1)
    field_rows = dot(ft[...], glb[...])

    def field_sums(k):
        part = field_rows[:, k * CH : (k + 1) * CH] + field_rows[:, (k + 1) * CH : (k + 2) * CH]
        on_land = jnp.sum(part[32:64], axis=0, keepdims=True)
        return jnp.where(which == CIN, on_land, part[0:24])

    alone = dot_nt(jnp.full((8, PIX), 1.0, BF16), ft[...])[0:1]
    msend[0] = field_sums(0)
    msend[1] = jnp.where(which == CIN + 1, alone, field_sums(2))
    m_swap = remote(msend.at[1 - core], mrecv, snd.at[13], rcv.at[13], core_dev)
    m_swap.start()

    out_rows(0)
    out_rows(1)

    start_level(xy_g, a2x, 11, add_up(end_level(a2c, 10)))

    goals = [(5 * t + 8 * core + 1) & (n_xy - 1) for t in range(3)]
    held = [goal == xy for goal in goals]
    holder = held[0] | held[1] | held[2]

    m_swap.wait_recv()
    mown[...] = msend[core] + mrecv[...]
    for t in range(3):
        strip = mown.at[8 * t : 8 * t + 8]

        @pl.when(jnp.logical_not(held[t]))
        def _():
            remote(strip, mxy.at[xy], snd.at[14], rcv.at[14], member_of(xy_g, at, goals[t])).start()

        @pl.when(held[t])
        def _():
            mxy[xy] = mown[8 * t : 8 * t + 8]

    long_rows = glong.shape[1] // n_xy
    long_tiles = long_rows // 8
    tiles = zsrc.shape[0] // 8
    spare = tiles - 1
    turn = (xy + 8 * core) & (n_z - 1)
    own = (z - turn) & (n_z // 2 - 1)
    twice = own == 0

    def send_tile(t, carry):
        for half in range(2):
            goal = (t + turn + half * n_z // 2) & (n_z - 1)
            slot = jnp.where(t == spare, 1, 0)

            @pl.when(goal != z)
            def _():
                remote(
                    zsrc.at[pl.ds(pl.multiple_of(t * 8, 8), 8)],
                    zb.at[slot, z],
                    snd.at[16],
                    rcv.at[jnp.where(t == spare, 26, 16)],
                    member_of(z_g, at, goal),
                ).start()

        return carry

    waiter(xylong.at[pl.ds(0, n_xy - 1)], 8).wait_recv()
    zsrc[0:long_rows] = add_up([xylong[i] for i in range(n_xy)])
    lax.fori_loop(0, long_tiles, send_tile, 0)
    waiter(xyshort.at[pl.ds(0, n_xy - 1)], 9).wait_recv()
    zsrc[long_rows:] = add_up([xyshort[i] for i in range(n_xy)])
    lax.fori_loop(long_tiles, tiles, send_tile, 0)

    start_level(z_g, a2z, 12, add_up(end_level(a2x, 11)))

    @pl.when(holder)
    def _():
        waiter(mxy.at[pl.ds(0, n_xy - 1)], 14).wait_recv()
        start_level(z_g, mz, 15, add_up([mxy[i] for i in range(n_xy)]))

    def whole_tile(slot, tile, k_in, k_out):
        spot = pl.ds(pl.multiple_of(tile * 8, 8), 8)
        zb[slot, z] = zsrc[spot, :]
        waiter(zb.at[slot, pl.ds(0, n_z - 1)], k_in).wait_recv()
        zres[spot, :] = add_up([zb[slot, i] for i in range(n_z)]) * report

        def send(k, carry):
            away = (k + 1) >> 1
            goal = z + jnp.where((k & 1) == 1, n_z // 4 - away, away - n_z // 4)
            device = member_of(z_g, at, (goal + n_z) & (n_z - 1))
            remote(zres.at[spot], zres.at[spot], snd.at[17], rcv.at[k_out], device).start()
            return carry

        lax.fori_loop(0, n_z // 2 - 1, send, 0)

    in_long = own < long_tiles

    @pl.when(in_long)
    def _():
        whole_tile(0, own, 16, 17)

    @pl.when(jnp.logical_not(in_long))
    def _():
        whole_tile(0, own, 16, 18)

    @pl.when(twice)
    def _():
        whole_tile(1, spare, 26, 18)

    totals = add_up(end_level(a2z, 12))
    ggain[...] = totals[1:2] * report
    plain_sum = group_sums(totals[0:1] * gain) * (1.0 / members)
    cross_sum = group_sums(totals[1:2] * gain) * (1.0 / members)

    def lifted_rows(i):
        first = 2 + i * 8
        normed = (ext[0, pl.ds(first, 8), inner, :] - group_mean[None]) * inv_spread[None]
        grad = gsc[pl.ds(i * 8, 8)] * gain[None] - plain_sum[None] - normed * cross_sum[None]
        grad = inv_spread[None] * grad + ext[1, pl.ds(first, 8), inner, :]
        glb[pl.ds(pl.multiple_of(i * 256, 256), 256), 0:CH] = grad.reshape(256, CH).astype(BF16)

    loop(4, lifted_rows)

    fine_hi, fine_lo = split_two(dot_nt(wext[0:32], glb[:, 0:CH]))
    stacked = jnp.concatenate(
        [fine_hi[:, 0:512], fine_hi[:, 512:], fine_lo[:, 0:512], fine_lo[:, 512:]], axis=0
    )
    lowered = dot_nt(stacked, up[...])
    lowered = lowered[0:64] + lowered[64:128]
    for s, (dr, dc) in enumerate(around):
        for m in range(2):
            ret_s[s, m] = weight[0, s, m] * lowered[0:24] + weight[1, s, m] * lowered[32:56]
        if s != 4:
            remote(ret_s.at[s], ret_r.at[8 - s], snd.at[19], rcv.at[19], near(dr, dc)).start()

    @pl.when(holder)
    def _():
        waiter(mz.at[pl.ds(0, n_z - 1)], 15).wait()

    for t in range(3):
        place = mall.at[core, 8 * t : 8 * t + 8]

        @pl.when(held[t])
        def _():
            mall[core, 8 * t : 8 * t + 8, :] = add_up([mz[i] for i in range(n_z)])

            def send(device, m):
                remote(place, place, snd.at[20], rcv.at[20], device).start()

            each_other(xy_g, at, send)

    def wait_tiles(count, some_mine, k):
        @pl.when(some_mine)
        def _():
            waiter(zres.at[pl.ds(0, (count - 1) * 8)], k).wait_recv()

        @pl.when(jnp.logical_not(some_mine))
        def _():
            waiter(zres.at[pl.ds(0, count * 8)], k).wait_recv()

    def send_shares(out, k):
        piece = out.at[core, xy]

        def send(device, m):
            remote(piece, piece, snd.at[k], rcv.at[k], device).start()

        each_other(xy_g, at, send)

    wait_tiles(long_tiles, in_long, 17)
    long_out[core, xy] = zres[0:long_rows].astype(BF16)
    send_shares(long_out, 21)
    wait_tiles(tiles - long_tiles, jnp.logical_not(in_long) | twice, 18)
    rest = zres[long_rows:]
    short_out[core, xy] = jnp.concatenate([rest, jnp.zeros((short_out.shape[2] - rest.shape[0], CH), F32)], axis=0).astype(BF16)
    send_shares(short_out, 22)

    long_all = n_xy * long_rows
    short_rows = zsrc.shape[0] - long_rows

    def widen_long(half):
        grads[half, 0:long_all, :] = long_out[half].astype(F32).reshape(long_all, CH)

    def widen_short(half):
        part = short_out[half][:, 0:short_rows, :].astype(F32)
        grads[half, long_all:, :] = part.reshape(n_xy * short_rows, CH)

    waiter(long_out.at[core, pl.ds(0, n_xy - 1)], 21).wait_recv()
    back_long = remote(long_out.at[core], long_out.at[core], snd.at[24], rcv.at[24], core_dev)
    back_long.start()
    waiter(ret_r.at[pl.ds(0, 8)], 19).wait()
    for m in range(2):
        total = ret_s[4, m]
        for s in range(9):
            if s != 4:
                total = total + ret_r[s, m]
        gcoarse[:, m, :] = total[0:CIN]

    @pl.when(holder)
    def _():
        waiter(mall.at[core, 0:16], 20).wait_recv()

    @pl.when(jnp.logical_not(holder))
    def _():
        waiter(mall.at[core], 20).wait_recv()

    m_back = remote(mall.at[core], mall.at[core], snd.at[23], rcv.at[23], core_dev)
    m_back.start()
    widen_long(core)

    waiter(short_out.at[core, pl.ds(0, n_xy - 1)], 22).wait_recv()
    back_short = remote(short_out.at[core], short_out.at[core], snd.at[25], rcv.at[25], core_dev)
    back_short.start()
    widen_short(core)

    m_back.wait()
    straight, crossed = mall[0], mall[1]
    fields = ((lane == which) & (which < CIN)) | ((which == CIN) & (lane >= 32) & (lane < 64))
    alone = jnp.sum(jnp.where(fields, crossed[CIN + 1 : CIN + 2], 0.0), axis=1, keepdims=True)
    lift_all = straight - (inv_spread * plain_sum) * alone - (inv_spread * cross_sum) * crossed
    lift_all = lift_all * report
    glift[...] = lift_all[0:CIN]
    gland[...] = lift_all[CIN : CIN + 1]

    waiter(cand.at[pl.ds(0, 8)], 0).wait_send()
    swap_long.wait_send()
    swap_short.wait_send()
    m_swap.wait_send()
    waiter(xylong.at[pl.ds(0, n_xy - 1)], 8).wait_send()
    waiter(xyshort.at[pl.ds(0, n_xy - 1)], 9).wait_send()
    waiter(long_out.at[core, pl.ds(0, n_xy - 1)], 21).wait_send()
    waiter(short_out.at[core, pl.ds(0, n_xy - 1)], 22).wait_send()

    @pl.when(holder)
    def _():
        waiter(mown.at[0:16], 14).wait_send()
        waiter(mxy.at[pl.ds(0, n_xy - 1)], 20).wait_send()

    @pl.when(jnp.logical_not(holder))
    def _():
        waiter(mown, 14).wait_send()

    once = n_z // 2 - 1
    waiter(zsrc, 16).wait_send()
    waiter(zb.at[0, pl.ds(0, once)], 17).wait_send()

    @pl.when(twice)
    def _():
        waiter(zsrc.at[pl.ds(0, (tiles - 2) * 8)], 16).wait_send()
        waiter(zb.at[0, pl.ds(0, once)], 17).wait_send()

    @pl.when(jnp.logical_not(twice))
    def _():
        waiter(zsrc.at[pl.ds(0, (tiles - 1) * 8)], 16).wait_send()

    back_long.wait()
    widen_long(1 - core)
    back_short.wait()
    widen_short(1 - core)


def finish(feat, gcoarse, grads, glift, gland, ggain, *rest):
    outs, dma = rest[:7], rest[7]
    sources = (grads.at[1], grads.at[0], feat, gcoarse, glift, gland, ggain)
    copies = [pltpu.make_async_copy(a, b, dma.at[k]) for k, (a, b) in enumerate(zip(sources, outs))]
    for copy in copies:
        copy.start()
    for copy in copies:
        copy.wait()


def shards(*args):
    (
        coarse_blocks,
        block_ids,
        quadrant,
        land_mask,
        lift_weight,
        land_vector,
        norm_gain,
        first_weight,
        second_weight,
        cotangent,
    ) = args
    n_row, n_col = lax.axis_size("row"), lax.axis_size("col")
    n_xy, n_z = n_row, n_col // 2

    def body(*refs):
        kernel(n_row, n_col, *refs)

    hbm = pl.BlockSpec(memory_space=pltpu.HBM)
    vmem = pl.BlockSpec(memory_space=pltpu.VMEM)
    rows_long = 6 * CH // n_xy
    rows_short = 3 * CH // n_xy
    pad_short = -(-rows_short // 16) * 16
    results = [
        jax.ShapeDtypeStruct((TILE, TILE, CH), BF16),
        jax.ShapeDtypeStruct((CIN, 2, CH), F32),
        jax.ShapeDtypeStruct((2, HALF, CH), F32),
        jax.ShapeDtypeStruct((CIN, CH), F32),
        jax.ShapeDtypeStruct((1, CH), F32),
        jax.ShapeDtypeStruct((1, CH), F32),
    ]
    scratch = [
        pltpu.VMEM((CIN, 2, CH), BF16),
        pltpu.SMEM(block_ids.shape, jnp.int32),
        pltpu.SMEM(quadrant.shape, jnp.int32),
        pltpu.VMEM((TILE, TILE), jnp.int32),
        pltpu.VMEM((CIN, CH), BF16),
        pltpu.VMEM((1, CH), F32),
        pltpu.VMEM((1, CH), F32),
        pltpu.VMEM((3, 32, CH), F32),
        pltpu.VMEM((9, 2, 32, CH), BF16),
        pltpu.VMEM((CH, 512), BF16),
        pltpu.VMEM((CH, PIX), BF16),
        pltpu.VMEM((CH, CH), BF16),
        pltpu.VMEM((2, 64, CH), BF16),
        pltpu.VMEM((512, 3 * CH), BF16),
        pltpu.VMEM((TAPS, CH, CH), BF16),
        pltpu.VMEM((TAPS, CH, CH), BF16),
        pltpu.VMEM((TILE, TILE, CH), BF16),
        pltpu.VMEM((CH, HALF), BF16),
        pltpu.VMEM((CH, HALF), BF16),
        pltpu.VMEM((2, ROWS, WIDE, CH), F32),
        pltpu.VMEM((2, 2, 2, TILE, CH), F32),
        pltpu.VMEM((2, 2, 2, TILE, CH), F32),
        pltpu.VMEM((2, 2, 2, 40, CH), F32),
        pltpu.VMEM((2, 2, 2, 40, CH), F32),
        pltpu.VMEM((2, ROWS, WIDE, 3 * CH), BF16),
        pltpu.VMEM((ROWS, WIDE, 3 * CH), BF16),
        pltpu.VMEM((ROWS, WIDE, 3 * CH), BF16),
        pltpu.VMEM((2, ROWS, WIDE, CH), BF16),
        pltpu.VMEM((ROWS, WIDE, CH), F32),
        pltpu.VMEM((TILE, TILE, CH), F32),
        pltpu.VMEM((PIX, 4 * CH), BF16),
        pltpu.VMEM((2, 2, CH), F32),
        pltpu.VMEM((n_xy, 2, CH), F32),
        pltpu.VMEM((n_z, 2, CH), F32),
        pltpu.VMEM((2, 2, CH), F32),
        pltpu.VMEM((n_xy, 2, CH), F32),
        pltpu.VMEM((n_z, 2, CH), F32),
        pltpu.VMEM((2, n_xy, rows_long, CH), BF16),
        pltpu.VMEM((2, n_xy, pad_short, CH), BF16),
        pltpu.VMEM((2, 24, CH), F32),
        pltpu.VMEM((24, CH), F32),
        pltpu.VMEM((n_xy, 8, CH), F32),
        pltpu.VMEM((24, CH), F32),
        pltpu.VMEM((n_z, 8, CH), F32),
        pltpu.VMEM((2, 24, CH), F32),
        pltpu.VMEM((2, 6 * CH, CH), F32),
        pltpu.VMEM((2, 3 * CH, CH), F32),
        pltpu.VMEM((6 * CH, CH), F32),
        pltpu.VMEM((3 * CH, CH), F32),
        pltpu.VMEM((n_xy, rows_long, CH), F32),
        pltpu.VMEM((n_xy, rows_short, CH), F32),
        pltpu.VMEM((n_xy, rows_long, CH), F32),
        pltpu.VMEM((n_xy, rows_short, CH), F32),
        pltpu.VMEM((rows_long + rows_short, CH), F32),
        pltpu.VMEM((2, n_z, 8, CH), F32),
        pltpu.VMEM((rows_long + rows_short, CH), F32),
        pltpu.VMEM((9, 2, 24, CH), F32),
        pltpu.VMEM((9, 2, 24, CH), F32),
        pltpu.SemaphoreType.DMA((10,)),
        pltpu.SemaphoreType.DMA((29,)),
        pltpu.SemaphoreType.DMA((29,)),
        pltpu.SemaphoreType.REGULAR,
    ]
    parts = pl.pallas_call(
        body,
        out_shape=results,
        in_specs=[hbm] * 10,
        out_specs=[vmem] * 6,
        scratch_shapes=scratch,
        compiler_params=pltpu.CompilerParams(
            collective_id=0, has_side_effects=True, vmem_limit_bytes=44 << 20
        ),
        name="block",
    )(
        *(
            pltpu.with_memory_space_constraint(operand, pltpu.HBM)
            for operand in (
                jnp.transpose(coarse_blocks[0, 0], (1, 0, 2)),
                block_ids,
                quadrant,
                land_mask,
                lift_weight,
                land_vector.reshape(1, CH),
                norm_gain.reshape(1, CH),
                first_weight,
                second_weight,
                cotangent,
            )
        )
    )
    wide = jax.ShapeDtypeStruct((HALF, CH), F32)
    outputs = [wide, wide, results[0], results[1]] + results[3:]
    grad_first, grad_second, features, grad_coarse, grad_lift, grad_land, grad_gain = pl.pallas_call(
        finish,
        out_shape=outputs,
        in_specs=[vmem] * 6,
        out_specs=[hbm] * 7,
        scratch_shapes=[pltpu.SemaphoreType.DMA((7,))],
        compiler_params=pltpu.CompilerParams(vmem_limit_bytes=16 << 20),
        name="finish",
    )(*parts)
    return (
        features,
        jnp.transpose(grad_coarse, (1, 0, 2))[None, None],
        grad_first.reshape(TAPS, CH, CH),
        grad_second.reshape(TAPS, CH, CH),
        grad_lift,
        grad_land.reshape(CH),
        grad_gain.reshape(CH),
    )


def solution(mesh):
    in_specs = (
        P("row", "col", None, None, None),
        P("row", "col", None),
        P("row", "col", None),
        P("row", "col"),
        P(),
        P(),
        P(),
        P(),
        P(),
        P("row", "col", None),
    )
    out_specs = (P("row", "col", None), P("row", "col", None, None, None), P(), P(), P(), P(), P())
    return jax.shard_map(shards, mesh=mesh, in_specs=in_specs, out_specs=out_specs, check_vma=False)
```
